128 devices in a mesh: seq: 16 (over x_lo, z, core), head: 8 (over y, x_hi).
Axes of the slice: x: 4 (x_hi: 2, x_lo: 2; x = x_hi * 2 + x_lo), y: 4, z: 4, core: 2. Of those that a mesh axis runs over, the one named last changes fastest.
Arguments:
- base_ids: int32 [16384], P('seq'), may hold values from 0 to 4
- embedding: bfloat16 [5, 1024], replicated, may hold values from -6 to 6
- in_weight: bfloat16 [1024, 4384], replicated, may hold values from -0.1875 to 0.1875
- conv_weight: float32 [4, 2304], replicated, may hold values from -3 to 3
- conv_bias: float32 [2304], replicated, may hold values from -3 to 3
- dt_bias: float32 [32], replicated, may hold values from -1.5 to 0
- a_log: float32 [32], replicated, may hold values from -14 to 0
- skip_weight: float32 [32], replicated, may hold values from 0.5 to 1.5
- norm_gain: float32 [2048], replicated, may hold values from 0.25 to 1.75
- out_weight: bfloat16 [2048, 1024], replicated, may hold values from -0.125 to 0.125
- cotangent: bfloat16 [16384, 1024], P(('seq', 'head')), may hold values from -24 to 24
Outputs:
- layer_out: bfloat16 [16384, 1024], P(('seq', 'head'))
- grad_w_in: float32 [1024, 4384], P('seq')
- grad_w_out: float32 [2048, 1024], P('head', 'seq')
- grad_embedding: float32 [5, 1024], replicated
- grad_conv: float32 [4, 2304], replicated
- grad_conv_bias: float32 [2304], replicated
- grad_dt_bias: float32 [32], replicated
- grad_a_log: float32 [32], replicated
- grad_skip: float32 [32], replicated
- grad_gain: float32 [2048], replicated
The draws below stay inside these ranges and needn't reach their ends.
Inputs may be any that keep to these rules, and one draw needn't show every extreme that they name: `base_ids`: 0 A, 1 C, 2 G, 3 T, 4 N; comp pairs A with T and C with G.
All inputs are finite; a program needn't handle non-finite values.
Results may differ from the reference program's by a relative error of at most 0.0046.
Values may be sent and summed in bfloat16 or wider, within the bound.
No kernel may reach another device: no remote copies, remote signals or barrier semaphores. Data moves between devices by JAX's collectives and lax.ppermute only.
A program may use at most 320 MiB of HBM per device.

```python
import jax
import jax.numpy as jnp
from jax import lax

D = 1024
HEADS = 32
HDIM = 64
STATE = 128
SPAN = 256
KCONV = 4
VOCAB = 5
INNER = 2048
XBC = 2304
PROJ = 4384
SEGMENT = 16384


def draw_a_log(key, part):
    key = jax.random.fold_in(key, 11)
    chooser, slow_key, fast_key = jax.random.split(key, 3)
    slow_share = 0.5
    slow_rates = jnp.log(0.3 / SEGMENT) + jax.random.uniform(slow_key, (HEADS,), jnp.float32) * jnp.log(20.0)
    fast_rates = jnp.log(0.05) + jax.random.uniform(fast_key, (HEADS,), jnp.float32) * jnp.log(10.0)
    is_slow = jax.random.uniform(chooser, (HEADS,), jnp.float32) < slow_share
    return jnp.where(is_slow, slow_rates, fast_rates).astype(jnp.float32)


def plant(drawn, rng, smallest, largest):
    extent = drawn.shape
    spot = [jax.random.randint(jax.random.fold_in(rng, axis), (), 0, extent[axis]) for axis in range(len(extent))]
    drawn = drawn.at[tuple(spot)].set(smallest)
    longest = extent.index(max(extent))
    spot[longest] = (spot[longest] + 1) % extent[longest]
    return drawn.at[tuple(spot)].set(largest)


def with_spikes(drawn, rng, source, target, blocks, factor):
    def block_of(dim):
        return (jnp.arange(drawn.shape[dim]) // (drawn.shape[dim] // blocks)).reshape((-1,) + (1,) * (drawn.ndim - 1 - dim))

    first = jax.random.permutation(rng, blocks)[block_of(target)]
    second = (block_of(target) + blocks // 2) % blocks
    return jnp.where((block_of(source) == first) | (block_of(source) == second), factor * drawn, drawn)


def level_of(key, shape, pieces, low, top_value):
    level, own = 1.0, jax.random.fold_in(key, 6)
    for position, shards_of in pieces:
        steps = jnp.exp(jax.random.uniform(jax.random.fold_in(own, position), (shards_of,), jnp.float32, low / len(pieces), top_value / len(pieces)))
        level = level * jnp.repeat(steps, shape[position] // shards_of).reshape([-1 if axis == position else 1 for axis in range(len(shape))])
    return level


def bell_draw(key, extent, spread, bound, cuts=(), held_as=jnp.bfloat16):
    loudness = level_of(key, extent, cuts, -0.22, 0.18) if cuts else 1.0
    entries = jax.random.normal(key, extent, jnp.float32) * spread * loudness
    return jnp.minimum(jnp.maximum(entries, -bound), bound).astype(held_as)


def noise_with(key, dims, deviation, bound, cuts, heavy, kind=jnp.bfloat16):
    values = deviation * jax.random.normal(key, dims, jnp.float32)
    if cuts:
        values = values * level_of(key, dims, cuts, -0.22, 0.18)
    return jnp.clip(with_spikes(values, jax.random.fold_in(key, 3), *heavy), -bound, bound).astype(kind)


def setup_inputs(seed: int = 0) -> dict:
    seeds = jax.random.split(jax.random.key(seed), 12)
    return {
        "base_ids": plant(jax.random.randint(seeds[0], (SEGMENT,), 0, 5), jax.random.fold_in(seeds[0], 1), 0, 4).astype(jnp.int32),
        "embedding": bell_draw(seeds[1], (VOCAB, D), 1.0, 6.0),
        "in_weight": bell_draw(seeds[2], (D, PROJ), D ** -0.5, 0.1875),
        "conv_weight": bell_draw(seeds[3], (KCONV, XBC), KCONV ** -0.5, 3.0, (), jnp.float32),
        "conv_bias": bell_draw(seeds[4], (XBC,), 0.5, 3.0, (), jnp.float32),
        "dt_bias": jnp.clip(jax.random.uniform(seeds[5], (HEADS,), jnp.float32, -1.5, 0.0), -1.5, 0.0),
        "a_log": draw_a_log(jax.random.fold_in(seeds[11], 71), 0),
        "skip_weight": jnp.clip(jax.random.uniform(seeds[7], (HEADS,), jnp.float32, 0.5, 1.5), 0.5, 1.5),
        "norm_gain": jnp.clip(1.0 + 0.15 * jax.random.normal(seeds[8], (INNER,), jnp.float32), 0.25, 1.75),
        "out_weight": bell_draw(seeds[9], (INNER, D), INNER ** -0.5, 0.125),
        "cotangent": noise_with(seeds[10], (SEGMENT, D), 1.0, 24.0, ((0, 128),), (0, 1, 128, 5.5)),
    }


EPSILON = 1e-05
HIGHEST = lax.Precision.HIGHEST

def complement_padded(symbols):
    return jnp.where((symbols >= 1) & (symbols <= 4), 5 - symbols, symbols)

def lookup(symbols, source):
    alphabet = jnp.arange(1, source.shape[0] + 1, dtype=jnp.int32)
    onehot = (symbols[:, None] == alphabet[None, :]).astype(jnp.float32)
    return jnp.dot(onehot, source, precision=HIGHEST)

def count_rows(symbols, values, vocab_size):
    alphabet = jnp.arange(1, vocab_size + 1, dtype=jnp.int32)
    onehot = (symbols[:, None] == alphabet[None, :]).astype(values.dtype)
    return lax.dot_general(onehot, values, (((0,), (0,)), ((), ())), precision=HIGHEST, preferred_element_type=jnp.float32)

def silu_slope(values):
    logistic = jax.nn.sigmoid(values)
    return logistic * (1.0 + values * (1.0 - logistic))

def ssd_mixer(tab_x, tab_bc, tab_step, conv_x, conv_bc, bias_x, bias_bc, step_bias, log_rate, skip, symbols):
    length = symbols.shape[0] - (KCONV - 1)
    head_count = step_bias.shape[0]
    head_width = tab_x.shape[1] // head_count
    state_size = tab_bc.shape[1] // 2
    x_values = lookup(symbols, tab_x)
    bc_values = lookup(symbols, tab_bc)
    x_conv = jnp.zeros((length, tab_x.shape[1]), jnp.float32) + bias_x[None, :]
    bc_conv = jnp.zeros((length, tab_bc.shape[1]), jnp.float32) + bias_bc[None, :]
    for tap in range(KCONV):
        x_conv = x_conv + conv_x[tap][None, :] * x_values[tap:tap + length]
        bc_conv = bc_conv + conv_bc[tap][None, :] * bc_values[tap:tap + length]
    x_act = jax.nn.silu(x_conv)
    bc_act = jax.nn.silu(bc_conv)
    b_rows = bc_act[:, :state_size]
    c_rows = bc_act[:, state_size:]
    step_size = jax.nn.softplus(lookup(symbols[KCONV - 1:], tab_step) + step_bias[None, :])
    log_decay = -(jnp.exp(log_rate)[None, :] * step_size)
    block_count = length // SPAN
    x_blocks = x_act.reshape(block_count, SPAN, head_count, head_width)
    decay_blocks = log_decay.T.reshape(head_count, block_count, SPAN).transpose(1, 0, 2)
    step_blocks = step_size.T.reshape(head_count, block_count, SPAN).transpose(1, 0, 2)
    b_blocks = b_rows.reshape(block_count, SPAN, state_size)
    c_blocks = c_rows.reshape(block_count, SPAN, state_size)
    causal = jnp.arange(SPAN)[:, None] >= jnp.arange(SPAN)[None, :]

    def block_step(carry, block):
        carry_state, offset = carry
        x_block, log_block, step_block, b_block, c_block = block
        cumulative = jnp.cumsum(log_block, axis=1)
        differences = cumulative[:, :, None] - cumulative[:, None, :]
        decays = jnp.where(causal[None], jnp.exp(jnp.where(causal[None], differences, 0.0)), 0.0)
        intersection = jnp.dot(c_block, b_block.T, precision=HIGHEST)
        scores = intersection[None] * decays * step_block[:, None, :]
        within = jnp.einsum('hts,shd->thd', scores, x_block, precision=HIGHEST)
        carried = jnp.einsum('tn,hnd->thd', c_block, carry_state, precision=HIGHEST) * jnp.exp(cumulative).T[:, :, None]
        tail_weight = jnp.exp(cumulative[:, -1:] - cumulative) * step_block
        new_state = jnp.exp(cumulative[:, -1])[:, None, None] * carry_state + jnp.einsum('sn,hs,shd->hnd', b_block, tail_weight, x_block, precision=HIGHEST)
        return ((new_state, offset + cumulative[:, -1]), (within + carried, offset[:, None] + cumulative))
    start_carry = (jnp.zeros((head_count, state_size, head_width), jnp.float32), jnp.zeros((head_count,), jnp.float32))
    (final_state, log_total), (outputs, cumulatives) = lax.scan(block_step, start_carry, (x_blocks, decay_blocks, step_blocks, b_blocks, c_blocks))
    result = outputs.reshape(length, head_count, head_width) + skip[None, :, None] * x_act.reshape(length, head_count, head_width)
    cumul_all = cumulatives.transpose(1, 0, 2).reshape(head_count, length)
    return (result.reshape(length, head_count * head_width), log_total, final_state, cumul_all, c_rows)

def gate_norm(values, gate):
    gated = values.astype(jnp.float32) * jax.nn.silu(gate)
    scale = lax.rsqrt(lax.optimization_barrier(jnp.mean(gated * gated, axis=1)) + EPSILON)
    return (gated, scale)

def norm_back(slope, gated, scale, gain, total):
    return gain[None, :] * scale[:, None] * slope - (scale * scale * scale * total / INNER)[:, None] * gated

def reference(base_ids, embedding, in_weight, conv_weight, conv_bias, dt_bias, a_log, skip_weight, norm_gain, out_weight, cotangent):
    lookup_table = jnp.dot(embedding, in_weight, preferred_element_type=jnp.float32)
    symbols = base_ids.astype(jnp.int32) + 1
    mirror_codes = complement_padded(symbols)
    leading = jnp.zeros((KCONV - 1,), jnp.int32)
    forward_symbols = jnp.concatenate([leading, symbols])
    mirror_symbols = jnp.concatenate([leading, jnp.flip(mirror_codes)])
    tab_x = lookup_table[:, INNER:2 * INNER].reshape(VOCAB, HEADS, HDIM).transpose(1, 0, 2)
    tab_step = lookup_table[:, 2 * INNER + 2 * STATE:].T[:, :, None]
    conv_x = conv_weight[:, :INNER].reshape(KCONV, HEADS, HDIM).transpose(1, 0, 2)
    bias_x = conv_bias[:INNER].reshape(HEADS, HDIM)
    own_params = (tab_x, tab_step, conv_x, bias_x, dt_bias[:, None], a_log[:, None], skip_weight[:, None])
    shared = (lookup_table[:, 2 * INNER:2 * INNER + 2 * STATE], conv_weight[:, INNER:], conv_bias[INNER:])

    def run_head(mine, common, sequence):
        return ssd_mixer(mine[0], common[0], mine[1], mine[2], common[1], mine[3], common[2], mine[4], mine[5], mine[6], sequence)[0]

    def both_ways(mine, common):
        return (run_head(mine, common, forward_symbols), run_head(mine, common, mirror_symbols))
    heads_fwd, heads_rev = lax.map(lambda mine: both_ways(mine, shared), own_params)
    fwd_values = heads_fwd.transpose(1, 0, 2).reshape(SEGMENT, INNER)
    rev_values = jnp.flip(heads_rev, 1).transpose(1, 0, 2).reshape(SEGMENT, INNER)
    gate_table = lookup_table[:, :INNER]
    fwd_gate = lookup(symbols, gate_table)
    rev_gate = lookup(mirror_codes, gate_table)
    fwd_gated, fwd_scale = gate_norm(fwd_values, fwd_gate)
    rev_gated, rev_scale = gate_norm(rev_values, rev_gate)
    normed = fwd_gated * fwd_scale[:, None] * norm_gain[None, :] + rev_gated * rev_scale[:, None] * norm_gain[None, :]
    mixed_sum = normed.astype(jnp.bfloat16)
    projected = jnp.dot(mixed_sum, out_weight, preferred_element_type=jnp.float32)
    layer_out = (lookup(symbols, embedding.astype(jnp.float32)) + projected).astype(jnp.bfloat16)
    slope = lax.dot_general(cotangent, out_weight, (((1,), (1,)), ((), ())), preferred_element_type=jnp.float32)
    grad_w_out = lax.dot_general(mixed_sum, cotangent, (((0,), (0,)), ((), ())), preferred_element_type=jnp.float32)
    grad_gain = lax.optimization_barrier(jnp.sum(slope * (fwd_gated * fwd_scale[:, None] + rev_gated * rev_scale[:, None]), axis=0))
    fwd_dg = norm_back(slope, fwd_gated, fwd_scale, norm_gain, lax.optimization_barrier(jnp.sum(slope * norm_gain[None, :] * fwd_gated, axis=1)))
    rev_dg = norm_back(slope, rev_gated, rev_scale, norm_gain, lax.optimization_barrier(jnp.sum(slope * norm_gain[None, :] * rev_gated, axis=1)))
    fwd_dy = fwd_dg * jax.nn.silu(fwd_gate)
    rev_dy = rev_dg * jax.nn.silu(rev_gate)
    fwd_dz = fwd_dg * fwd_values * silu_slope(fwd_gate)
    rev_dz = rev_dg * rev_values * silu_slope(rev_gate)
    fwd_cot = fwd_dy.reshape(SEGMENT, HEADS, HDIM).transpose(1, 0, 2)
    rev_cot = jnp.flip(rev_dy.reshape(SEGMENT, HEADS, HDIM).transpose(1, 0, 2), 1)

    def pull_head(item):
        mine, first_cot, second_cot = item
        unused, backward = jax.vjp(both_ways, mine, shared)
        return backward((first_cot, second_cot))
    grads_own, grads_shared = lax.map(pull_head, (own_params, fwd_cot, rev_cot))
    tab_x_grad, tab_step_grad, conv_x_grad, bias_x_grad, step_bias_grad, log_rate_grad, skip_grad = grads_own
    tab_bc_grad, conv_bc_grad, bias_bc_grad = jax.tree.map(lambda stacked: lax.optimization_barrier(jnp.sum(stacked, axis=0)), grads_shared)
    gate_grad = count_rows(symbols, fwd_dz, VOCAB) + count_rows(mirror_codes, rev_dz, VOCAB)
    table_grad = jnp.concatenate([gate_grad, tab_x_grad.transpose(1, 0, 2).reshape(VOCAB, INNER), tab_bc_grad, tab_step_grad[:, :, 0].T], axis=1)
    grad_conv = jnp.concatenate([conv_x_grad.transpose(1, 0, 2).reshape(KCONV, INNER), conv_bc_grad], axis=1)
    grad_conv_bias = jnp.concatenate([bias_x_grad.reshape(INNER), bias_bc_grad])
    grad_w_in = jnp.dot(embedding.astype(jnp.float32).T, table_grad, precision=HIGHEST)
    grad_embedding = jnp.dot(table_grad, in_weight.astype(jnp.float32).T, precision=HIGHEST) + count_rows(symbols, cotangent, VOCAB)
    return (layer_out, grad_w_in, grad_w_out, grad_embedding, grad_conv, grad_conv_bias, step_bias_grad[:, 0], log_rate_grad[:, 0], skip_grad[:, 0], grad_gain)
```

```python
import jax
import jax.numpy as jnp
import numpy as np
from jax import lax
from jax.experimental import pallas as pl
from jax.experimental.pallas import tpu as pltpu
from jax.sharding import PartitionSpec as P

D = 1024
HEADS = 32
HDIM = 64
STATE = 128
BLOCK = 256
KCONV = 4
INNER = 2048
EPSILON = 1e-05

f32 = jnp.float32
bf16 = jnp.bfloat16
NN = (((1,), (0,)), ((), ()))
NT = (((1,), (1,)), ((), ()))
TN = (((0,), (0,)), ((), ()))

CODES = 32


def _decode_codes():
    first = np.zeros((CODES,), np.int32)
    second = np.zeros((CODES,), np.int32)
    for code in range(25):
        first[code], second[code] = code // 5 + 1, code % 5 + 1
    for code in range(25, 30):
        second[code] = code - 24
    return first, second


def _gram_onehot():
    first, second = _decode_codes()
    early, late = np.divmod(np.arange(CODES * CODES), CODES)
    symbols = (first[early], second[early], first[late], second[late])
    rows = np.zeros((CODES * CODES, 128), np.float32)
    for tap, symbol in enumerate(symbols):
        valid = symbol > 0
        rows[np.arange(CODES * CODES)[valid], (8 * tap + symbol)[valid]] = 1.0
    rows[:, 6] = 1.0
    rows[:, 64:96] = rows[:, :32]
    return rows


def encode(earlier, later):
    return jnp.where(
        earlier > 0, (earlier - 1) * 5 + later - 1, jnp.where(later > 0, 24 + later, 30)
    )


def complement_padded(symbols):
    return jnp.where((symbols >= 1) & (symbols <= 4), 5 - symbols, symbols)


def halves(values):
    high = values.astype(bf16)
    return high, (values - high.astype(f32)).astype(bf16)


def dot1(a, b, dims=NN):
    return lax.dot_general(a.astype(bf16), b.astype(bf16), dims, preferred_element_type=f32)


def dot2(a, b, dims=NN):
    high, low = halves(b)
    a = a.astype(bf16)
    return dot1(a, high, dims) + dot1(a, low, dims)


def dot2l(a, b, dims=NN):
    high, low = halves(a)
    b = b.astype(bf16)
    return dot1(high, b, dims) + dot1(low, b, dims)


def dot3(a, b, dims=NN):
    a_high, a_low = halves(a)
    b_high, b_low = halves(b)
    return dot1(a_high, b_high, dims) + (dot1(a_high, b_low, dims) + dot1(a_low, b_high, dims))


def iota(shape, axis):
    return lax.broadcasted_iota(jnp.int32, shape, axis)


def ones_where(condition):
    return jnp.where(condition, 1.0, 0.0).astype(bf16)


def expand_grams(sums):
    grams = CODES * CODES
    early = ones_where(iota((grams, CODES), 0) // CODES == iota((grams, CODES), 1))
    spread = dot2(early, sums, NT)
    mine = iota((grams, 128), 0) % CODES == iota((grams, 128), 1) % CODES
    spread = jnp.where(mine, spread, 0.0)
    widen = ones_where(iota((128, 256), 0) // CODES == iota((128, 256), 1) // HDIM)
    return dot2l(spread, widen)


def gather_grams(values):
    grams = CODES * CODES
    narrow = ones_where(iota((256, 128), 0) // HDIM == iota((256, 128), 1) // CODES)
    spread = dot2l(values, narrow)
    mine = iota((grams, 128), 0) % CODES == iota((grams, 128), 1) % CODES
    spread = jnp.where(mine, spread, 0.0)
    early = ones_where(iota((CODES, grams), 1) // CODES == iota((CODES, grams), 0))
    return dot2(early, spread)


def sigmoid(values):
    return 1.0 / (1.0 + jnp.exp(-values))


def scan_inputs(oh_ref, oht_ref, tt_ref, lx_ref, lrow_ref, rows, branch):
    onehot = oh_ref[rows, :]
    onehot_t = oht_ref[:, rows]
    before = branch * 512
    pre = dot1(onehot, tt_ref[:, before : before + 512])
    step = dot1(onehot, tt_ref[:, 1024 + branch * 256 : 1280 + branch * 256])
    row = iota((BLOCK, BLOCK), 0)
    col = iota((BLOCK, BLOCK), 1)
    lower = ones_where(row >= col)
    upper = ones_where(row <= col)
    counts = dot1(lower if branch == 0 else upper, onehot).astype(bf16)
    counts_t = dot1(onehot_t, upper if branch == 0 else lower)
    log_wide = dot1(counts, lx_ref[:, branch * 256 : branch * 256 + 256])
    log_cols = dot1(counts, lx_ref[:, 512:640])
    log_rows = dot1(lrow_ref[...], counts_t)
    return onehot_t, pre, step, counts_t, log_wide, log_cols, log_rows


def forward_kernel(
    seq_ref, ltab_ref, qs_ref, ca_ref, cb_ref, oh_ref, oht_ref, goh_ref, tt_ref, lx_ref, lrow_ref,
    skip_ref,
    y_ref, states_ref, sums_ref, decay_ref, after_ref,
    high_ref, low_ref, lhs_ref, rhs_ref, carry_ref,
):
    seq = seq_ref[0]
    first = seq * 8
    symbols = qs_ref[...]
    row = iota((128, 128), 0)
    col = iota((128, 128), 1)
    upto = ones_where(row <= col)
    every = jnp.ones((128, 128), bf16)
    signs = (jnp.where(col < row, 1.0, 0.0) - jnp.where(col < first, 1.0, 0.0)).astype(bf16)
    is_before = row < first
    logs = [jnp.zeros((128, 128), f32) for _ in range(4)]
    for symbol in range(1, 6):
        here = symbols == symbol
        found = ones_where(here)
        within = dot1(found, upto)
        total = dot1(found, every)
        upper = within + dot1(signs, total)
        after = jnp.where(is_before, -upper, upper - jnp.where(here, 1.0, 0.0))
        after_ref[symbol - 1] = after
        for h in range(4):
            logs[h] = logs[h] + after * ltab_ref[h, symbol]
    for h in range(4):
        decay = jnp.where(symbols > 0, jnp.exp(logs[h]), 0.0)
        decay_ref[h] = decay
        high = decay.astype(bf16).astype(f32)
        high_ref[h] = high
        low_ref[h] = decay - high
    codes = iota((CODES, 128), 0)

    def add_shard(shard, total):
        at = pl.ds(pl.multiple_of(shard * 8, 8), 8)
        early = ca_ref[at, :]
        late = cb_ref[at, :]
        for j in range(8):
            cols = slice(128 * j, 128 * j + 128)
            rhs_ref[:, cols] = ones_where(early[j : j + 1] == codes)
            mine = late[j : j + 1] == codes
            for h in range(4):
                lhs_ref[32 * h : 32 * h + 32, cols] = jnp.where(
                    mine, high_ref[h, at, :][j : j + 1], 0.0
                ).astype(bf16)
                lhs_ref[128 + 32 * h : 160 + 32 * h, cols] = jnp.where(
                    mine, low_ref[h, at, :][j : j + 1], 0.0
                ).astype(bf16)
        return total + dot1(lhs_ref[...], rhs_ref[...], NT)

    zero = jnp.zeros((256, CODES), f32)
    both = (
        lax.fori_loop(0, seq, add_shard, zero),
        lax.fori_loop(seq + 1, 16, add_shard, zero),
    )
    gram_pre = dot1(goh_ref[...], tt_ref[:, :512])
    gram_act = gram_pre * sigmoid(gram_pre)
    gram_x = gram_act[:, :256]
    gram_b = gram_act[:, 256:384]
    gram_xs = gram_x * dot1(goh_ref[...], tt_ref[:, 1024:1280])
    skip = skip_ref[...]
    row = iota((BLOCK, BLOCK), 0)
    col = iota((BLOCK, BLOCK), 1)
    for branch in range(2):
        sums = both[branch][:128] + both[branch][128:]
        sums_ref[branch] = sums
        weights = expand_grams(sums)
        carry_ref[...] = dot3(gram_b, weights * gram_xs, TN)
        causal = row >= col if branch == 0 else row <= col

        def block_step(k, unused, branch=branch, causal=causal):
            block = k if branch == 0 else 3 - k
            rows = pl.ds(pl.multiple_of(block * BLOCK, BLOCK), BLOCK)
            onehot_t, pre, step, counts_t, log_wide, log_cols, log_rows = scan_inputs(
                oh_ref, oht_ref, tt_ref, lx_ref, lrow_ref, rows, branch
            )
            act = pre * sigmoid(pre)
            x = act[:, :256]
            b = act[:, 256:384]
            c = act[:, 384:]
            xs = x * step
            state = carry_ref[...]
            states_ref[branch * 4 + block] = state
            inner = dot3(c, b, NT)
            parts = []
            for h in range(4):
                lane = branch * 4 + h
                decays = jnp.exp(
                    jnp.where(
                        causal,
                        log_cols[:, lane : lane + 1]
                        - log_rows[branch * 8 + h : branch * 8 + h + 1, :],
                        -1e30,
                    )
                )
                parts.append(dot1(inner * decays, xs[:, h * HDIM : (h + 1) * HDIM]))
            within = jnp.concatenate(parts, axis=1)
            y = within + dot3(c, state) * jnp.exp(log_wide)
            y_ref[branch, rows, :] = y + skip * x
            edge = log_wide[BLOCK - 1 :] if branch == 0 else log_wide[:1]
            carry_ref[...] = jnp.exp(edge) * state + dot3(b, jnp.exp(edge - log_wide) * xs, TN)
            return unused

        lax.fori_loop(0, 4, block_step, 0)


def slope_kernel(y_ref, oh_ref, tt_ref, cot_ref, ow_ref, gain_ref, slope_ref, sums_ref):
    slope = lax.dot_general(cot_ref[...], ow_ref[...], NT, preferred_element_type=f32)
    slope_ref[...] = slope
    weighted = slope * gain_ref[...]
    every = jnp.ones((8, 256), bf16)
    for branch in range(2):
        gate = dot1(oh_ref[...], tt_ref[:, 1536 + 256 * branch : 1792 + 256 * branch])
        g = y_ref[branch] * gate
        for kind, product in enumerate((g * g, weighted * g)):
            at = 2 * branch + kind
            sums_ref[at : at + 1, :] = dot2(every, product, NT)[:1]
    sums_ref[4:, :] = jnp.zeros((4, sums_ref.shape[1]), f32)


def mix_kernel(
    y_ref, oh_ref, oht_ref, tt_ref, slope_ref, gain_ref, cols_ref,
    mixed_ref, dy_ref, dgate_ref, dgain_ref,
):
    gain = gain_ref[...]
    slope = slope_ref[...]
    cols = cols_ref[...]
    sloped = slope * gain
    total = None
    for branch in range(2):
        gate = dot1(oh_ref[...], tt_ref[:, 1536 + 256 * branch : 1792 + 256 * branch])
        y = y_ref[branch]
        g = y * gate
        scale = cols[:, 2 * branch : 2 * branch + 1]
        weight = cols[:, 2 * branch + 1 : 2 * branch + 2]
        normed = g * scale
        total = normed if total is None else total + normed
        dg = scale * sloped - weight * g
        dy_ref[branch] = dg * gate
        lanes = oht_ref[32 * branch : 32 * branch + 32, :]
        dgate_ref[branch] = dot2(lanes, dg * y)
    mixed_ref[...] = (total * gain).astype(bf16)
    dgain_ref[...] = jnp.sum(slope * total, axis=0, keepdims=True)


def backward_kernel(
    seq_ref, ca_ref, cb_ref, oh_ref, oht_ref, goh_ref, goht_ref, tt_ref, lx_ref, lrow_ref, skip_ref,
    y_ref, states_ref, sums_ref, decay_ref, after_ref, dy_ref,
    tables_ref, steps_ref, logs_ref, skips_ref, far_ref,
    carry_ref, pulls_ref, mark_ref, found_ref,
):
    skip = skip_ref[...]
    row = iota((BLOCK, BLOCK), 0)
    col = iota((BLOCK, BLOCK), 1)
    tables_ref[...] = jnp.zeros_like(tables_ref)
    steps_ref[...] = jnp.zeros_like(steps_ref)
    logs_ref[...] = jnp.zeros_like(logs_ref)
    skips_ref[...] = jnp.zeros_like(skips_ref)
    for branch in range(2):
        causal = row <= col if branch == 0 else row >= col
        carry_ref[...] = jnp.zeros_like(carry_ref)

        def block_step(k, unused, branch=branch, causal=causal):
            block = 3 - k if branch == 0 else k
            later = jnp.minimum(block + 1, 3) if branch == 0 else jnp.maximum(block - 1, 0)
            rows = pl.ds(pl.multiple_of(block * BLOCK, BLOCK), BLOCK)
            onehot_t, pre, step, counts_t, log_wide, log_cols, log_rows = scan_inputs(
                oh_ref, oht_ref, tt_ref, lx_ref, lrow_ref, rows, branch
            )
            lanes = slice(32 * branch, 32 * branch + 32)
            onehot_t = onehot_t[lanes]
            counts_t = counts_t[lanes]
            logistic = sigmoid(pre)
            act = pre * logistic
            bend = logistic * (1.0 + pre * (1.0 - logistic))
            x = act[:, :256]
            b = act[:, 256:384]
            c = act[:, 384:]
            xs = x * step
            dy = dy_ref[branch, rows, :]
            own = y_ref[branch, rows, :] - skip * x
            state = states_ref[branch * 4 + block]
            pull = carry_ref[...]
            xs_low = xs.astype(bf16)
            dy_low = dy.astype(bf16)
            inner = dot3(b, c, NT)
            parts = []
            slopes = jnp.zeros((BLOCK, BLOCK), f32)
            for h in range(4):
                lane = branch * 4 + h
                wide = slice(h * HDIM, (h + 1) * HDIM)
                decays = jnp.exp(
                    jnp.where(
                        causal,
                        log_rows[branch * 8 + h : branch * 8 + h + 1, :]
                        - log_cols[:, lane : lane + 1],
                        -1e30,
                    )
                )
                parts.append(dot1(inner * decays, dy_low[:, wide]))
                slopes = slopes + dot1(xs_low[:, wide], dy_low[:, wide], NT) * decays
            within = jnp.concatenate(parts, axis=1)
            faded = jnp.exp(log_wide) * dy
            edge = log_wide[BLOCK - 1 :] if branch == 0 else log_wide[:1]
            tail = jnp.exp(edge - log_wide)
            db = dot1(slopes, c) + dot1(tail * xs, pull, NT)
            dc = dot1(slopes, b, TN) + dot1(faded, state, NT)
            dxs = within + tail * dot1(b, pull)
            dlog = dy_low.astype(f32) * own - xs_low.astype(f32) * dxs
            edge_count = counts_t[:, BLOCK - 1 :] if branch == 0 else counts_t[:, :1]
            ahead = jnp.sum(states_ref[branch * 4 + later] * pull, axis=0, keepdims=True)
            logs_ref[...] += dot2(counts_t, dlog) + edge_count * ahead
            carry_ref[...] = dot1(c, faded, TN) + jnp.exp(edge) * pull
            dpre = jnp.concatenate([step * dxs + skip * dy, db, dc], axis=1) * bend
            tables_ref[...] += dot2(onehot_t, dpre)
            steps_ref[...] += dot2(onehot_t, x * dxs)
            skips_ref[...] += jnp.sum(dy * x, axis=0, keepdims=True)
            return unused

        lax.fori_loop(0, 4, block_step, 0)
        pulls_ref[branch] = carry_ref[...]

    seq = seq_ref[0]
    gram_pre = dot1(goh_ref[...], tt_ref[:, :512])
    logistic = sigmoid(gram_pre)
    gram_act = gram_pre * logistic
    bend = logistic * (1.0 + gram_pre * (1.0 - logistic))
    gram_x = gram_act[:, :256]
    gram_b = gram_act[:, 256:384]
    gram_step = dot1(goh_ref[...], tt_ref[:, 1024:1280])
    gram_xs = gram_x * gram_step
    dxs = jnp.zeros((CODES * CODES, 256), f32)
    db = jnp.zeros((CODES * CODES, 128), f32)
    found = []
    for branch in range(2):
        pull = pulls_ref[branch]
        weights = expand_grams(sums_ref[branch])
        met = dot1(gram_b, pull)
        dxs = dxs + weights * met
        db = db + dot1(weights * gram_xs, pull, NT)
        found.append(gather_grams(gram_xs * met))
    dpre = jnp.concatenate([gram_step * dxs, db], axis=1) * bend[:, :384]
    gram_t = goht_ref[...]
    tables_ref[:, :384] += dot2(gram_t, dpre)
    steps_ref[...] += dot2(gram_t, gram_x * dxs)
    codes = iota((CODES, 128), 0)

    def look_up(branch):
        table_high, table_low = halves(found[branch])

        def one_shard(shard, unused):
            at = pl.ds(pl.multiple_of(shard * 8, 8), 8)
            early = ca_ref[at, :]
            late = cb_ref[at, :]
            for j in range(8):
                mark_ref[:, 128 * j : 128 * j + 128] = ones_where(early[j : j + 1] == codes)
            marks = mark_ref[...]
            looked = dot1(table_high, marks, TN) + dot1(table_low, marks, TN)
            for h in range(4):
                rows = []
                for j in range(8):
                    part = looked[32 * h : 32 * h + 32, 128 * j : 128 * j + 128]
                    mine = late[j : j + 1] == codes
                    rows.append(jnp.sum(jnp.where(mine, part, 0.0), axis=0, keepdims=True))
                found_ref[h, at, :] = jnp.concatenate(rows, axis=0)
            return unused

        return one_shard

    found_ref[...] = jnp.zeros_like(found_ref)
    lax.fori_loop(0, seq, look_up(0), 0)
    lax.fori_loop(seq + 1, 16, look_up(1), 0)
    for h in range(4):
        weighted = found_ref[h] * decay_ref[h]
        for symbol in range(5):
            far_ref[5 * h + symbol : 5 * h + symbol + 1, :] = jnp.sum(
                weighted * after_ref[symbol], axis=0, keepdims=True
            )


VMEM = pl.BlockSpec(memory_space=pltpu.VMEM)
SMEM = pl.BlockSpec(memory_space=pltpu.SMEM)


def call(kernel, outs, in_specs, scratch=()):
    return pl.pallas_call(
        kernel,
        out_shape=[jax.ShapeDtypeStruct(shape, kind) for shape, kind in outs],
        in_specs=in_specs,
        out_specs=[VMEM] * len(outs),
        scratch_shapes=list(scratch),
        compiler_params=pltpu.CompilerParams(vmem_limit_bytes=56 * 1024 * 1024),
    )


def gather(shard, axis):
    devices = lax.axis_size(axis)
    spread = jnp.broadcast_to(shard[None], (devices,) + shard.shape)
    return lax.all_to_all(spread, axis, split_axis=0, concat_axis=0, tiled=True)


def split_two(values):
    high = lax.reduce_precision(values, 8, 7)
    return high.astype(bf16), (values - high).astype(bf16)


def two_halves(table):
    high, low = split_two(table)
    return jnp.concatenate([high, low], axis=0)


def silu_slope(values):
    logistic = jax.nn.sigmoid(values)
    return logistic * (1.0 + values * (1.0 - logistic))


def body(
    base_ids, embedding, in_weight, conv_weight, conv_bias, dt_bias, a_log, skip_weight, norm_gain,
    out_weight, cotangent,
):
    groups = lax.axis_size("head")
    shards = lax.axis_size("seq")
    local_heads = HEADS // groups
    width = local_heads * HDIM
    head_rank = lax.axis_index("head")
    seq_rank = lax.axis_index("seq")
    length = base_ids.shape[0]
    token_rows = length // groups
    column_start = head_rank * width
    head_start = head_rank * local_heads

    everyone = gather(base_ids.reshape(8, 128), "seq").reshape(shards * length)
    cot_all = gather(cotangent, "head").reshape(length, D)

    def cols(array, start, size):
        return lax.dynamic_slice_in_dim(array, start, size, array.ndim - 1)

    weight_own = jnp.concatenate(
        [
            cols(in_weight, column_start, width),
            cols(in_weight, INNER + column_start, width),
            in_weight[:, 2 * INNER :],
        ],
        axis=1,
    )
    table = jnp.dot(embedding, weight_own, preferred_element_type=f32)
    tab_gate = table[:, :width]
    tab_conv = table[:, width : 2 * width + 2 * STATE]
    tab_step = cols(table[:, 2 * width + 2 * STATE :], head_start, local_heads)
    conv = jnp.concatenate([cols(conv_weight, column_start, width), conv_weight[:, INNER:]], axis=1)
    bias = jnp.concatenate([cols(conv_bias, column_start, width), conv_bias[INNER:]])
    rate = jnp.exp(cols(a_log, head_start, local_heads))
    pre_step = tab_step + cols(dt_bias, head_start, local_heads)[None, :]
    step_tab = jax.nn.softplus(pre_step)
    log_tab = -(rate[None, :] * step_tab)
    gain_own = cols(norm_gain, column_start, width)[None, :]
    skip_own = jnp.repeat(cols(skip_weight, head_start, local_heads), HDIM)[None, :]
    ow_own = lax.dynamic_slice_in_dim(out_weight, column_start, width, 0)

    def own_symbol(values, branch):
        start = 32 * branch + 25
        return jnp.pad(values, ((start, 64 - start - 5), (0, 0)))

    taps = jnp.pad(conv[:, None, :] * tab_conv[None, :, :], ((0, 0), (1, 2), (0, 0)))
    taps = taps.reshape(32, width + 2 * STATE)
    taps = taps + jnp.pad(bias[None, :], ((6, 25), (0, 0)))
    step_wide = jnp.repeat(step_tab, HDIM, axis=1)
    log_wide = jnp.repeat(log_tab, HDIM, axis=1)
    gate_act = jax.nn.silu(tab_gate)
    big = jnp.concatenate(
        [
            jnp.pad(taps, ((0, 32), (0, 0))),
            jnp.pad(taps, ((32, 0), (0, 0))),
            own_symbol(step_wide, 0),
            own_symbol(step_wide, 1),
            own_symbol(gate_act, 0),
            own_symbol(gate_act, 1),
        ],
        axis=1,
    )
    big = two_halves(big)
    log_cols = jnp.concatenate([own_symbol(log_tab, 0), own_symbol(log_tab, 1)], axis=1)
    log_cols = jnp.pad(log_cols, ((0, 0), (0, 120)))
    logs = two_halves(
        jnp.concatenate([own_symbol(log_wide, 0), own_symbol(log_wide, 1), log_cols], axis=1)
    )
    log_rows = jnp.concatenate(
        [
            jnp.pad(own_symbol(log_tab, 0).T, ((0, 4), (0, 0))),
            jnp.pad(own_symbol(log_tab, 1).T, ((0, 4), (0, 0))),
        ],
        axis=0,
    )
    log_rows = jnp.concatenate(split_two(log_rows), axis=1)
    log_small = jnp.pad(log_tab.T, ((0, 0), (1, 2)))

    total = shards * length
    symbols = everyone + 1
    padded = jnp.pad(symbols, (3, 3))
    mirrored = complement_padded(padded)
    ahead = [padded[k : k + total] for k in range(4)]
    behind = [mirrored[6 - k : 6 - k + total] for k in range(4)]
    shard_of = jnp.arange(total, dtype=jnp.int32) // length
    is_before = shard_of < seq_rank
    far = [jnp.where(is_before, a, b) for a, b in zip(ahead, behind)]
    early = encode(far[0], far[1]).reshape(128, 128)
    late = encode(far[2], far[3]).reshape(128, 128)
    own = jnp.where(shard_of == seq_rank, 0, far[3]).reshape(128, 128)
    window = lax.dynamic_slice_in_dim(padded, seq_rank * length, length + 6, 0)
    turned = complement_padded(window)
    lane = jnp.arange(128, dtype=jnp.int32)

    def onehot_of(axis):
        at = jnp.expand_dims(lane, 1 - axis)
        at = at % 64
        tap = (at % 32) // 8
        symbol = at % 8
        value = jnp.zeros(at.shape, jnp.int32)
        for k in range(4):
            first = jnp.expand_dims(window[k : k + length], axis)
            second = jnp.expand_dims(turned[6 - k : 6 - k + length], axis)
            value = jnp.where(tap == k, jnp.where(at < 32, first, second), value)
        hit = (value == symbol) & (symbol > 0) | (at % 32 == 6)
        return hit.astype(bf16)

    onehot = onehot_of(1)
    onehot_t = onehot_of(0)
    grams = _gram_onehot()
    gram_rows = jnp.asarray(grams, bf16)
    gram_cols = jnp.asarray(np.ascontiguousarray(grams[:, :32].T), bf16)
    seq_at = jnp.reshape(seq_rank, (1,)).astype(jnp.int32)

    y, states, sums, decays, after = call(
        forward_kernel,
        [
            ((2, length, width), f32),
            ((8, STATE, width), f32),
            ((2, 128, CODES), f32),
            ((4, 128, 128), f32),
            ((5, 128, 128), f32),
        ],
        [SMEM, SMEM] + [VMEM] * 10,
        [
            pltpu.VMEM((4, 128, 128), f32),
            pltpu.VMEM((4, 128, 128), f32),
            pltpu.VMEM((256, 1024), bf16),
            pltpu.VMEM((32, 1024), bf16),
            pltpu.VMEM((STATE, width), f32),
        ],
    )(
        seq_at, log_small, own, early, late, onehot, onehot_t, gram_rows, big, logs, log_rows,
        skip_own,
    )

    slope, row_sums = call(
        slope_kernel, [((length, width), f32), ((8, length), f32)], [VMEM] * 6
    )(y, onehot, big, cot_all, ow_own, gain_own)
    row_sums = jnp.sum(gather(row_sums, "head").reshape(groups, 8, length), axis=0)
    squares = jnp.stack([row_sums[0], row_sums[2]])
    crossed = jnp.stack([row_sums[1], row_sums[3]])
    scale = lax.rsqrt(squares / INNER + EPSILON)
    weight = scale * scale * scale * crossed / INNER
    scalars = jnp.stack([scale[0], weight[0], scale[1], weight[1]] + [scale[0]] * 4, axis=1)

    mixed, dy, dgate, dgain = call(
        mix_kernel,
        [
            ((length, width), bf16),
            ((2, length, width), f32),
            ((2, 32, width), f32),
            ((1, width), f32),
        ],
        [VMEM] * 7,
    )(y, onehot, onehot_t, big, slope, gain_own, scalars)

    mixed_all = lax.all_to_all(
        mixed.reshape(groups, token_rows, width), "head", split_axis=0, concat_axis=0, tiled=True
    )
    partial = lax.dot_general(cot_all, mixed, TN, preferred_element_type=f32)
    partial = lax.all_to_all(
        partial.reshape(shards, D // shards, width), "seq", split_axis=0, concat_axis=0, tiled=True
    )

    tables, steps, logs_back, skips, far_logs = call(
        backward_kernel,
        [
            ((32, 512), f32),
            ((32, width), f32),
            ((32, width), f32),
            ((1, width), f32),
            ((20, 128), f32),
        ],
        [SMEM] + [VMEM] * 16,
        [
            pltpu.VMEM((STATE, width), f32),
            pltpu.VMEM((2, STATE, width), f32),
            pltpu.VMEM((32, 1024), bf16),
            pltpu.VMEM((4, 128, 128), f32),
        ],
    )(
        seq_at, early, late, onehot, onehot_t, gram_rows, gram_cols, big, logs, log_rows, skip_own,
        y, states, sums, decays, after, dy,
    )

    grad_w_out = jnp.sum(partial, axis=0).T
    token_ids = lax.dynamic_slice_in_dim(base_ids, head_rank * token_rows, token_rows, 0)
    alphabet = jnp.arange(5, dtype=jnp.int32)
    token_hot = (token_ids[:, None] == alphabet[None, :]).astype(bf16)
    residual = jnp.dot(token_hot, embedding, preferred_element_type=f32)
    mixed_rows = mixed_all.transpose(1, 0, 2).reshape(token_rows, INNER)
    layer_out = (
        residual + jnp.dot(mixed_rows, out_weight, preferred_element_type=f32)
    ).astype(bf16)

    def own_rows(values):
        return jnp.sum(values[25:30].reshape(5, local_heads, HDIM), axis=2)

    by_tap = tables.reshape(KCONV, 8, width + 2 * STATE)
    grad_bias = tables[6]
    by_tap = by_tap[:, 1:6]
    conv_part = jnp.sum(by_tap * tab_conv[None], axis=1)
    tab_part = jnp.sum(by_tap * conv[:, None, :], axis=0)
    far_part = jnp.sum(far_logs, axis=1).reshape(local_heads, 5).T
    log_part = own_rows(logs_back) + far_part
    rate_part = jnp.sum(log_part * log_tab, axis=0)
    step_part = own_rows(steps) - rate[None, :] * log_part
    step_part = step_part * jax.nn.sigmoid(pre_step)
    skip_part = jnp.sum(skips.reshape(local_heads, HDIM), axis=1)
    gate_part = (dgate[0, 25:30] + dgate[1, 25:30]) * silu_slope(tab_gate)
    counts = lax.dot_general(token_hot, cotangent, TN, preferred_element_type=f32)
    step_cols = lax.dynamic_update_slice_in_dim(
        jnp.zeros((5, HEADS), f32), step_part, head_start, 1
    )
    table_part = jnp.concatenate([gate_part, tab_part, step_cols], axis=1)
    embed_part = counts + lax.dot_general(
        table_part, weight_own.astype(f32), NT, precision=lax.Precision.HIGHEST
    )
    heads_row = jnp.concatenate(
        [step_part, jnp.sum(step_part, axis=0)[None], rate_part[None], skip_part[None]], axis=0
    )
    heads_row = jnp.pad(heads_row.reshape(1, 8 * local_heads), ((0, 0), (0, width - 32)))
    packed = jnp.concatenate(
        [
            gate_part,
            tab_part[:, :width],
            conv_part[:, :width],
            grad_bias[None, :width],
            dgain,
            heads_row,
            tab_part[:, width:],
            conv_part[:, width:],
            grad_bias[None, width:],
            embed_part.reshape(20, width),
            jnp.zeros((1, width), f32),
        ],
        axis=0,
    )
    rows = packed.shape[0]
    pieces = lax.all_to_all(
        packed.reshape(shards, rows // shards, width), "seq", split_axis=0, concat_axis=0, tiled=True
    )
    piece = jnp.sum(pieces, axis=0)
    whole = gather(piece, ("seq", "head")).reshape(shards, groups, rows // shards, width)
    whole = whole.transpose(1, 0, 2, 3).reshape(groups, rows, width)
    mine = whole[:, :17]
    shared = jnp.sum(whole[:, 17:], axis=0)

    def lay(rows_of):
        return rows_of.transpose(1, 0, 2).reshape(rows_of.shape[1], INNER)

    heads_all = mine[:, 16, :32].reshape(groups, 8, local_heads)
    heads_all = heads_all.transpose(1, 0, 2).reshape(8, HEADS)
    table_sum = jnp.concatenate(
        [lay(mine[:, :5]), lay(mine[:, 5:10]), shared[:5], heads_all[:5]], axis=1
    )
    grad_conv = jnp.concatenate([lay(mine[:, 10:14]), shared[5:9]], axis=1)
    grad_conv_bias = jnp.concatenate([mine[:, 14].reshape(INNER), shared[9]])
    grad_gain = mine[:, 15].reshape(INNER)
    grad_embedding = shared[10:30].reshape(5, D)
    row_count = D // shards
    embed_columns = lax.dynamic_slice_in_dim(embedding, seq_rank * row_count, row_count, 1)
    grad_w_in = lax.dot_general(
        embed_columns.astype(f32), table_sum, TN, precision=lax.Precision.HIGHEST
    )
    return (
        layer_out,
        grad_w_in,
        grad_w_out,
        grad_embedding,
        grad_conv,
        grad_conv_bias,
        heads_all[5],
        heads_all[6],
        heads_all[7],
        grad_gain,
    )


def solution(mesh):
    return jax.shard_map(
        body,
        mesh=mesh,
        in_specs=(P("seq"), P(), P(), P(), P(), P(), P(), P(), P(), P(), P(("seq", "head"), None)),
        out_specs=(
            P(("seq", "head"), None),
            P("seq", None),
            P("head", "seq"),
            P(),
            P(),
            P(),
            P(),
            P(),
            P(),
            P(),
        ),
        check_vma=False,
    )
```

```python
import jax
import jax.numpy as jnp
import numpy as np
from jax import lax
from jax.experimental import pallas as pl
from jax.experimental.pallas import tpu as pltpu
from jax.sharding import PartitionSpec as P

D = 1024
HEADS = 32
HDIM = 64
STATE = 128
BLOCK = 256
KCONV = 4
INNER = 2048
EPSILON = 1e-05

f32 = jnp.float32
bf16 = jnp.bfloat16
NN = (((1,), (0,)), ((), ()))
NT = (((1,), (1,)), ((), ()))
TN = (((0,), (0,)), ((), ()))

CODES = 32


def _decode_codes():
    first = np.zeros((CODES,), np.int32)
    second = np.zeros((CODES,), np.int32)
    for code in range(25):
        first[code], second[code] = code // 5 + 1, code % 5 + 1
    for code in range(25, 30):
        second[code] = code - 24
    return first, second


def _gram_onehot():
    first, second = _decode_codes()
    early, late = np.divmod(np.arange(CODES * CODES), CODES)
    symbols = (first[early], second[early], first[late], second[late])
    rows = np.zeros((CODES * CODES, 128), np.float32)
    for tap, symbol in enumerate(symbols):
        valid = symbol > 0
        rows[np.arange(CODES * CODES)[valid], (8 * tap + symbol)[valid]] = 1.0
    rows[:, 6] = 1.0
    rows[:, 64:96] = rows[:, :32]
    return rows


def encode(earlier, later):
    return jnp.where(
        earlier > 0, (earlier - 1) * 5 + later - 1, jnp.where(later > 0, 24 + later, 30)
    )


def complement_padded(symbols):
    return jnp.where((symbols >= 1) & (symbols <= 4), 5 - symbols, symbols)


def halves(values):
    high = values.astype(bf16)
    return high, (values - high.astype(f32)).astype(bf16)


def dot1(a, b, dims=NN):
    return lax.dot_general(a.astype(bf16), b.astype(bf16), dims, preferred_element_type=f32)


def doubled(values, axis):
    return jnp.concatenate([values, values], axis=axis)


def dot2(a, b, dims=NN):
    high, low = halves(b)
    a = a.astype(bf16)
    if a.shape[dims[0][0][0]] <= 128:
        pieces = jnp.concatenate([high, low], axis=dims[0][1][0])
        return dot1(doubled(a, dims[0][0][0]), pieces, dims)
    return dot1(a, high, dims) + dot1(a, low, dims)


def dot2l(a, b, dims=NN):
    high, low = halves(a)
    b = b.astype(bf16)
    if b.shape[dims[0][1][0]] <= 128:
        pieces = jnp.concatenate([high, low], axis=dims[0][0][0])
        return dot1(pieces, doubled(b, dims[0][1][0]), dims)
    return dot1(high, b, dims) + dot1(low, b, dims)


def dot3(a, b, dims=NN):
    a_high, a_low = halves(a)
    b_high, b_low = halves(b)
    if a.shape[dims[0][0][0]] <= 128:
        pieces = jnp.concatenate([a_high, a_low], axis=dims[0][0][0])
        return dot1(pieces, doubled(b_high, dims[0][1][0]), dims) + dot1(a_high, b_low, dims)
    return dot1(a_high, b_high, dims) + (dot1(a_high, b_low, dims) + dot1(a_low, b_high, dims))


def dot_exact(a, b, dims=NN):
    first = a.astype(bf16)
    rest = a - first.astype(f32)
    second = rest.astype(bf16)
    third = rest - second.astype(f32)
    b = b.astype(bf16)
    return dot1(first, b, dims) + (dot1(second, b, dims) + dot1(third, b, dims))


def iota(shape, axis):
    return lax.broadcasted_iota(jnp.int32, shape, axis)


def ones_where(condition):
    return jnp.where(condition, 1.0, 0.0).astype(bf16)


def expand_grams(sums):
    grams = CODES * CODES
    early = ones_where(iota((grams, CODES), 0) // CODES == iota((grams, CODES), 1))
    spread = dot2(early, sums)
    mine = iota((grams, 128), 0) % CODES == iota((grams, 128), 1) % CODES
    spread = jnp.where(mine, spread, 0.0)
    widen = ones_where(iota((128, 256), 0) // CODES == iota((128, 256), 1) // HDIM)
    return dot2l(spread, widen)


def gather_grams(values):
    grams = CODES * CODES
    narrow = ones_where(iota((256, 128), 0) // HDIM == iota((256, 128), 1) // CODES)
    spread = dot2l(values, narrow)
    mine = iota((grams, 128), 0) % CODES == iota((grams, 128), 1) % CODES
    spread = jnp.where(mine, spread, 0.0)
    early = ones_where(iota((CODES, grams), 1) // CODES == iota((CODES, grams), 0))
    return dot2(early, spread)


def sigmoid(values):
    return 0.5 * jnp.tanh(0.5 * values) + 0.5


def scan_inputs(oh_ref, oht_ref, tt_ref, lx_ref, lrow_ref, rows, branch):
    onehot = oh_ref[rows, :]
    onehot_t = oht_ref[:, rows]
    before = branch * 512
    pre = dot1(onehot, tt_ref[:, before : before + 512])
    step = dot1(onehot, tt_ref[:, 1024 + branch * 256 : 1280 + branch * 256])
    row = iota((BLOCK, BLOCK), 0)
    col = iota((BLOCK, BLOCK), 1)
    lower = ones_where(row >= col)
    upper = ones_where(row <= col)
    counts = dot1(lower if branch == 0 else upper, onehot).astype(bf16)
    counts_t = dot1(onehot_t, upper if branch == 0 else lower)
    log_wide = dot1(counts, lx_ref[:, branch * 256 : branch * 256 + 256])
    log_rows = dot1(lrow_ref[...].astype(bf16), counts_t)
    return onehot_t, pre, step, counts_t, log_wide, log_rows


def prep_kernel(
    at_ref, embed_ref, gate_w_ref, x_w_ref, bc_w_ref, step_w_ref, conv_x_ref, conv_bc_ref,
    bias_x_ref, bias_bc_ref, heads_ref, goh_ref,
    big_ref, logs_ref, lrow_ref, tab_ref, wide_ref, weight_ref, gact_ref, gbend_ref, gstep_ref,
):
    rank = at_ref[1]
    place = ones_where(iota((8, 5), 0) == iota((8, 5), 1) + 1)
    embed = dot1(place, embed_ref[...]).astype(bf16)
    gate_w = gate_w_ref[...]
    x_w = x_w_ref[...]
    bc_w = bc_w_ref[...]
    step_w = step_w_ref[...]
    weight_ref[:256, :] = gate_w
    weight_ref[256:512, :] = x_w
    weight_ref[512:768, :] = bc_w
    step_w = jnp.where(iota((128, D), 0) < HEADS, step_w.astype(f32), 0.0).astype(bf16)
    weight_ref[768:896, :] = step_w
    gate = dot1(embed, gate_w, NT)
    x = dot1(embed, x_w, NT)
    bc = dot1(embed, bc_w, NT)
    tab_ref[:, :256] = gate
    tab_ref[:, 256:512] = x
    tab_ref[:, 512:768] = bc
    row = iota((8, 128), 0)
    lane = iota((8, 128), 1)
    valid = (row >= 1) & (row <= 5)
    pre = dot1(embed, step_w, NT) + heads_ref[0:1, :]
    valid = valid & (lane < HEADS)
    step = jnp.maximum(pre, 0.0) + jnp.log1p(jnp.exp(-jnp.abs(pre)))
    rate = jnp.exp(heads_ref[1:2, :])
    logs = jnp.where(valid, -(rate * step), 0.0)
    step = jnp.where(valid, step, 0.0)
    bent = jnp.where(valid, sigmoid(pre), 0.0)
    widen = ones_where(iota((128, 256), 0) == rank * 4 + iota((128, 256), 1) // HDIM)
    step_wide = dot_exact(step, widen)
    logs_wide = dot_exact(logs, widen)
    wide_ref[0:8, :] = dot_exact(bent, widen)
    wide_ref[8:16, :] = logs_wide
    others = jnp.where(row == 0, rate, jnp.where(row == 1, heads_ref[2:3, :], 0.0))
    others = jnp.where(lane < HEADS, others, 0.0)
    wide_ref[16:24, :] = dot_exact(others, widen)
    one_row = iota((8, 256), 0) == 6
    conv_x = conv_x_ref[...]
    conv_bc = conv_bc_ref[...]
    taps = []
    for k in range(4):
        tap_x = conv_x[k : k + 1] * x
        tap_bc = conv_bc[k : k + 1] * bc
        if k == 0:
            tap_x = jnp.where(one_row, bias_x_ref[...], tap_x)
            tap_bc = jnp.where(one_row, bias_bc_ref[...], tap_bc)
        taps.append(jnp.concatenate([tap_x, tap_bc], axis=1))
    silu_gate = gate * sigmoid(gate)

    def put(ref, start, pieces):
        nothing = jnp.zeros(pieces[0][1].shape, f32)
        pieces = dict(pieces)
        table = jnp.concatenate([pieces.get(k, nothing) for k in range(8)], axis=0)
        high, low = halves(table)
        ref[0:64, start : start + table.shape[1]] = high
        ref[64:128, start : start + table.shape[1]] = low
        return high, low

    first_high, first_low = put(big_ref, 0, list(enumerate(taps)))
    put(big_ref, 512, [(4 + k, tap) for k, tap in enumerate(taps)])
    step_high, step_low = put(big_ref, 1024, [(3, step_wide)])
    put(big_ref, 1280, [(7, step_wide)])
    put(big_ref, 1536, [(3, silu_gate)])
    put(big_ref, 1792, [(7, silu_gate)])
    put(logs_ref, 0, [(3, logs_wide)])
    put(logs_ref, 256, [(7, logs_wide)])
    pick = ones_where((iota((8, 128), 1) == rank * 4 + row) & (row < 4))
    nothing = jnp.zeros((8, 128), f32)
    for branch in range(2):
        spot = 3 + 4 * branch
        rows = jnp.concatenate([logs if k % 8 == spot else nothing for k in range(16)], axis=0)
        first = rows.astype(bf16)
        rest = rows - first.astype(f32)
        second = rest.astype(bf16)
        third = rest - second.astype(f32)
        values = dot1(pick, first, NT) + (dot1(pick, second, NT) + dot1(pick, third, NT))
        high = values.astype(bf16).astype(f32)
        lrow_ref[8 * branch : 8 * branch + 8, :] = jnp.where(lane < 64, high, values - high)
    grams = goh_ref[...]
    pre = dot1(grams, big_ref[:, :384])
    logistic = sigmoid(pre)
    gact_ref[...] = pre * logistic
    gbend_ref[...] = logistic * (1.0 + pre * (1.0 - logistic))
    gstep_ref[...] = dot1(grams, big_ref[:, 1024:1280])


def shifted(symbols, by):
    row = iota((128, 128), 0)
    col = iota((128, 128), 1)
    if by > 0:
        rolled = pltpu.roll(symbols, by, axis=1)
        other = jnp.where(row == 0, 0, pltpu.roll(rolled, 1, axis=0))
        return jnp.where(col < by, other, rolled)
    rolled = pltpu.roll(symbols, 128 + by, axis=1)
    other = jnp.where(row == 127, 0, pltpu.roll(rolled, 127, axis=0))
    return jnp.where(col >= 128 + by, other, rolled)


def read_symbols(
    seq, ids_ref, ca_ref, cb_ref, taps_ref, oh_ref, oht_ref
):
    symbols = ids_ref[...] + 1
    taps = [shifted(symbols, 3 - k) if k < 3 else symbols for k in range(4)]
    turned = [complement_padded(shifted(symbols, k - 3) if k < 3 else symbols) for k in range(4)]
    row = iota((128, 128), 0)
    is_before = row < seq * 8
    far = [jnp.where(is_before, a, b) for a, b in zip(taps, turned)]
    ca_ref[...] = encode(far[0], far[1])
    cb_ref[...] = encode(far[2], far[3])
    for k in range(4):
        taps_ref[k] = taps[k]
        taps_ref[4 + k] = turned[k]
    at = pl.ds(pl.multiple_of(seq * 8, 8), 8)
    own = [taps_ref[k, at, :] for k in range(8)]
    sub = iota((8, 128), 0)
    for j in range(8):
        groups = []
        for k in range(8):
            hit = (own[k][j : j + 1] == sub) & (sub > 0)
            if k % 4 == 0:
                hit = hit | (sub == 6)
            groups.append(jnp.where(hit, 1.0, 0.0))
        rows = jnp.concatenate(groups + groups, axis=0)
        cols = slice(128 * j, 128 * j + 128)
        oht_ref[:, cols] = rows.astype(bf16)
        oh_ref[cols, :] = jnp.transpose(rows).astype(bf16)
    is_own = (row >= seq * 8) & (row < seq * 8 + 8)
    return jnp.where(is_own, 0, far[3])


def forward_kernel(
    at_ref, ids_ref, tt_ref, lx_ref, lrow_ref, wide_ref, gact_ref, gstep_ref,
    y_ref, states_ref, sums_ref, decay_ref, after_ref, oh_ref, oht_ref, ca_ref, cb_ref,
    taps_ref, lhs_ref, rhs_ref, carry_ref,
):
    seq = at_ref[0]
    first = seq * 8
    symbols = read_symbols(seq, ids_ref, ca_ref, cb_ref, taps_ref, oh_ref, oht_ref)
    log_small = lrow_ref[0:8, :] + pltpu.roll(lrow_ref[0:8, :], 64, axis=1)
    row = iota((128, 128), 0)
    col = iota((128, 128), 1)
    upto = ones_where(row <= col)
    every = jnp.ones((128, 128), bf16)
    signs = (jnp.where(col < row, 1.0, 0.0) - jnp.where(col < first, 1.0, 0.0)).astype(bf16)
    is_before = row < first
    logs = [jnp.zeros((128, 128), f32) for _ in range(4)]
    for symbol in range(1, 6):
        here = symbols == symbol
        found = ones_where(here)
        within = dot1(found, upto)
        total = dot1(found, every)
        upper = within + dot1(signs, total)
        after = jnp.where(is_before, -upper, upper - jnp.where(here, 1.0, 0.0))
        after_ref[symbol - 1] = after
        for h in range(4):
            logs[h] = logs[h] + after * log_small[h : h + 1, 24 + symbol : 25 + symbol]
    for h in range(4):
        decay = jnp.where(symbols > 0, jnp.exp(logs[h]), 0.0)
        decay_ref[h] = decay
    codes = iota((CODES, 128), 0)

    def add_shard(shard, total):
        at = pl.ds(pl.multiple_of(shard * 8, 8), 8)
        early = ca_ref[at, :]
        late = cb_ref[at, :]
        for j in range(8):
            cols = slice(128 * j, 128 * j + 128)
            rhs_ref[:, cols] = ones_where(early[j : j + 1] == codes)
            mine = late[j : j + 1] == codes
            for h in range(4):
                lhs_ref[32 * h : 32 * h + 32, cols] = jnp.where(
                    mine, decay_ref[h, at, :][j : j + 1], 0.0
                ).astype(bf16)
        return total + dot1(rhs_ref[...], lhs_ref[...], NT)

    zero = jnp.zeros((CODES, 128), f32)
    both = (
        lax.fori_loop(0, seq, add_shard, zero),
        lax.fori_loop(seq + 1, 16, add_shard, zero),
    )
    gram_b = gact_ref[:, 256:384]
    gram_xs = gact_ref[:, :256] * gstep_ref[...]
    skip = wide_ref[17:18, :]
    row = iota((BLOCK, BLOCK), 0)
    col = iota((BLOCK, BLOCK), 1)
    for branch in range(2):
        sums = both[branch]
        sums_ref[branch] = sums
        weights = expand_grams(sums)
        carry_ref[...] = dot3(gram_b, weights * gram_xs, TN)
        causal = row >= col if branch == 0 else row <= col

        def block_step(k, unused, branch=branch, causal=causal):
            block = k if branch == 0 else 3 - k
            rows = pl.ds(pl.multiple_of(block * BLOCK, BLOCK), BLOCK)
            onehot_t, pre, step, counts_t, log_wide, log_rows = scan_inputs(
                oh_ref, oht_ref, tt_ref, lx_ref, lrow_ref, rows, branch
            )
            act = pre * sigmoid(pre)
            x = act[:, :256]
            b = act[:, 256:384]
            c = act[:, 384:]
            xs = x * step
            state = carry_ref[...]
            states_ref[branch * 4 + block] = state
            inner = dot3(c, b, NT)
            parts = []
            for h in range(4):
                decays = jnp.exp(
                    jnp.where(
                        causal,
                        log_wide[:, h * HDIM : h * HDIM + 1]
                        - log_rows[branch * 8 + h : branch * 8 + h + 1, :],
                        -1e30,
                    )
                )
                parts.append(dot1(inner * decays, xs[:, h * HDIM : (h + 1) * HDIM]))
            within = jnp.concatenate(parts, axis=1)
            y = within + dot3(c, state) * jnp.exp(log_wide)
            y_ref[branch, rows, :] = y + skip * x
            edge = log_wide[BLOCK - 1 :] if branch == 0 else log_wide[:1]
            carry_ref[...] = jnp.exp(edge) * state + dot3(b, jnp.exp(edge - log_wide) * xs, TN)
            return unused

        lax.fori_loop(0, 4, block_step, 0)


def slope_kernel(at_ref, y_ref, oh_ref, tt_ref, cot_ref, ow_ref, gain_ref, slope_ref, sums_ref):
    slope = lax.dot_general(cot_ref[...], ow_ref[...], NT, preferred_element_type=f32)
    slope_ref[...] = slope
    weighted = slope * gain_ref[...]
    for branch in range(2):
        gate = dot1(oh_ref[...], tt_ref[:, 1536 + 256 * branch : 1792 + 256 * branch])
        g = y_ref[branch] * gate
        for kind, product in enumerate((g * g, weighted * g)):
            at = 2 * branch + kind
            product = product[:, :128] + product[:, 128:]
            for j in range(8):
                cols = slice(128 * j, 128 * j + 128)
                total = jnp.sum(jnp.transpose(product[cols]), axis=0, keepdims=True)
                for peer in range(sums_ref.shape[0]):
                    sums_ref[peer, at : at + 1, cols] = total


def mix_kernel(
    at_ref, y_ref, oh_ref, oht_ref, tt_ref, slope_ref, gain_ref, sums_ref,
    mixed_ref, dy_ref, dgate_ref, dgain_ref,
    cols_ref,
):
    gain = gain_ref[...]
    slope = slope_ref[...]
    sums = sums_ref[0]
    for peer in range(1, sums_ref.shape[0]):
        sums = sums + sums_ref[peer]
    scale = lax.rsqrt(sums / INNER + EPSILON)
    crossed = jnp.concatenate([sums[1:2], sums[1:2], sums[3:4], sums[3:4]], axis=0)
    weight = scale * scale * scale * crossed / INNER
    kind = iota(sums.shape, 0)
    weight = jnp.concatenate([weight[0:1], weight[0:1], weight[2:3], weight[2:3]], axis=0)
    rows = jnp.where(kind % 2 == 0, scale, weight)
    rows = jnp.concatenate([rows, rows] * 16, axis=0)
    for j in range(8):
        cols = slice(128 * j, 128 * j + 128)
        cols_ref[cols, :] = jnp.transpose(rows[:, cols])
    sloped = slope * gain
    total = None
    for branch in range(2):
        gate = dot1(oh_ref[...], tt_ref[:, 1536 + 256 * branch : 1792 + 256 * branch])
        y = y_ref[branch]
        g = y * gate
        scale = cols_ref[:, 2 * branch : 2 * branch + 1]
        weight = cols_ref[:, 2 * branch + 1 : 2 * branch + 2]
        normed = g * scale
        total = normed if total is None else total + normed
        dg = scale * sloped - weight * g
        dy_ref[branch] = dg * gate
        lanes = oht_ref[32 * branch : 32 * branch + 32, :]
        dgate_ref[branch] = dot2(lanes, dg * y)
    mixed_ref[...] = (total * gain).astype(bf16)
    dgain_ref[...] = jnp.sum(slope * total, axis=0, keepdims=True)


def backward_scan(
    branch, oh_ref, oht_ref, tt_ref, lx_ref, lrow_ref, wide_ref, y_ref, states_ref, dy_ref,
    tables_ref, steps_ref, logs_ref, skips_ref, carry_ref,
):
    skip = wide_ref[17:18, :]
    row = iota((BLOCK, BLOCK), 0)
    col = iota((BLOCK, BLOCK), 1)
    causal = row <= col if branch == 0 else row >= col
    carry_ref[...] = jnp.zeros_like(carry_ref)

    def block_step(k, unused):
        block = 3 - k if branch == 0 else k
        later = jnp.minimum(block + 1, 3) if branch == 0 else jnp.maximum(block - 1, 0)
        rows = pl.ds(pl.multiple_of(block * BLOCK, BLOCK), BLOCK)
        onehot_t, pre, step, counts_t, log_wide, log_rows = scan_inputs(
            oh_ref, oht_ref, tt_ref, lx_ref, lrow_ref, rows, branch
        )
        lanes = slice(32 * branch, 32 * branch + 32)
        onehot_t = onehot_t[lanes]
        counts_t = counts_t[lanes]
        logistic = sigmoid(pre)
        act = pre * logistic
        bend = logistic * (1.0 + pre * (1.0 - logistic))
        x = act[:, :256]
        b = act[:, 256:384]
        c = act[:, 384:]
        xs = x * step
        dy = dy_ref[branch, rows, :]
        own = y_ref[branch, rows, :] - skip * x
        state = states_ref[branch * 4 + block]
        pull = carry_ref[...]
        xs_low = xs.astype(bf16)
        dy_low = dy.astype(bf16)
        inner = dot3(b, c, NT)
        parts = []
        slopes = jnp.zeros((BLOCK, BLOCK), f32)
        for h in range(4):
            wide = slice(h * HDIM, (h + 1) * HDIM)
            decays = jnp.exp(
                jnp.where(
                    causal,
                    log_rows[branch * 8 + h : branch * 8 + h + 1, :]
                    - log_wide[:, h * HDIM : h * HDIM + 1],
                    -1e30,
                )
            )
            parts.append(dot1(inner * decays, dy_low[:, wide]))
            slopes = slopes + dot1(xs_low[:, wide], dy_low[:, wide], NT) * decays
        within = jnp.concatenate(parts, axis=1)
        faded = jnp.exp(log_wide) * dy
        edge = log_wide[BLOCK - 1 :] if branch == 0 else log_wide[:1]
        tail = jnp.exp(edge - log_wide)
        db = dot1(slopes, c) + dot1(tail * xs, pull, NT)
        dc = dot1(slopes, b, TN) + dot1(faded, state, NT)
        dxs = within + tail * dot1(b, pull)
        dlog = dy_low.astype(f32) * own - xs_low.astype(f32) * dxs
        edge_count = counts_t[:, BLOCK - 1 :] if branch == 0 else counts_t[:, :1]
        ahead = jnp.sum(states_ref[branch * 4 + later] * pull, axis=0, keepdims=True)
        logs_ref[...] += dot2(counts_t, dlog) + edge_count * ahead
        carry_ref[...] = dot1(c, faded, TN) + jnp.exp(edge) * pull
        dpre = jnp.concatenate([step * dxs + skip * dy, db, dc], axis=1) * bend
        tables_ref[...] += dot2(onehot_t, dpre)
        steps_ref[...] += dot2(onehot_t, x * dxs)
        skips_ref[...] += jnp.sum(dy * x, axis=0, keepdims=True)
        return unused

    lax.fori_loop(0, 4, block_step, 0)


def first_backward_kernel(
    at_ref, oh_ref, oht_ref, tt_ref, lx_ref, lrow_ref, wide_ref, y_ref, states_ref, dy_ref,
    cot_ref, mixed_ref,
    tables_ref, steps_ref, logs_ref, skips_ref, pull_ref, outer_ref,
):
    for ref in (tables_ref, steps_ref, logs_ref, skips_ref):
        ref[...] = jnp.zeros_like(ref)
    backward_scan(
        0, oh_ref, oht_ref, tt_ref, lx_ref, lrow_ref, wide_ref, y_ref, states_ref, dy_ref,
        tables_ref, steps_ref, logs_ref, skips_ref, pull_ref,
    )
    outer_ref[...] = lax.dot_general(cot_ref[...], mixed_ref[...], TN, preferred_element_type=f32)


def second_backward_kernel(
    at_ref, ca_ref, cb_ref, oh_ref, oht_ref, goht_ref, tt_ref, lx_ref, lrow_ref, wide_ref,
    y_ref, states_ref, sums_ref, decay_ref, after_ref, dy_ref, gact_ref, gbend_ref, gstep_ref,
    tab_ref, weight_ref, cot_ref, conv_x_ref, conv_bc_ref, dgate_ref, dgain_ref,
    tables_in_ref, steps_in_ref, logs_in_ref, skips_in_ref, pull_in_ref,
    packed_ref,
    pull_ref, mark_ref, found_ref, tables_ref, steps_ref, logs_ref, skips_ref,
):
    tables_ref[...] = tables_in_ref[...]
    steps_ref[...] = steps_in_ref[...]
    logs_ref[...] = logs_in_ref[...]
    skips_ref[...] = skips_in_ref[...]
    backward_scan(
        1, oh_ref, oht_ref, tt_ref, lx_ref, lrow_ref, wide_ref, y_ref, states_ref, dy_ref,
        tables_ref, steps_ref, logs_ref, skips_ref, pull_ref,
    )
    seq = at_ref[0]
    gram_x = gact_ref[:, :256]
    gram_b = gact_ref[:, 256:]
    gram_step = gstep_ref[...]
    gram_xs = gram_x * gram_step
    dxs = jnp.zeros((CODES * CODES, 256), f32)
    db = jnp.zeros((CODES * CODES, 128), f32)
    found = []
    for branch in range(2):
        pull = (pull_in_ref, pull_ref)[branch][...]
        weights = expand_grams(sums_ref[branch])
        met = dot1(gram_b, pull)
        dxs = dxs + weights * met
        db = db + dot1(weights * gram_xs, pull, NT)
        found.append(gather_grams(gram_xs * met))
    dpre = jnp.concatenate([gram_step * dxs, db], axis=1) * gbend_ref[...]
    gram_t = goht_ref[...]
    tables_ref[:, :384] += dot2(gram_t, dpre)
    steps_ref[...] += dot2(gram_t, gram_x * dxs)
    codes = iota((CODES, 128), 0)

    def look_up(branch):
        table = found[branch].astype(bf16)

        def one_shard(shard, unused):
            at = pl.ds(pl.multiple_of(shard * 8, 8), 8)
            early = ca_ref[at, :]
            late = cb_ref[at, :]
            for j in range(8):
                mark_ref[:, 128 * j : 128 * j + 128] = ones_where(early[j : j + 1] == codes)
            marks = mark_ref[...]
            looked = dot1(table, marks, TN)
            for h in range(4):
                rows = []
                for j in range(8):
                    part = looked[32 * h : 32 * h + 32, 128 * j : 128 * j + 128]
                    mine = late[j : j + 1] == codes
                    rows.append(jnp.sum(jnp.where(mine, part, 0.0), axis=0, keepdims=True))
                found_ref[h, at, :] = jnp.concatenate(rows, axis=0)
            return unused

        return one_shard

    found_ref[...] = jnp.zeros_like(found_ref)
    lax.fori_loop(0, seq, look_up(0), 0)
    lax.fori_loop(seq + 1, 16, look_up(1), 0)
    lane_head = iota((1, 256), 1) // HDIM
    sub = iota((8, 256), 0)
    far = jnp.zeros((8, 256), f32)
    for h in range(4):
        weighted = found_ref[h] * decay_ref[h]
        for symbol in range(5):
            total = jnp.sum(weighted * after_ref[symbol], axis=0, keepdims=True)
            total = jnp.sum(total, axis=1, keepdims=True)
            far = far + jnp.where((lane_head == h) & (sub == symbol + 1), total, 0.0)

    gate_tab = tab_ref[:, :256]
    x_tab = tab_ref[:, 256:512]
    bc_tab = tab_ref[:, 512:768]
    logistic = sigmoid(gate_tab)
    gate_part = (dgate_ref[0, 24:32, :] + dgate_ref[1, 24:32, :]) * (
        logistic * (1.0 + gate_tab * (1.0 - logistic))
    )
    conv_x = conv_x_ref[...]
    conv_bc = conv_bc_ref[...]
    x_part = jnp.zeros((8, 256), f32)
    bc_part = jnp.zeros((8, 256), f32)
    x_taps = []
    bc_taps = []
    for k in range(KCONV):
        dtap_x = tables_ref[8 * k : 8 * k + 8, :256]
        dtap_bc = tables_ref[8 * k : 8 * k + 8, 256:]
        x_part = x_part + conv_x[k : k + 1] * dtap_x
        bc_part = bc_part + conv_bc[k : k + 1] * dtap_bc
        x_taps.append(jnp.sum(dtap_x * x_tab, axis=0, keepdims=True))
        bc_taps.append(jnp.sum(dtap_bc * bc_tab, axis=0, keepdims=True))
    bias = tables_ref[6:7, :]
    same = ones_where(iota((256, 256), 0) // HDIM == iota((256, 256), 1) // HDIM)
    log_part = dot_exact(logs_ref[24:32, :], same) + far
    step_part = dot_exact(steps_ref[24:32, :], same) - wide_ref[16:17, :] * log_part
    step_part = step_part * wide_ref[0:8, :]
    rate_part = jnp.sum(log_part * wide_ref[8:16, :], axis=0, keepdims=True)
    skip_part = dot_exact(jnp.broadcast_to(skips_ref[...], (8, 256)), same)
    valid = (sub >= 1) & (sub <= 5)
    step_part = jnp.where(valid, step_part, 0.0)
    step_rows = jnp.where(
        sub == 0,
        jnp.sum(step_part, axis=0, keepdims=True),
        jnp.where(sub == 6, rate_part, jnp.where(sub == 7, skip_part, step_part)),
    )
    rank = at_ref[1]
    spread = iota((256, 128), 1)
    narrow = ones_where(
        (iota((256, 128), 0) % HDIM == 0)
        & (rank * 4 + iota((256, 128), 0) // HDIM == spread)
    )
    step_heads = dot_exact(step_rows, narrow)

    def against(part, first, last):
        first_piece = part.astype(bf16)
        rest = part - first_piece.astype(f32)
        second_piece = rest.astype(bf16)
        third_piece = rest - second_piece.astype(f32)
        weights = weight_ref[first:last, :]
        return dot1(first_piece, weights) + (
            dot1(second_piece, weights) + dot1(third_piece, weights)
        )

    tokens = oht_ref[16:32, pl.ds(pl.multiple_of(rank * 128, 128), 128)]
    embed_part = (
        dot1(tokens, cot_ref[...])[8:]
        + against(jnp.where(valid, gate_part, 0.0), 0, 256)
        + against(jnp.where(valid, x_part, 0.0), 256, 512)
        + against(jnp.where(valid, bc_part, 0.0), 512, 768)
        + against(jnp.where(valid[:, :128], step_heads, 0.0), 768, 896)
    )

    def rows_of(part, zero, six, seven):
        return jnp.where(
            sub == 0, zero, jnp.where(sub == 6, six, jnp.where(sub == 7, seven, part))
        )

    gate_rows = rows_of(gate_part, x_taps[0], x_taps[1], x_taps[2])
    x_rows = rows_of(x_part, x_taps[3], bias[:, :256], dgain_ref[...])
    bc_rows = rows_of(bc_part, bc_taps[0], bc_taps[1], bc_taps[2])
    embed_first = rows_of(embed_part[:, :256], bc_taps[3], bias[:, 256:], 0.0)
    for half in range(2):
        cols = slice(128 * half, 128 * half + 128)
        packed_ref[half] = gate_rows[:, cols]
        packed_ref[2 + half] = x_rows[:, cols]
        packed_ref[4 + half] = bc_rows[:, cols]
        packed_ref[7 + half] = embed_first[:, cols]
    packed_ref[6] = step_heads
    for piece in range(2, 8):
        packed_ref[7 + piece] = embed_part[:, 128 * piece : 128 * piece + 128]
    packed_ref[15] = jnp.zeros((8, 128), f32)


def out_kernel(mixed_ref, ow_ref, token_ref, embed_ref, out_ref):
    total = dot1(token_ref[...], embed_ref[...])
    for peer in range(mixed_ref.shape[0]):
        total = total + dot1(mixed_ref[peer], ow_ref[256 * peer : 256 * peer + 256, :])
    out_ref[...] = total.astype(bf16)


def sum_kernel(pieces_ref, spread_ref):
    total = pieces_ref[0]
    for k in range(1, pieces_ref.shape[0]):
        total = total + pieces_ref[k]
    spread_ref[...] = jnp.broadcast_to(total[None], spread_ref.shape)


def final_kernel(
    whole_ref, embed_ref,
    w_in_ref, embedding_ref, conv_ref, bias_ref, dt_ref, rate_ref, skip_ref, gain_ref,
):
    def summed(piece):
        total = whole_ref[8 * piece]
        for k in range(1, 8):
            total = total + whole_ref[8 * piece + k]
        return total

    embed = embed_ref[...]

    def outer(table, first):
        one = table.astype(bf16)
        rest = table - one.astype(f32)
        two = rest.astype(bf16)
        three = rest - two.astype(f32)
        pieces = jnp.concatenate([one.astype(f32), two.astype(f32), three], axis=0)
        value = dot1(embed, pieces)
        w_in_ref[:, first : first + table.shape[1]] = value

    for rank in range(8):
        for half in range(2):
            gate = whole_ref[8 * half + rank]
            x = whole_ref[8 * (2 + half) + rank]
            at = 256 * rank + 128 * half
            cols = slice(at, at + 128)
            outer(gate, at)
            outer(x, INNER + at)
            conv_ref[0:1, cols] = gate[0:1]
            conv_ref[1:2, cols] = gate[6:7]
            conv_ref[2:3, cols] = gate[7:8]
            conv_ref[3:4, cols] = x[0:1]
            bias_ref[:, cols] = x[6:7]
            gain_ref[:, cols] = x[7:8]
    for half in range(2):
        bc = summed(4 + half)
        at = INNER + 128 * half
        cols = slice(at, at + 128)
        outer(bc, INNER + at)
        rest = summed(7 + half)
        conv_ref[0:1, cols] = bc[0:1]
        conv_ref[1:2, cols] = bc[6:7]
        conv_ref[2:3, cols] = bc[7:8]
        conv_ref[3:4, cols] = rest[0:1]
        bias_ref[:, cols] = rest[6:7]
    steps = summed(6)[:, :HEADS]
    outer(steps, 2 * INNER + 2 * STATE)
    dt_ref[...] = steps[0:1]
    rate_ref[...] = steps[6:7]
    skip_ref[...] = steps[7:8]
    for piece in range(8):
        embedding_ref[:, 128 * piece : 128 * piece + 128] = summed(7 + piece)[1:6]


VMEM = pl.BlockSpec(memory_space=pltpu.VMEM)


def whole(array):
    zeros = (0,) * array.ndim
    return pl.BlockSpec(array.shape, lambda i, at: zeros)


def own(shape, index):
    return pl.BlockSpec(shape, index)


def call(kernel, at, operands, outs, scratch=(), cost=5e9):
    arrays = [item[0] if isinstance(item, tuple) else item for item in operands]
    specs = [
        own(item[1], item[2]) if isinstance(item, tuple) else whole(item) for item in operands
    ]
    shapes = [jax.ShapeDtypeStruct(shape, kind) for shape, kind in outs]
    return pl.pallas_call(
        kernel,
        out_shape=shapes,
        grid_spec=pltpu.PrefetchScalarGridSpec(
            num_scalar_prefetch=1,
            grid=(1,),
            in_specs=specs,
            out_specs=[whole(shape) for shape in shapes],
            scratch_shapes=list(scratch),
        ),
        compiler_params=pltpu.CompilerParams(vmem_limit_bytes=58 * 1024 * 1024),
        cost_estimate=pl.CostEstimate(flops=int(cost), bytes_accessed=4000000, transcendentals=0),
    )(at, *arrays)


def call_plain(kernel, operands, outs, cost=1e9):
    return pl.pallas_call(
        kernel,
        out_shape=[jax.ShapeDtypeStruct(shape, kind) for shape, kind in outs],
        in_specs=[VMEM] * len(operands),
        out_specs=[VMEM] * len(outs),
        compiler_params=pltpu.CompilerParams(vmem_limit_bytes=48 * 1024 * 1024),
        cost_estimate=pl.CostEstimate(flops=int(cost), bytes_accessed=1000000, transcendentals=0),
    )(*operands)


def gather(shard, axis):
    devices = lax.axis_size(axis)
    spread = jnp.broadcast_to(shard[None], (devices,) + shard.shape)
    return lax.all_to_all(spread, axis, split_axis=0, concat_axis=0, tiled=True)


def exchange(array, axis):
    return lax.all_to_all(array, axis, split_axis=0, concat_axis=0, tiled=True)


def body(
    base_ids, embedding, in_weight, conv_weight, conv_bias, dt_bias, a_log, skip_weight, norm_gain,
    out_weight, cotangent,
):
    groups = lax.axis_size("head")
    shards = lax.axis_size("seq")
    width = HEADS // groups * HDIM
    head_rank = lax.axis_index("head")
    seq_rank = lax.axis_index("seq")
    length = base_ids.shape[0]
    token_rows = length // groups
    at = jnp.stack([seq_rank, head_rank]).astype(jnp.int32)

    ids = gather(base_ids.reshape(8, 128), "seq").reshape(128, 128)
    cot_spread = jnp.broadcast_to(cotangent[None], (groups,) + cotangent.shape)

    weight_t = in_weight.T
    heads = jnp.pad(jnp.stack([dt_bias, a_log, skip_weight]), ((0, 5), (0, 128 - HEADS)))
    bias_row = conv_bias[None, :]
    gain_row = norm_gain[None, :]
    grams = _gram_onehot()
    gram_rows = jnp.asarray(grams, bf16)
    gram_cols = jnp.asarray(np.ascontiguousarray(grams[:, :32].T), bf16)
    conv_x = (conv_weight, (KCONV, width), lambda i, at: (0, at[1]))
    conv_bc = (conv_weight, (KCONV, width), lambda i, at: (0, INNER // width))
    count = CODES * CODES
    big, logs, log_rows, tab, wide, weight_own, gact, gbend, gstep = call(
        prep_kernel,
        at,
        [
            embedding,
            (weight_t, (width, D), lambda i, at: (at[1], 0)),
            (weight_t, (width, D), lambda i, at: (INNER // width + at[1], 0)),
            (weight_t, (256, D), lambda i, at: (16, 0)),
            (weight_t, (128, D), lambda i, at: (34, 0)),
            conv_x,
            conv_bc,
            (bias_row, (1, width), lambda i, at: (0, at[1])),
            (bias_row, (1, width), lambda i, at: (0, INNER // width)),
            heads,
            gram_rows,
        ],
        [
            ((128, 2048), bf16),
            ((128, 512), bf16),
            ((16, 128), f32),
            ((8, 768), f32),
            ((24, width), f32),
            ((896, D), bf16),
            ((count, 384), f32),
            ((count, 384), f32),
            ((count, width), f32),
        ],
        cost=3e9,
    )

    ids, cot_spread, big = lax.optimization_barrier((ids, cot_spread, big))
    cot_all = exchange(cot_spread, "head").reshape(length, D)
    y, states, sums, decays, after, onehot, onehot_t, early, late = call(
        forward_kernel,
        at,
        [ids, big, logs, log_rows, wide, gact, gstep],
        [
            ((2, length, width), f32),
            ((8, STATE, width), f32),
            ((2, CODES, 128), f32),
            ((4, 128, 128), f32),
            ((5, 128, 128), f32),
            ((length, 128), bf16),
            ((128, length), bf16),
            ((128, 128), jnp.int32),
            ((128, 128), jnp.int32),
        ],
        [
            pltpu.VMEM((8, 128, 128), jnp.int32),
            pltpu.VMEM((128, 1024), bf16),
            pltpu.VMEM((32, 1024), bf16),
            pltpu.VMEM((STATE, width), f32),
        ],
        cost=1.5e10,
    )

    gain_own = (gain_row, (1, width), lambda i, at: (0, at[1]))
    slope, row_sums = call(
        slope_kernel,
        at,
        [y, onehot, big, cot_all, (out_weight, (width, D), lambda i, at: (at[1], 0)), gain_own],
        [((length, width), f32), ((groups, 4, length), f32)],
        cost=4e9,
    )
    row_sums = exchange(row_sums, "head")
    mixed, dy, dgate, dgain = call(
        mix_kernel,
        at,
        [y, onehot, onehot_t, big, slope, gain_own, row_sums],
        [
            ((length, width), bf16),
            ((2, length, width), f32),
            ((2, 32, width), f32),
            ((1, width), f32),
        ],
        [pltpu.VMEM((length, 128), f32)],
        cost=4e9,
    )

    mixed_all = exchange(mixed.reshape(groups, token_rows, width), "head")
    shared = [onehot, onehot_t, big, logs, log_rows, wide, y, states]
    accumulators = [((32, 512), f32), ((32, width), f32), ((32, width), f32), ((1, width), f32)]
    *grads, pull, partial = call(
        first_backward_kernel,
        at,
        shared + [dy, cot_all, mixed],
        accumulators + [((STATE, width), f32), ((D, width), f32)],
        cost=1.5e10,
    )
    mixed_all, partial, pull = lax.optimization_barrier((mixed_all, partial, pull))
    partial = exchange(partial.reshape(shards, D // shards, width), "seq")
    (packed,) = call(
        second_backward_kernel,
        at,
        [
            early, late, onehot, onehot_t, gram_cols, big, logs, log_rows, wide, y, states, sums,
            decays, after, dy, gact, gbend, gstep, tab, weight_own, cotangent, conv_x, conv_bc,
            dgate, dgain, *grads, pull,
        ],
        [((shards, 8, 128), f32)],
        [
            pltpu.VMEM((STATE, width), f32),
            pltpu.VMEM((32, 1024), bf16),
            pltpu.VMEM((4, 128, 128), f32),
            *[pltpu.VMEM(shape, kind) for shape, kind in accumulators],
        ],
        cost=2e10,
    )
    packed, partial = lax.optimization_barrier((packed, partial))

    grad_w_out = jnp.sum(partial, axis=0).T
    token_ids = lax.dynamic_slice_in_dim(base_ids, head_rank * token_rows, token_rows, 0)
    alphabet = jnp.arange(5, dtype=jnp.int32)
    token_hot = (token_ids[:, None] == alphabet[None, :]).astype(bf16)
    (layer_out,) = call_plain(
        out_kernel,
        [mixed_all, out_weight, token_hot, embedding],
        [((token_rows, D), bf16)],
        4e9,
    )

    pieces = exchange(packed, "seq")
    (spread,) = call_plain(sum_kernel, [pieces], [((shards * groups, 8, 128), f32)], 1e8)
    everything = exchange(spread, ("seq", "head"))
    row_count = D // shards
    columns = lax.dynamic_slice_in_dim(embedding, seq_rank * row_count, row_count, 1)
    columns = jnp.pad(columns, ((1, 2), (0, 0)))
    columns = jnp.concatenate([columns] * 3, axis=0).T
    w_in, embed, conv, bias, dt, rate, skip, gain = call_plain(
        final_kernel,
        [everything, columns],
        [
            ((row_count, in_weight.shape[1]), f32),
            (embedding.shape, f32),
            (conv_weight.shape, f32),
            ((1, conv_bias.shape[0]), f32),
            ((1, HEADS), f32),
            ((1, HEADS), f32),
            ((1, HEADS), f32),
            ((1, INNER), f32),
        ],
    )
    return (
        layer_out, w_in, grad_w_out, embed, conv, bias[0], dt[0], rate[0], skip[0], gain[0],
    )


def solution(mesh):
    return jax.shard_map(
        body,
        mesh=mesh,
        in_specs=(P("seq"), P(), P(), P(), P(), P(), P(), P(), P(), P(), P(("seq", "head"), None)),
        out_specs=(
            P(("seq", "head"), None),
            P("seq", None),
            P("head", "seq"),
            P(),
            P(),
            P(),
            P(),
            P(),
            P(),
            P(),
        ),
        check_vma=False,
    )
```

```python
import jax
import jax.numpy as jnp
import numpy as np
from jax import lax
from jax.experimental import pallas as pl
from jax.experimental.pallas import tpu as pltpu
from jax.sharding import PartitionSpec as P

D = 1024
HEADS = 32
HDIM = 64
STATE = 128
BLOCK = 256
KCONV = 4
INNER = 2048
EPSILON = 1e-05
LOG2E = 1.4426950408889634

f32 = jnp.float32
bf16 = jnp.bfloat16
NN = (((1,), (0,)), ((), ()))
NT = (((1,), (1,)), ((), ()))
TN = (((0,), (0,)), ((), ()))

CODES = 32


def _decode_codes():
    first = np.zeros((CODES,), np.int32)
    second = np.zeros((CODES,), np.int32)
    for code in range(25):
        first[code], second[code] = code // 5 + 1, code % 5 + 1
    for code in range(25, 30):
        second[code] = code - 24
    return first, second


def _gram_onehot():
    first, second = _decode_codes()
    early, late = np.divmod(np.arange(CODES * CODES), CODES)
    symbols = (first[early], second[early], first[late], second[late])
    rows = np.zeros((CODES * CODES, 128), np.float32)
    for tap, symbol in enumerate(symbols):
        valid = symbol > 0
        rows[np.arange(CODES * CODES)[valid], (8 * tap + symbol)[valid]] = 1.0
    rows[:, 6] = 1.0
    rows[:, 64:96] = rows[:, :32]
    return rows


def encode(earlier, later):
    return jnp.where(
        earlier > 0, (earlier - 1) * 5 + later - 1, jnp.where(later > 0, 24 + later, 30)
    )


def complement_padded(symbols):
    return jnp.where((symbols >= 1) & (symbols <= 4), 5 - symbols, symbols)


def halves(values):
    high = values.astype(bf16)
    return high, (values - high.astype(f32)).astype(bf16)


def dot1(a, b, dims=NN):
    return lax.dot_general(a.astype(bf16), b.astype(bf16), dims, preferred_element_type=f32)


def doubled(values, axis):
    return jnp.concatenate([values, values], axis=axis)


def dot2(a, b, dims=NN):
    high, low = halves(b)
    a = a.astype(bf16)
    if a.shape[dims[0][0][0]] <= 128:
        pieces = jnp.concatenate([high, low], axis=dims[0][1][0])
        return dot1(doubled(a, dims[0][0][0]), pieces, dims)
    return dot1(a, high, dims) + dot1(a, low, dims)


def dot2l(a, b, dims=NN):
    high, low = halves(a)
    b = b.astype(bf16)
    if b.shape[dims[0][1][0]] <= 128:
        pieces = jnp.concatenate([high, low], axis=dims[0][0][0])
        return dot1(pieces, doubled(b, dims[0][1][0]), dims)
    return dot1(high, b, dims) + dot1(low, b, dims)


def dot3(a, b, dims=NN):
    a_high, a_low = halves(a)
    b_high, b_low = halves(b)
    if a.shape[dims[0][0][0]] <= 128:
        pieces = jnp.concatenate([a_high, a_low], axis=dims[0][0][0])
        return dot1(pieces, doubled(b_high, dims[0][1][0]), dims) + dot1(a_high, b_low, dims)
    return dot1(a_high, b_high, dims) + (dot1(a_high, b_low, dims) + dot1(a_low, b_high, dims))


def dot_exact(a, b, dims=NN):
    first = a.astype(bf16)
    rest = a - first.astype(f32)
    second = rest.astype(bf16)
    third = rest - second.astype(f32)
    b = b.astype(bf16)
    return dot1(first, b, dims) + (dot1(second, b, dims) + dot1(third, b, dims))


def iota(shape, axis):
    return lax.broadcasted_iota(jnp.int32, shape, axis)


def ones_where(condition):
    return jnp.where(condition, 1.0, 0.0).astype(bf16)


def expand_grams(sums):
    grams = CODES * CODES
    early = ones_where(iota((grams, CODES), 0) // CODES == iota((grams, CODES), 1))
    both = dot2(early, jnp.concatenate([sums[:CODES], sums[CODES:]], axis=1))
    mine = iota((grams, 128), 0) % CODES == iota((grams, 128), 1) % CODES
    widen = ones_where(iota((128, 256), 0) // CODES == iota((128, 256), 1) // HDIM)
    return [
        dot2l(jnp.where(mine, both[:, 128 * k : 128 * k + 128], 0.0), widen) for k in range(2)
    ]


def gather_grams(values):
    grams = CODES * CODES
    narrow = ones_where(iota((256, 128), 0) // HDIM == iota((256, 128), 1) // CODES)
    mine = iota((grams, 128), 0) % CODES == iota((grams, 128), 1) % CODES
    spread = [jnp.where(mine, dot1(value, narrow), 0.0) for value in values]
    early = ones_where(iota((CODES, grams), 1) // CODES == iota((CODES, grams), 0))
    both = dot1(early, jnp.concatenate(spread, axis=1))
    return jnp.concatenate([both[:, :128], both[:, 128:]], axis=0)


def sigmoid(values):
    return 0.5 * jnp.tanh(0.5 * values) + 0.5


def scan_inputs(onehot, onehot_t, pre_tab, step_tab, log_tab, log_rows, ahead, behind):
    pre = dot1(onehot, pre_tab)
    step = dot1(onehot, step_tab)
    counts = dot1(ones_where(behind), onehot).astype(bf16)
    counts_t = dot1(onehot_t, ones_where(ahead))
    log_wide = dot1(counts, log_tab)
    log_rows = dot1(log_rows.astype(bf16), counts_t)
    return pre, step, counts_t, log_wide, log_rows


def prep_kernel(
    at_ref, embed_ref, gate_w_ref, x_w_ref, bc_w_ref, step_w_ref, conv_x_ref, conv_bc_ref,
    bias_ref, dt_ref, rate_ref, skip_ref, goh_ref,
    big_ref, logs_ref, lrow_ref, tab_ref, wide_ref, gxs_ref, gbt_ref,
):
    rank = at_ref[1]
    place = ones_where(iota((8, 5), 0) == iota((8, 5), 1) + 1)
    embed = dot1(place, embed_ref[...]).astype(bf16)
    gate_w = gate_w_ref[...]
    x_w = x_w_ref[...]
    bc_w = bc_w_ref[...]
    step_w = step_w_ref[...]
    step_w = jnp.where(iota((128, D), 0) < HEADS, step_w.astype(f32), 0.0).astype(bf16)

    def heads_row(ref):
        return jnp.concatenate([ref[...], jnp.zeros((1, 128 - HEADS), f32)], axis=1)

    bias_x = jnp.concatenate(
        [bias_ref[pl.ds(2 * rank, 1), :], bias_ref[pl.ds(2 * rank + 1, 1), :]], axis=1
    )
    bias_bc = jnp.concatenate([bias_ref[16:17, :], bias_ref[17:18, :]], axis=1)
    gate = dot1(embed, gate_w, NT)
    x = dot1(embed, x_w, NT)
    bc = dot1(embed, bc_w, NT)
    tab_ref[:, :256] = gate
    tab_ref[:, 256:512] = x
    tab_ref[:, 512:768] = bc
    row = iota((8, 128), 0)
    lane = iota((8, 128), 1)
    valid = (row >= 1) & (row <= 5)
    pre = dot1(embed, step_w, NT) + heads_row(dt_ref)
    valid = valid & (lane < HEADS)
    step = jnp.maximum(pre, 0.0) + jnp.log1p(jnp.exp(-jnp.abs(pre)))
    rate = jnp.exp(heads_row(rate_ref))
    logs = jnp.where(valid, -(rate * step), 0.0)
    step = jnp.where(valid, step, 0.0)
    bent = jnp.where(valid, sigmoid(pre), 0.0)
    widen = ones_where(iota((128, 256), 0) == rank * 4 + iota((128, 256), 1) // HDIM)
    step_wide = dot_exact(step, widen)
    logs_wide = dot_exact(logs, widen)
    logs = logs * LOG2E
    wide_ref[0:8, :] = dot_exact(bent, widen)
    wide_ref[8:16, :] = logs_wide
    others = jnp.where(row == 0, rate, jnp.where(row == 1, heads_row(skip_ref), 0.0))
    others = jnp.where(lane < HEADS, others, 0.0)
    wide_ref[16:24, :] = dot_exact(others, widen)
    one_row = iota((8, 256), 0) == 6
    conv_x = conv_x_ref[...]
    conv_bc = conv_bc_ref[...]
    taps = []
    for k in range(4):
        tap_x = conv_x[k : k + 1] * x
        tap_bc = conv_bc[k : k + 1] * bc
        if k == 0:
            tap_x = jnp.where(one_row, bias_x, tap_x)
            tap_bc = jnp.where(one_row, bias_bc, tap_bc)
        taps.append(jnp.concatenate([tap_x, tap_bc], axis=1))
    silu_gate = gate * sigmoid(gate)

    def put(ref, start, pieces):
        nothing = jnp.zeros(pieces[0][1].shape, f32)
        pieces = dict(pieces)
        table = jnp.concatenate([pieces.get(k, nothing) for k in range(8)], axis=0)
        high, low = halves(table)
        ref[0:64, start : start + table.shape[1]] = high
        ref[64:128, start : start + table.shape[1]] = low
        return high, low

    first_high, first_low = put(big_ref, 0, list(enumerate(taps)))
    put(big_ref, 512, [(4 + k, tap) for k, tap in enumerate(taps)])
    step_high, step_low = put(big_ref, 1024, [(3, step_wide)])
    put(big_ref, 1280, [(7, step_wide)])
    put(big_ref, 1536, [(3, silu_gate)])
    put(big_ref, 1792, [(7, silu_gate)])
    put(logs_ref, 0, [(3, logs_wide * LOG2E)])
    put(logs_ref, 256, [(7, logs_wide * LOG2E)])
    pick = ones_where((iota((8, 128), 1) == rank * 4 + row) & (row < 4))
    nothing = jnp.zeros((8, 128), f32)
    for branch in range(2):
        spot = 3 + 4 * branch
        rows = jnp.concatenate([logs if k % 8 == spot else nothing for k in range(16)], axis=0)
        first = rows.astype(bf16)
        rest = rows - first.astype(f32)
        second = rest.astype(bf16)
        third = rest - second.astype(f32)
        values = dot1(pick, first, NT) + (dot1(pick, second, NT) + dot1(pick, third, NT))
        high = values.astype(bf16).astype(f32)
        lrow_ref[8 * branch : 8 * branch + 8, :] = jnp.where(lane < 64, high, values - high)
    grams = goh_ref[...]
    pre = dot1(grams, big_ref[:, :384])
    act = pre * sigmoid(pre)
    for j in range(8):
        cols = slice(128 * j, 128 * j + 128)
        gbt_ref[:, cols] = jnp.transpose(act[cols, 256:])
    gxs_ref[...] = act[:, :256] * dot1(grams, big_ref[:, 1024:1280])


def gram_kernel(at_ref, goh_ref, pre_ref, step_ref, gact_ref, gbend_ref, gstep_ref):
    pre = dot1(goh_ref[...], pre_ref[:, :384])
    logistic = sigmoid(pre)
    gact_ref[...] = pre * logistic
    gbend_ref[...] = logistic * (1.0 + pre * (1.0 - logistic))
    gstep_ref[...] = dot1(goh_ref[...], step_ref[...])


def shifted(symbols, by):
    row = iota((128, 128), 0)
    col = iota((128, 128), 1)
    if by > 0:
        rolled = pltpu.roll(symbols, by, axis=1)
        other = jnp.where(row == 0, 0, pltpu.roll(rolled, 1, axis=0))
        return jnp.where(col < by, other, rolled)
    rolled = pltpu.roll(symbols, 128 + by, axis=1)
    other = jnp.where(row == 127, 0, pltpu.roll(rolled, 127, axis=0))
    return jnp.where(col >= 128 + by, other, rolled)


def read_symbols(
    seq, ids_ref, ca_ref, cb_ref, taps_ref, oh_ref, oht_ref
):
    symbols = []
    for shard in range(16):
        mask = jnp.bitwise_xor(seq, shard)
        near = jnp.bitwise_and(mask, 1) + 2 * jnp.bitwise_and(mask // 8, 1)
        symbols.append(ids_ref[jnp.bitwise_and(mask // 2, 3) * 4 + near])
    symbols = jnp.concatenate(symbols, axis=0) + 1
    taps = [shifted(symbols, 3 - k) if k < 3 else symbols for k in range(4)]
    turned = [complement_padded(shifted(symbols, k - 3) if k < 3 else symbols) for k in range(4)]
    row = iota((128, 128), 0)
    is_before = row < seq * 8
    far = [jnp.where(is_before, a, b) for a, b in zip(taps, turned)]
    ca_ref[...] = encode(far[0], far[1]) + jnp.where(is_before, 0, CODES)
    cb_ref[...] = encode(far[2], far[3])
    for k in range(4):
        taps_ref[k] = taps[k]
        taps_ref[4 + k] = turned[k]
    at = pl.ds(pl.multiple_of(seq * 8, 8), 8)
    own = [taps_ref[k, at, :] for k in range(8)]
    sub = iota((8, 128), 0)
    for j in range(8):
        groups = []
        for k in range(8):
            hit = (own[k][j : j + 1] == sub) & (sub > 0)
            if k % 4 == 0:
                hit = hit | (sub == 6)
            groups.append(jnp.where(hit, 1.0, 0.0))
        rows = jnp.concatenate(groups + groups, axis=0)
        cols = slice(128 * j, 128 * j + 128)
        oht_ref[:, cols] = rows.astype(bf16)
        oh_ref[cols, :] = jnp.transpose(rows).astype(bf16)
    is_own = (row >= seq * 8) & (row < seq * 8 + 8)
    return jnp.where(is_own, 0, far[3])


def triangle(lower, column, row, inner, sign=1.0):
    half = BLOCK // 2
    apart = iota((half, half), 0) - iota((half, half), 1)
    keep = apart >= 0 if lower else apart <= 0
    parts = []
    for i in range(2):
        rows = slice(half * i, half * i + half)
        line = []
        for j in range(2):
            cols = slice(half * j, half * j + half)
            if (i < j) if lower else (i > j):
                line.append(jnp.zeros((half, half), f32))
                continue
            apart = column[rows] - row[:, cols] if sign > 0 else row[:, cols] - column[rows]
            if i == j:
                apart = jnp.where(keep, apart, -1e30)
            value = jnp.exp2(apart)
            line.append(value if inner is None else value * inner[rows, cols])
        parts.append(jnp.concatenate(line, axis=1))
    return jnp.concatenate(parts, axis=0)


def gram_sums(ca_ref, cb_ref, decay_ref, lhs_ref, rhs_ref):
    early_codes = iota((2 * CODES, 128), 0)
    late_codes = iota((CODES, 128), 0)

    def add(k, total):
        for j in range(32):
            if j % 8 == 0:
                at = pl.ds(pl.multiple_of(k * 32 + j, 8), 8)
                early = ca_ref[at, :]
                late = cb_ref[at, :]
                decays = [decay_ref[h, at, :] for h in range(4)]
            cols = slice(128 * j, 128 * j + 128)
            one = slice(j % 8, j % 8 + 1)
            rhs_ref[:, cols] = ones_where(early[one] == early_codes)
            mine = late[one] == late_codes
            for h in range(4):
                lhs_ref[32 * h : 32 * h + 32, cols] = jnp.where(mine, decays[h][one], 0.0).astype(
                    bf16
                )
        return total + dot1(rhs_ref[...], lhs_ref[...], NT)

    return lax.fori_loop(0, 4, add, jnp.zeros((2 * CODES, 128), f32), unroll=2)


def forward_kernel(
    at_ref, ids_ref, pre_ref, step_ref, lx_ref, lrow_ref, wide_ref, gxs_ref, gbt_ref,
    y_first_ref, y_second_ref, states_ref, sums_ref, decay_ref, after_ref, oh_ref, oht_ref,
    ca_ref, cb_ref,
    taps_ref, lhs_ref, rhs_ref, carry_ref,
):
    step_at = pl.program_id(0)
    y_refs = (y_first_ref, y_second_ref)

    @pl.when(step_at == 0)
    def _():
        seq = at_ref[0]
        first = seq * 8
        symbols = read_symbols(seq, ids_ref, ca_ref, cb_ref, taps_ref, oh_ref, oht_ref)
        log_small = lrow_ref[0:8, :] + pltpu.roll(lrow_ref[0:8, :], 64, axis=1)
        row = iota((128, 128), 0)
        col = iota((128, 128), 1)
        upto = ones_where(row <= col)
        every = jnp.ones((128, 128), bf16)
        signs = (jnp.where(col < row, 1.0, 0.0) - jnp.where(col < first, 1.0, 0.0)).astype(bf16)
        is_before = row < first
        logs = [jnp.zeros((128, 128), f32) for _ in range(4)]
        for symbol in range(1, 6):
            here = symbols == symbol
            found = ones_where(here)
            upper = dot1(found, upto) + dot1(signs, dot1(found, every))
            after = jnp.where(is_before, -upper, upper - jnp.where(here, 1.0, 0.0))
            after_ref[symbol - 1] = after
            for h in range(4):
                logs[h] = logs[h] + after * log_small[h : h + 1, 24 + symbol : 25 + symbol]
        for h in range(4):
            decay_ref[h] = jnp.where(symbols > 0, jnp.exp2(logs[h]), 0.0)
        sums = gram_sums(ca_ref, cb_ref, decay_ref, lhs_ref, rhs_ref)
        sums_ref[...] = sums
        gram_xs = gxs_ref[...]
        both = jnp.concatenate([weights * gram_xs for weights in expand_grams(sums)], axis=1)
        states = dot3(gbt_ref[...], both)
        carry_ref[0] = states[:, :256]
        carry_ref[1] = states[:, 256:]

    for branch in range(2):
        block = step_at if branch == 0 else 3 - step_at
        rows = pl.ds(pl.multiple_of(block * BLOCK, BLOCK), BLOCK)
        apart = iota((BLOCK, BLOCK), 0) - iota((BLOCK, BLOCK), 1)
        lower = branch == 0
        behind = apart >= 0 if lower else apart <= 0
        ahead = apart <= 0 if lower else apart >= 0
        pre, step, counts_t, log_wide, log_rows = scan_inputs(
            oh_ref[rows, :], oht_ref[:, rows], pre_ref[:, 512 * branch : 512 * branch + 512],
            step_ref[:, 256 * branch : 256 * branch + 256],
            lx_ref[:, 256 * branch : 256 * branch + 256],
            lrow_ref[8 * branch : 8 * branch + 8, :], ahead, behind,
        )
        act = pre * sigmoid(pre)
        x = act[:, :256]
        b = act[:, 256:384]
        c = act[:, 384:]
        xs = x * step
        state = carry_ref[branch]
        states_ref[branch, 0] = state
        inner = dot3(c, b, NT)
        parts = []
        for h in range(4):
            decays = triangle(
                lower, log_wide[:, h * HDIM : h * HDIM + 1], log_rows[h : h + 1, :], inner
            )
            parts.append(dot1(decays, xs[:, h * HDIM : (h + 1) * HDIM]))
        within = jnp.concatenate(parts, axis=1)
        y = within + dot3(c, state) * jnp.exp2(log_wide)
        y_refs[branch][...] = y + wide_ref[17:18, :] * x
        edge = log_wide[BLOCK - 1 :] if lower else log_wide[:1]
        carry_ref[branch] = jnp.exp2(edge) * state + dot3(b, jnp.exp2(edge - log_wide) * xs, TN)


def own_row(ref, rank):
    return jnp.concatenate([ref[pl.ds(2 * rank, 1), :], ref[pl.ds(2 * rank + 1, 1), :]], axis=1)


def slope_kernel(
    at_ref, y_first_ref, y_second_ref, oh_ref, gate_ref, cot_ref, ow_ref, gain_ref,
    slope_ref, sums_ref,
):
    slope = lax.dot_general(cot_ref[...], ow_ref[...], NT, preferred_element_type=f32)
    slope_ref[...] = slope
    weighted = slope * own_row(gain_ref, at_ref[1])
    gates = dot1(oh_ref[...], gate_ref[...])
    for branch in range(2):
        g = (y_first_ref, y_second_ref)[branch][...] * gates[:, 256 * branch : 256 * branch + 256]
        for kind, product in enumerate((g * g, weighted * g)):
            at = 2 * branch + kind
            product = product[:, :128] + product[:, 128:]
            for j in range(product.shape[0] // 128):
                cols = slice(128 * j, 128 * j + 128)
                total = jnp.sum(jnp.transpose(product[cols]), axis=0, keepdims=True)
                for peer in range(sums_ref.shape[0]):
                    sums_ref[peer, at : at + 1, cols] = total


def mix_kernel(
    at_ref, y_first_ref, y_second_ref, oh_ref, oht_ref, gate_ref, slope_ref, gain_ref, sums_ref,
    mixed_ref, dy_first_ref, dy_second_ref, dgate_ref, dgain_ref,
):
    @pl.when(pl.program_id(0) == 0)
    def _():
        dgate_ref[...] = jnp.zeros_like(dgate_ref)
        dgain_ref[...] = jnp.zeros_like(dgain_ref)

    gain = own_row(gain_ref, at_ref[1])
    slope = slope_ref[...]
    sums = sums_ref[0]
    for peer in range(1, sums_ref.shape[0]):
        sums = sums + sums_ref[peer]
    scale = lax.rsqrt(sums / INNER + EPSILON)
    crossed = jnp.concatenate([sums[1:2], sums[1:2], sums[3:4], sums[3:4]], axis=0)
    weight = scale * scale * scale * crossed / INNER
    kind = iota(sums.shape, 0)
    weight = jnp.concatenate([weight[0:1], weight[0:1], weight[2:3], weight[2:3]], axis=0)
    rows = jnp.where(kind % 2 == 0, scale, weight)
    rows = jnp.concatenate([rows, rows] * 16, axis=0)
    parts = []
    for j in range(rows.shape[1] // 128):
        parts.append(jnp.transpose(rows[:, 128 * j : 128 * j + 128]))
    columns = jnp.concatenate(parts, axis=0)
    sloped = slope * gain
    gates = dot1(oh_ref[...], gate_ref[...])
    total = None
    for branch in range(2):
        gate = gates[:, 256 * branch : 256 * branch + 256]
        y = (y_first_ref, y_second_ref)[branch][...]
        g = y * gate
        scale = columns[:, 2 * branch : 2 * branch + 1]
        weight = columns[:, 2 * branch + 1 : 2 * branch + 2]
        normed = g * scale
        total = normed if total is None else total + normed
        dg = scale * sloped - weight * g
        (dy_first_ref, dy_second_ref)[branch][...] = dg * gate
        lanes = oht_ref[32 * branch : 32 * branch + 32, :]
        dgate_ref[branch] += dot2(lanes, dg * y)
    mixed_ref[...] = (total * gain).astype(bf16)
    dgain_ref[...] += jnp.sum(slope * total, axis=0, keepdims=True)


def backward_scan(
    branch, oh_ref, oht_ref, y_ref, state_ref, later_ref, dy_ref, pre_ref, step_ref, lx_ref,
    lrow_ref, wide_ref,
    tables_ref, steps_ref, logs_ref, skips_ref, carry_ref,
):
    skip = wide_ref[17:18, :]
    apart = iota((BLOCK, BLOCK), 0) - iota((BLOCK, BLOCK), 1)
    ahead = apart <= 0 if branch == 0 else apart >= 0
    behind = apart >= 0 if branch == 0 else apart <= 0
    onehot_t = oht_ref[32 * branch : 32 * branch + 32, :]
    pre, step, counts_t, log_wide, log_rows = scan_inputs(
        oh_ref[...], oht_ref[...], pre_ref[:, 512 * branch : 512 * branch + 512],
        step_ref[:, 256 * branch : 256 * branch + 256],
        lx_ref[:, 256 * branch : 256 * branch + 256],
        lrow_ref[8 * branch : 8 * branch + 8, :], ahead, behind,
    )
    counts_t = counts_t[32 * branch : 32 * branch + 32]
    logistic = sigmoid(pre)
    act = pre * logistic
    bend = logistic * (1.0 + pre * (1.0 - logistic))
    x = act[:, :256]
    b = act[:, 256:384]
    c = act[:, 384:]
    xs = x * step
    dy = dy_ref[...]
    own = y_ref[...] - skip * x
    state = state_ref[0, 0]
    pull = carry_ref[branch]
    xs_low = xs.astype(bf16)
    dy_low = dy.astype(bf16)
    inner = dot3(b, c, NT)
    parts = []
    slopes = jnp.zeros((BLOCK, BLOCK), f32)
    for h in range(4):
        wide = slice(h * HDIM, (h + 1) * HDIM)
        decays = triangle(
            branch == 1, log_wide[:, h * HDIM : h * HDIM + 1], log_rows[h : h + 1, :], None, -1.0
        )
        parts.append(dot1(inner * decays, dy_low[:, wide]))
        slopes = slopes + dot1(xs_low[:, wide], dy_low[:, wide], NT) * decays
    within = jnp.concatenate(parts, axis=1)
    faded = jnp.exp2(log_wide) * dy
    edge = log_wide[BLOCK - 1 :] if branch == 0 else log_wide[:1]
    tail = jnp.exp2(edge - log_wide)
    db = dot1(slopes, c) + dot1(tail * xs, pull, NT)
    dc = dot1(slopes, b, TN) + dot1(faded, state, NT)
    dxs = within + tail * dot1(b, pull)
    dlog = dy_low.astype(f32) * own - xs_low.astype(f32) * dxs
    edge_count = counts_t[:, BLOCK - 1 :] if branch == 0 else counts_t[:, :1]
    ahead = jnp.sum(later_ref[0, 0] * pull, axis=0, keepdims=True)
    logs_ref[...] += dot2(counts_t, dlog) + edge_count * ahead
    carry_ref[branch] = dot1(c, faded, TN) + jnp.exp2(edge) * pull
    dpre = jnp.concatenate([step * dxs + skip * dy, db, dc], axis=1) * bend
    tables_ref[...] += dot2(onehot_t, dpre)
    steps_ref[...] += dot2(onehot_t, x * dxs)
    skips_ref[...] += jnp.sum(dy * x, axis=0, keepdims=True)


def first_backward_kernel(at_ref, *refs):
    blocks = (refs[0:6], refs[6:12])
    tables, (cot_ref, mixed_ref) = refs[12:17], refs[17:19]
    sums, outer_ref = refs[19:24], refs[24]

    @pl.when(pl.program_id(0) == 0)
    def _():
        for ref in refs[19:]:
            ref[...] = jnp.zeros_like(ref)

    for branch in range(2):
        backward_scan(branch, *blocks[branch], *tables, *sums)
    outer_ref[...] += lax.dot_general(cot_ref[...], mixed_ref[...], TN, preferred_element_type=f32)


def second_backward_kernel(at_ref, *refs):
    blocks = (refs[0:6], refs[6:12])
    tables, sums_in = refs[12:17], refs[17:22]
    (
        ca_ref, cb_ref, tokens_ref, goht_ref, sums_ref, decay_ref, after_ref, gact_any, gbend_any,
        gstep_any, tab_ref, weight_any, cot_any, conv_x_ref, conv_bc_ref, dgate_ref, dgain_ref,
        packed_ref,
        mark_ref, found_ref, tables_ref, steps_ref, logs_ref, skips_ref, pull_ref,
        gact_ref, gbend_ref, gstep_ref, gate_w_ref, x_w_ref, bc_w_ref, step_w_ref, cot_ref, sems,
    ) = refs[22:]
    wide_ref = tables[4]
    sums = (tables_ref, steps_ref, logs_ref, skips_ref, pull_ref)
    own_at = pl.multiple_of(at_ref[1] * 256, 256)
    fetched = (
        (gact_any, gact_ref),
        (gbend_any, gbend_ref),
        (gstep_any, gstep_ref),
        (weight_any.at[pl.ds(own_at, 256), :], gate_w_ref),
        (weight_any.at[pl.ds(INNER + own_at, 256), :], x_w_ref),
        (weight_any.at[pl.ds(2 * INNER, 256), :], bc_w_ref),
        (weight_any.at[pl.ds(2 * INNER + 256, HEADS), :], step_w_ref),
        (cot_any, cot_ref),
    )
    copies = [
        pltpu.make_async_copy(source, target, sems.at[k])
        for k, (source, target) in enumerate(fetched)
    ]

    @pl.when(pl.program_id(0) == 0)
    def _():
        for copy in copies:
            copy.start()
        for ref, ref_in in zip(sums, sums_in):
            ref[...] = ref_in[...]

    for branch in range(2):
        backward_scan(branch, *blocks[branch], *tables, *sums)

    @pl.when(pl.program_id(0) == 1)
    def _():
        for copy in copies:
            copy.wait()
        far_and_pack(
            at_ref[1], pull_ref, wide_ref, ca_ref, cb_ref, tokens_ref, goht_ref,
            sums_ref, decay_ref, after_ref, gact_ref, gbend_ref, gstep_ref, tab_ref, gate_w_ref,
            x_w_ref, bc_w_ref, step_w_ref, cot_ref, conv_x_ref, conv_bc_ref, dgate_ref, dgain_ref,
            packed_ref, mark_ref, found_ref, tables_ref, steps_ref, logs_ref, skips_ref,
        )


def far_and_pack(
    rank, pull_ref, wide_ref, ca_ref, cb_ref, tokens_ref, goht_ref,
    sums_ref, decay_ref, after_ref, gact_ref, gbend_ref, gstep_ref, tab_ref, gate_w_ref,
    x_w_ref, bc_w_ref, step_w_ref, cot_ref, conv_x_ref, conv_bc_ref, dgate_ref, dgain_ref,
    packed_ref, mark_ref, found_ref, tables_ref, steps_ref, logs_ref, skips_ref,
):
    gram_x = gact_ref[:, :256]
    gram_b = gact_ref[:, 256:]
    gram_step = gstep_ref[...]
    gram_xs = gram_x * gram_step
    dxs = jnp.zeros((CODES * CODES, 256), f32)
    db = jnp.zeros((CODES * CODES, 128), f32)
    found = []
    expanded = expand_grams(sums_ref[...])
    for branch, weights in enumerate(expanded):
        pull = pull_ref[branch]
        met = dot1(gram_b, pull)
        dxs = dxs + weights * met
        db = db + dot1(weights * gram_xs, pull, NT)
        found.append(gram_xs * met)
    dpre = jnp.concatenate([gram_step * dxs, db], axis=1) * gbend_ref[...]
    gram_t = goht_ref[...]
    tables_ref[:, :384] += dot2(gram_t, dpre)
    steps_ref[...] += dot2(gram_t, gram_x * dxs)
    table = gather_grams(found).astype(bf16)
    early_codes = iota((2 * CODES, 128), 0)
    late_codes = iota((CODES, 128), 0)

    def look_up(shard, unused):
        at = pl.ds(pl.multiple_of(shard * 8, 8), 8)
        early = ca_ref[at, :]
        late = cb_ref[at, :]
        for j in range(8):
            mark_ref[:, 128 * j : 128 * j + 128] = ones_where(early[j : j + 1] == early_codes)
        looked = dot1(table, mark_ref[...], TN)
        for h in range(4):
            rows = []
            for j in range(8):
                part = looked[32 * h : 32 * h + 32, 128 * j : 128 * j + 128]
                mine = late[j : j + 1] == late_codes
                rows.append(jnp.sum(jnp.where(mine, part, 0.0), axis=0, keepdims=True))
            found_ref[h, at, :] = jnp.concatenate(rows, axis=0)
        return unused

    lax.fori_loop(0, 16, look_up, 0, unroll=4)
    lane_head = iota((1, 256), 1) // HDIM
    sub = iota((8, 256), 0)
    far = jnp.zeros((8, 256), f32)
    for h in range(4):
        weighted = found_ref[h] * decay_ref[h]
        for symbol in range(5):
            total = jnp.sum(weighted * after_ref[symbol], axis=0, keepdims=True)
            total = jnp.sum(total, axis=1, keepdims=True)
            far = far + jnp.where((lane_head == h) & (sub == symbol + 1), total, 0.0)

    gate_tab = tab_ref[:, :256]
    x_tab = tab_ref[:, 256:512]
    bc_tab = tab_ref[:, 512:768]
    logistic = sigmoid(gate_tab)
    gate_part = (dgate_ref[0, 24:32, :] + dgate_ref[1, 24:32, :]) * (
        logistic * (1.0 + gate_tab * (1.0 - logistic))
    )
    conv_x = conv_x_ref[...]
    conv_bc = conv_bc_ref[...]
    x_part = jnp.zeros((8, 256), f32)
    bc_part = jnp.zeros((8, 256), f32)
    x_taps = []
    bc_taps = []
    for k in range(KCONV):
        dtap_x = tables_ref[8 * k : 8 * k + 8, :256]
        dtap_bc = tables_ref[8 * k : 8 * k + 8, 256:]
        x_part = x_part + conv_x[k : k + 1] * dtap_x
        bc_part = bc_part + conv_bc[k : k + 1] * dtap_bc
        x_taps.append(jnp.sum(dtap_x * x_tab, axis=0, keepdims=True))
        bc_taps.append(jnp.sum(dtap_bc * bc_tab, axis=0, keepdims=True))
    bias = tables_ref[6:7, :]
    same = ones_where(iota((256, 256), 0) // HDIM == iota((256, 256), 1) // HDIM)
    log_part = dot_exact(logs_ref[24:32, :], same) + far
    step_part = dot_exact(steps_ref[24:32, :], same) - wide_ref[16:17, :] * log_part
    step_part = step_part * wide_ref[0:8, :]
    rate_part = jnp.sum(log_part * wide_ref[8:16, :], axis=0, keepdims=True)
    skip_part = dot_exact(jnp.broadcast_to(skips_ref[...], (8, 256)), same)
    valid = (sub >= 1) & (sub <= 5)
    step_part = jnp.where(valid, step_part, 0.0)
    step_rows = jnp.where(
        sub == 0,
        jnp.sum(step_part, axis=0, keepdims=True),
        jnp.where(sub == 6, rate_part, jnp.where(sub == 7, skip_part, step_part)),
    )
    spread = iota((256, 128), 1)
    narrow = ones_where(
        (iota((256, 128), 0) % HDIM == 0)
        & (rank * 4 + iota((256, 128), 0) // HDIM == spread)
    )
    step_heads = dot_exact(step_rows, narrow)

    def against(part, weights):
        first_piece = part.astype(bf16)
        rest = part - first_piece.astype(f32)
        second_piece = rest.astype(bf16)
        third_piece = rest - second_piece.astype(f32)
        return dot1(first_piece, weights) + (
            dot1(second_piece, weights) + dot1(third_piece, weights)
        )

    embed_part = (
        dot1(tokens_ref[...], cot_ref[...])[24:32]
        + against(jnp.where(valid, gate_part, 0.0), gate_w_ref[...])
        + against(jnp.where(valid, x_part, 0.0), x_w_ref[...])
        + against(jnp.where(valid, bc_part, 0.0), bc_w_ref[...])
        + against(jnp.where(valid[:, :HEADS], step_heads[:, :HEADS], 0.0), step_w_ref[...])
    )

    def rows_of(part, zero, six, seven):
        return jnp.where(
            sub == 0, zero, jnp.where(sub == 6, six, jnp.where(sub == 7, seven, part))
        )

    gate_rows = rows_of(gate_part, x_taps[0], x_taps[1], x_taps[2])
    x_rows = rows_of(x_part, x_taps[3], bias[:, :256], dgain_ref[...])
    bc_rows = rows_of(bc_part, bc_taps[0], bc_taps[1], bc_taps[2])
    embed_first = rows_of(embed_part[:, :256], bc_taps[3], bias[:, 256:], 0.0)
    for half in range(2):
        cols = slice(128 * half, 128 * half + 128)
        packed_ref[half] = gate_rows[:, cols]
        packed_ref[2 + half] = x_rows[:, cols]
        packed_ref[4 + half] = bc_rows[:, cols]
        packed_ref[7 + half] = embed_first[:, cols]
    packed_ref[6] = step_heads
    for piece in range(2, 8):
        packed_ref[7 + piece] = embed_part[:, 128 * piece : 128 * piece + 128]
    packed_ref[15] = jnp.zeros((8, 128), f32)


def out_kernel(mixed_ref, ow_ref, token_ref, embed_ref, out_ref):
    total = dot1(token_ref[...], embed_ref[...])
    for peer in range(mixed_ref.shape[0]):
        total = total + dot1(mixed_ref[peer], ow_ref[256 * peer : 256 * peer + 256, :])
    out_ref[...] = total.astype(bf16)


def sum_kernel(pieces_ref, spread_ref):
    total = pieces_ref[0]
    for k in range(1, pieces_ref.shape[0]):
        total = total + pieces_ref[k]
    spread_ref[...] = jnp.broadcast_to(total[None], spread_ref.shape)


def final_kernel(
    whole_ref, embed_ref,
    w_in_ref, embedding_ref, conv_ref, bias_ref, dt_ref, rate_ref, skip_ref, gain_ref,
):
    def summed(piece):
        total = whole_ref[8 * piece]
        for k in range(1, 8):
            total = total + whole_ref[8 * piece + k]
        return total

    embed = embed_ref[...]

    def outer(table, first):
        one = table.astype(bf16)
        rest = table - one.astype(f32)
        two = rest.astype(bf16)
        three = rest - two.astype(f32)
        pieces = jnp.concatenate([one.astype(f32), two.astype(f32), three], axis=0)
        value = dot1(embed, pieces)
        w_in_ref[:, first : first + table.shape[1]] = value

    for rank in range(8):
        for half in range(2):
            gate = whole_ref[8 * half + rank]
            x = whole_ref[8 * (2 + half) + rank]
            at = 256 * rank + 128 * half
            cols = slice(at, at + 128)
            outer(gate, at)
            outer(x, INNER + at)
            conv_ref[0:1, cols] = gate[0:1]
            conv_ref[1:2, cols] = gate[6:7]
            conv_ref[2:3, cols] = gate[7:8]
            conv_ref[3:4, cols] = x[0:1]
            bias_ref[2 * rank + half : 2 * rank + half + 1, :] = x[6:7]
            gain_ref[2 * rank + half : 2 * rank + half + 1, :] = x[7:8]
    for half in range(2):
        bc = summed(4 + half)
        at = INNER + 128 * half
        cols = slice(at, at + 128)
        outer(bc, INNER + at)
        rest = summed(7 + half)
        conv_ref[0:1, cols] = bc[0:1]
        conv_ref[1:2, cols] = bc[6:7]
        conv_ref[2:3, cols] = bc[7:8]
        conv_ref[3:4, cols] = rest[0:1]
        bias_ref[16 + half : 17 + half, :] = rest[6:7]
    steps = summed(6)[:, :HEADS]
    outer(steps, 2 * INNER + 2 * STATE)
    dt_ref[...] = steps[0:1]
    rate_ref[...] = steps[6:7]
    skip_ref[...] = steps[7:8]
    for piece in range(8):
        embedding_ref[:, 128 * piece : 128 * piece + 128] = summed(7 + piece)[1:6]


VMEM = pl.BlockSpec(memory_space=pltpu.VMEM)
VMEM_LIMIT = 62 * 1024 * 1024
TOKEN_STEPS = 2
ANY = pl.BlockSpec(memory_space=pl.ANY)


def whole(array):
    zeros = (0,) * array.ndim
    return pl.BlockSpec(array.shape, lambda i, at: zeros)


def own(shape, index):
    return pl.BlockSpec(shape, index)


def call(kernel, at, operands, outs, scratch=(), cost=5e9, steps=1):
    arrays = [item[0] if isinstance(item, tuple) else item for item in operands]
    specs = [
        (own(*item[1:]) if len(item) > 2 else ANY) if isinstance(item, tuple) else whole(item)
        for item in operands
    ]
    shapes = [jax.ShapeDtypeStruct(item[0], item[1]) for item in outs]
    out_specs = [
        own(item[2], item[3]) if len(item) > 2 else whole(shape)
        for item, shape in zip(outs, shapes)
    ]
    return pl.pallas_call(
        kernel,
        out_shape=shapes,
        grid_spec=pltpu.PrefetchScalarGridSpec(
            num_scalar_prefetch=1,
            grid=(steps,),
            in_specs=specs,
            out_specs=out_specs,
            scratch_shapes=list(scratch),
        ),
        compiler_params=pltpu.CompilerParams(vmem_limit_bytes=VMEM_LIMIT),
        cost_estimate=pl.CostEstimate(flops=int(cost), bytes_accessed=4000000, transcendentals=0),
    )(at, *arrays)


def call_plain(kernel, operands, outs, cost=1e9):
    return pl.pallas_call(
        kernel,
        out_shape=[jax.ShapeDtypeStruct(shape, kind) for shape, kind in outs],
        in_specs=[VMEM] * len(operands),
        out_specs=[VMEM] * len(outs),
        compiler_params=pltpu.CompilerParams(vmem_limit_bytes=VMEM_LIMIT),
        cost_estimate=pl.CostEstimate(flops=int(cost), bytes_accessed=1000000, transcendentals=0),
    )(*operands)


def gather(shard, axis):
    devices = lax.axis_size(axis)
    spread = jnp.broadcast_to(shard[None], (devices,) + shard.shape)
    return lax.all_to_all(spread, axis, split_axis=0, concat_axis=0, tiled=True)


def gather_by_flips(array, axis, flips):
    pairs = [[(i, i ^ flip) for i in range(lax.axis_size(axis))] for flip in flips]
    return jnp.concatenate([array] + [lax.ppermute(array, axis, pair) for pair in pairs], axis=0)


def exchange(array, axis):
    return lax.all_to_all(array, axis, split_axis=0, concat_axis=0, tiled=True)


def body(
    base_ids, embedding, in_weight, conv_weight, conv_bias, dt_bias, a_log, skip_weight, norm_gain,
    out_weight, cotangent,
):
    groups = lax.axis_size("head")
    shards = lax.axis_size("seq")
    width = HEADS // groups * HDIM
    head_rank = lax.axis_index("head")
    seq_rank = lax.axis_index("seq")
    length = base_ids.shape[0]
    token_rows = length // groups
    at = jnp.stack([seq_rank, head_rank]).astype(jnp.int32)

    near = gather_by_flips(base_ids.reshape(1, 8, 128), "seq", (1, 8, 9))
    near, in_weight = lax.optimization_barrier((near, in_weight))
    ids = gather_by_flips(near, "seq", (2, 4, 6))
    cot_all = gather(cotangent, "head").reshape(length, D)
    weight_t = in_weight.T
    gain_rows = norm_gain.reshape(INNER // 128, 128)
    grams = _gram_onehot()
    gram_rows = jnp.asarray(grams, bf16)
    gram_cols = jnp.asarray(np.ascontiguousarray(grams[:, :32].T), bf16)
    weights = [
        (weight_t, (width, D), lambda i, at: (at[1], 0)),
        (weight_t, (width, D), lambda i, at: (INNER // width + at[1], 0)),
        (weight_t, (256, D), lambda i, at: (16, 0)),
        (weight_t, (128, D), lambda i, at: (34, 0)),
    ]
    convs = [
        (conv_weight, (KCONV, width), lambda i, at: (0, at[1])),
        (conv_weight, (KCONV, width), lambda i, at: (0, INNER // width)),
    ]
    count = CODES * CODES
    big, logs, log_rows, tab, wide, gxs, gbt = call(
        prep_kernel,
        at,
        [
            embedding,
            *weights,
            *convs,
            conv_bias.reshape(conv_bias.shape[0] // 128, 128),
            dt_bias[None, :],
            a_log[None, :],
            skip_weight[None, :],
            gram_rows,
        ],
        [
            ((128, 2048), bf16),
            ((128, 512), bf16),
            ((16, 128), f32),
            ((8, 768), f32),
            ((24, width), f32),
            ((count, width), f32),
            ((STATE, count), f32),
        ],
        cost=6e9,
    )

    blocks = length // BLOCK

    tables = [
        (big, (128, 1024), lambda k, at: (0, 0)),
        (big, (128, 512), lambda k, at: (0, 2)),
        logs,
        log_rows,
        wide,
    ]

    def rows_at(array, rows, index):
        return (array, (rows, array.shape[1]), lambda k, at: (index(k), 0))

    y_first, y_second, states, sums, decays, after, onehot, onehot_t, early, late = call(
        forward_kernel,
        at,
        [ids, *tables, gxs, gbt],
        [
            ((length, width), f32, (BLOCK, width), lambda k, at: (k, 0)),
            ((length, width), f32, (BLOCK, width), lambda k, at: (blocks - 1 - k, 0)),
            (
                (2, blocks, STATE, width), f32,
                (2, 1, STATE, width), lambda k, at: (0, k, 0, 0),
            ),
            ((2 * CODES, 128), f32),
            ((4, 128, 128), f32),
            ((5, 128, 128), f32),
            ((length, 128), bf16),
            ((128, length), bf16),
            ((128, 128), jnp.int32),
            ((128, 128), jnp.int32),
        ],
        [
            pltpu.VMEM((8, 128, 128), jnp.int32),
            pltpu.VMEM((128, 4096), bf16),
            pltpu.VMEM((2 * CODES, 4096), bf16),
            pltpu.VMEM((2, STATE, width), f32),
        ],
        cost=1.5e10,
        steps=blocks,
    )

    chunk = length // TOKEN_STEPS
    gates = (big, (128, 512), lambda k, at: (0, 3))
    y_rows = [rows_at(y, chunk, lambda k: k) for y in (y_first, y_second)]
    hot_rows = rows_at(onehot, chunk, lambda k: k)
    slope, row_sums = call(
        slope_kernel,
        at,
        [
            *y_rows,
            hot_rows,
            gates,
            rows_at(cot_all, chunk, lambda k: k),
            (out_weight, (width, D), lambda k, at: (at[1], 0)),
            gain_rows,
        ],
        [
            ((length, width), f32, (chunk, width), lambda k, at: (k, 0)),
            ((groups, 4, length), f32, (groups, 4, chunk), lambda k, at: (0, 0, k)),
        ],
        cost=4e9,
        steps=TOKEN_STEPS,
    )
    row_sums, big, ids_later, embed_later = lax.optimization_barrier(
        (row_sums, big, base_ids, embedding)
    )
    gact, gbend, gstep = call(
        gram_kernel,
        at,
        [
            gram_rows,
            (big, (128, 512), lambda k, at: (0, 0)),
            (big, (128, 256), lambda k, at: (0, 4)),
        ],
        [((count, 384), f32), ((count, 384), f32), ((count, width), f32)],
        cost=2e9,
    )
    row_sums = exchange(row_sums, "head")
    mixed, dy_first, dy_second, dgate, dgain = call(
        mix_kernel,
        at,
        [
            *y_rows,
            hot_rows,
            (onehot_t, (128, chunk), lambda k, at: (0, k)),
            gates,
            rows_at(slope, chunk, lambda k: k),
            gain_rows,
            (row_sums, (groups, 4, chunk), lambda k, at: (0, 0, k)),
        ],
        [
            ((length, width), bf16, (chunk, width), lambda k, at: (k, 0)),
            ((length, width), f32, (chunk, width), lambda k, at: (k, 0)),
            ((length, width), f32, (chunk, width), lambda k, at: (k, 0)),
            ((2, 32, width), f32),
            ((1, width), f32),
        ],
        cost=4e9,
        steps=TOKEN_STEPS,
    )

    mixed_all = exchange(mixed.reshape(groups, token_rows, width), "head")

    def scan_operands(first_step):
        operands = []
        for branch, y, dy in ((0, y_first, dy_first), (1, y_second, dy_second)):

            def nth(k):
                return first_step + k

            def block(k, branch=branch):
                return blocks - 1 - nth(k) if branch == 0 else nth(k)

            def state(k, at, branch=branch):
                return (branch, blocks - 1 - nth(k), 0, 0)

            def later(k, at, branch=branch):
                return (branch, jnp.minimum(blocks - nth(k), blocks - 1), 0, 0)

            one = (1, 1, STATE, width)
            operands += [
                rows_at(onehot, BLOCK, block),
                (onehot_t, (128, BLOCK), lambda k, at, block=block: (0, block(k))),
                rows_at(y, BLOCK, block),
                (states, one, state),
                (states, one, later),
                rows_at(dy, BLOCK, block),
            ]
        return operands + tables

    accumulators = [
        ((32, 512), f32),
        ((32, width), f32),
        ((32, width), f32),
        ((1, width), f32),
        ((2, STATE, width), f32),
    ]
    *grads, partial = call(
        first_backward_kernel,
        at,
        scan_operands(0)
        + [rows_at(cot_all, length // 2, lambda k: k), rows_at(mixed, length // 2, lambda k: k)],
        accumulators + [((D, width), f32)],
        cost=1.5e10,
        steps=blocks // 2,
    )
    mixed_all, partial, grads = lax.optimization_barrier((mixed_all, partial, grads))
    partial = exchange(partial.reshape(shards, D // shards, width), "seq")
    (packed,) = call(
        second_backward_kernel,
        at,
        scan_operands(blocks // 2)
        + [
            *grads,
            early,
            late,
            (onehot_t, (32, token_rows), lambda k, at: (0, at[1])),
            gram_cols,
            sums,
            decays,
            after,
            (gact,),
            (gbend,),
            (gstep,),
            tab,
            (weight_t,),
            (cotangent,),
            *convs,
            dgate,
            dgain,
        ],
        [((shards, 8, 128), f32)],
        [
            pltpu.VMEM((2 * CODES, 1024), bf16),
            pltpu.VMEM((4, 128, 128), f32),
            *[pltpu.VMEM(shape, kind) for shape, kind in accumulators],
            pltpu.VMEM((count, 384), f32),
            pltpu.VMEM((count, 384), f32),
            pltpu.VMEM((count, width), f32),
            pltpu.VMEM((width, D), bf16),
            pltpu.VMEM((width, D), bf16),
            pltpu.VMEM((256, D), bf16),
            pltpu.VMEM((HEADS, D), bf16),
            pltpu.VMEM((token_rows, D), bf16),
            pltpu.SemaphoreType.DMA((8,)),
        ],
        cost=2e10,
        steps=blocks // 2,
    )
    packed, partial = lax.optimization_barrier((packed, partial))

    grad_w_out = jnp.sum(partial, axis=0).T
    token_ids = lax.dynamic_slice_in_dim(ids_later, head_rank * token_rows, token_rows, 0)
    alphabet = jnp.arange(5, dtype=jnp.int32)
    token_hot = (token_ids[:, None] == alphabet[None, :]).astype(bf16)
    (layer_out,) = call_plain(
        out_kernel,
        [mixed_all, out_weight, token_hot, embedding],
        [((token_rows, D), bf16)],
        4e9,
    )

    pieces = exchange(packed, "seq")
    row_count = D // shards
    columns = lax.dynamic_slice_in_dim(embed_later, seq_rank * row_count, row_count, 1)
    columns = jnp.pad(columns, ((1, 2), (0, 0)))
    columns = jnp.concatenate([columns] * 3, axis=0).T
    pieces, layer_out, grad_w_out, columns = lax.optimization_barrier(
        (pieces, layer_out, grad_w_out, columns)
    )
    (spread,) = call_plain(sum_kernel, [pieces], [((shards * groups, 8, 128), f32)], 1e8)
    everything = exchange(spread, ("seq", "head"))
    w_in, embed, conv, bias, dt, rate, skip, gain = call_plain(
        final_kernel,
        [everything, columns],
        [
            ((row_count, in_weight.shape[1]), f32),
            (embedding.shape, f32),
            (conv_weight.shape, f32),
            ((conv_bias.shape[0] // 128, 128), f32),
            ((1, HEADS), f32),
            ((1, HEADS), f32),
            ((1, HEADS), f32),
            ((INNER // 128, 128), f32),
        ],
    )
    return (
        layer_out, w_in, grad_w_out, embed, conv, bias.reshape(-1), dt[0], rate[0], skip[0],
        gain.reshape(-1),
    )


def solution(mesh):
    return jax.shard_map(
        body,
        mesh=mesh,
        in_specs=(P("seq"), P(), P(), P(), P(), P(), P(), P(), P(), P(), P(("seq", "head"), None)),
        out_specs=(
            P(("seq", "head"), None),
            P("seq", None),
            P("head", "seq"),
            P(),
            P(),
            P(),
            P(),
            P(),
            P(),
            P(),
        ),
        check_vma=False,
    )
```

```python
import jax
import jax.numpy as jnp
import numpy as np
from jax import lax
from jax.experimental import pallas as pl
from jax.experimental.pallas import tpu as pltpu
from jax.sharding import PartitionSpec as P

D = 1024
HEADS = 32
HDIM = 64
STATE = 128
BLOCK = 256
KCONV = 4
INNER = 2048
EPSILON = 1e-05
LOG2E = 1.4426950408889634

f32 = jnp.float32
bf16 = jnp.bfloat16
NN = (((1,), (0,)), ((), ()))
NT = (((1,), (1,)), ((), ()))
TN = (((0,), (0,)), ((), ()))

CODES = 32


def _decode_codes():
    first = np.zeros((CODES,), np.int32)
    second = np.zeros((CODES,), np.int32)
    for code in range(25):
        first[code], second[code] = code // 5 + 1, code % 5 + 1
    for code in range(25, 30):
        second[code] = code - 24
    return first, second


def _gram_onehot():
    first, second = _decode_codes()
    early, late = np.divmod(np.arange(CODES * CODES), CODES)
    symbols = (first[early], second[early], first[late], second[late])
    rows = np.zeros((CODES * CODES, 128), np.float32)
    for tap, symbol in enumerate(symbols):
        valid = symbol > 0
        rows[np.arange(CODES * CODES)[valid], (8 * tap + symbol)[valid]] = 1.0
    rows[:, 6] = 1.0
    rows[:, 64:96] = rows[:, :32]
    return rows


def encode(earlier, later):
    return jnp.where(
        earlier > 0, (earlier - 1) * 5 + later - 1, jnp.where(later > 0, 24 + later, 30)
    )


def complement_padded(symbols):
    return jnp.where((symbols >= 1) & (symbols <= 4), 5 - symbols, symbols)


def halves(values):
    high = values.astype(bf16)
    return high, (values - high.astype(f32)).astype(bf16)


def dot1(a, b, dims=NN):
    return lax.dot_general(a.astype(bf16), b.astype(bf16), dims, preferred_element_type=f32)


def doubled(values, axis):
    return jnp.concatenate([values, values], axis=axis)


def dot2(a, b, dims=NN):
    high, low = halves(b)
    a = a.astype(bf16)
    if a.shape[dims[0][0][0]] <= 128:
        pieces = jnp.concatenate([high, low], axis=dims[0][1][0])
        return dot1(doubled(a, dims[0][0][0]), pieces, dims)
    return dot1(a, high, dims) + dot1(a, low, dims)


def dot2l(a, b, dims=NN):
    high, low = halves(a)
    b = b.astype(bf16)
    if b.shape[dims[0][1][0]] <= 128:
        pieces = jnp.concatenate([high, low], axis=dims[0][0][0])
        return dot1(pieces, doubled(b, dims[0][1][0]), dims)
    return dot1(high, b, dims) + dot1(low, b, dims)


def dot3(a, b, dims=NN):
    a_high, a_low = halves(a)
    b_high, b_low = halves(b)
    if a.shape[dims[0][0][0]] <= 128:
        pieces = jnp.concatenate([a_high, a_low], axis=dims[0][0][0])
        return dot1(pieces, doubled(b_high, dims[0][1][0]), dims) + dot1(a_high, b_low, dims)
    return dot1(a_high, b_high, dims) + (dot1(a_high, b_low, dims) + dot1(a_low, b_high, dims))


def dot_exact(a, b, dims=NN):
    first = a.astype(bf16)
    rest = a - first.astype(f32)
    second = rest.astype(bf16)
    third = rest - second.astype(f32)
    b = b.astype(bf16)
    return dot1(first, b, dims) + (dot1(second, b, dims) + dot1(third, b, dims))


def iota(shape, axis):
    return lax.broadcasted_iota(jnp.int32, shape, axis)


def ones_where(condition):
    return jnp.where(condition, 1.0, 0.0).astype(bf16)


def expand_grams(sums):
    grams = CODES * CODES
    early = ones_where(iota((grams, CODES), 0) // CODES == iota((grams, CODES), 1))
    both = dot2(early, jnp.concatenate([sums[:CODES], sums[CODES:]], axis=1))
    mine = iota((grams, 128), 0) % CODES == iota((grams, 128), 1) % CODES
    widen = ones_where(iota((128, 256), 0) // CODES == iota((128, 256), 1) // HDIM)
    return [
        dot2l(jnp.where(mine, both[:, 128 * k : 128 * k + 128], 0.0), widen) for k in range(2)
    ]


def gather_grams(values):
    grams = CODES * CODES
    narrow = ones_where(iota((256, 128), 0) // HDIM == iota((256, 128), 1) // CODES)
    mine = iota((grams, 128), 0) % CODES == iota((grams, 128), 1) % CODES
    spread = [jnp.where(mine, dot1(value, narrow), 0.0) for value in values]
    early = ones_where(iota((CODES, grams), 1) // CODES == iota((CODES, grams), 0))
    both = dot1(early, jnp.concatenate(spread, axis=1))
    return jnp.concatenate([both[:, :128], both[:, 128:]], axis=0)


def sigmoid(values):
    return 0.5 * jnp.tanh(0.5 * values) + 0.5


def scan_inputs(onehot, onehot_t, pre_tab, step_tab, log_tab, log_rows, ahead, behind):
    pre = dot1(onehot, pre_tab)
    step = dot1(onehot, step_tab)
    counts = dot1(ones_where(behind), onehot).astype(bf16)
    counts_t = dot1(onehot_t, ones_where(ahead))
    log_wide = dot1(counts, log_tab)
    log_rows = dot1(log_rows.astype(bf16), counts_t)
    return pre, step, counts_t, log_wide, log_rows


def prep_kernel(
    at_ref, embed_ref, gate_w_ref, x_w_ref, bc_w_ref, step_w_ref, conv_x_ref, conv_bc_ref,
    bias_ref, dt_ref, rate_ref, skip_ref, goh_ref,
    big_ref, logs_ref, lrow_ref, tab_ref, wide_ref, gxs_ref, gbt_ref,
):
    rank = at_ref[1]
    place = ones_where(iota((8, 5), 0) == iota((8, 5), 1) + 1)
    embed = dot1(place, embed_ref[...]).astype(bf16)
    gate_w = gate_w_ref[...]
    x_w = x_w_ref[...]
    bc_w = bc_w_ref[...]
    step_w = step_w_ref[...]
    step_w = jnp.where(iota((128, D), 0) < HEADS, step_w.astype(f32), 0.0).astype(bf16)

    def heads_row(ref):
        return jnp.concatenate([ref[...], jnp.zeros((1, 128 - HEADS), f32)], axis=1)

    bias_x = jnp.concatenate(
        [bias_ref[pl.ds(2 * rank, 1), :], bias_ref[pl.ds(2 * rank + 1, 1), :]], axis=1
    )
    bias_bc = jnp.concatenate([bias_ref[16:17, :], bias_ref[17:18, :]], axis=1)
    gate = dot1(embed, gate_w, NT)
    x = dot1(embed, x_w, NT)
    bc = dot1(embed, bc_w, NT)
    tab_ref[:, :256] = gate
    tab_ref[:, 256:512] = x
    tab_ref[:, 512:768] = bc
    row = iota((8, 128), 0)
    lane = iota((8, 128), 1)
    valid = (row >= 1) & (row <= 5)
    pre = dot1(embed, step_w, NT) + heads_row(dt_ref)
    valid = valid & (lane < HEADS)
    step = jnp.maximum(pre, 0.0) + jnp.log1p(jnp.exp(-jnp.abs(pre)))
    rate = jnp.exp(heads_row(rate_ref))
    logs = jnp.where(valid, -(rate * step), 0.0)
    step = jnp.where(valid, step, 0.0)
    bent = jnp.where(valid, sigmoid(pre), 0.0)
    widen = ones_where(iota((128, 256), 0) == rank * 4 + iota((128, 256), 1) // HDIM)
    step_wide = dot_exact(step, widen)
    logs_wide = dot_exact(logs, widen)
    logs = logs * LOG2E
    wide_ref[0:8, :] = dot_exact(bent, widen)
    wide_ref[8:16, :] = logs_wide
    others = jnp.where(row == 0, rate, jnp.where(row == 1, heads_row(skip_ref), 0.0))
    others = jnp.where(lane < HEADS, others, 0.0)
    wide_ref[16:24, :] = dot_exact(others, widen)
    one_row = iota((8, 256), 0) == 6
    conv_x = conv_x_ref[...]
    conv_bc = conv_bc_ref[...]
    taps = []
    for k in range(4):
        tap_x = conv_x[k : k + 1] * x
        tap_bc = conv_bc[k : k + 1] * bc
        if k == 0:
            tap_x = jnp.where(one_row, bias_x, tap_x)
            tap_bc = jnp.where(one_row, bias_bc, tap_bc)
        taps.append(jnp.concatenate([tap_x, tap_bc], axis=1))
    silu_gate = gate * sigmoid(gate)

    def put(ref, start, pieces):
        nothing = jnp.zeros(pieces[0][1].shape, f32)
        pieces = dict(pieces)
        table = jnp.concatenate([pieces.get(k, nothing) for k in range(8)], axis=0)
        high, low = halves(table)
        ref[0:64, start : start + table.shape[1]] = high
        ref[64:128, start : start + table.shape[1]] = low
        return high, low

    first_high, first_low = put(big_ref, 0, list(enumerate(taps)))
    put(big_ref, 512, [(4 + k, tap) for k, tap in enumerate(taps)])
    step_high, step_low = put(big_ref, 1024, [(3, step_wide)])
    put(big_ref, 1280, [(7, step_wide)])
    put(big_ref, 1536, [(3, silu_gate)])
    put(big_ref, 1792, [(7, silu_gate)])
    put(logs_ref, 0, [(3, logs_wide * LOG2E)])
    put(logs_ref, 256, [(7, logs_wide * LOG2E)])
    pick = ones_where((iota((8, 128), 1) == rank * 4 + row) & (row < 4))
    nothing = jnp.zeros((8, 128), f32)
    for branch in range(2):
        spot = 3 + 4 * branch
        rows = jnp.concatenate([logs if k % 8 == spot else nothing for k in range(16)], axis=0)
        first = rows.astype(bf16)
        rest = rows - first.astype(f32)
        second = rest.astype(bf16)
        third = rest - second.astype(f32)
        values = dot1(pick, first, NT) + (dot1(pick, second, NT) + dot1(pick, third, NT))
        high = values.astype(bf16).astype(f32)
        lrow_ref[8 * branch : 8 * branch + 8, :] = jnp.where(lane < 64, high, values - high)
    grams = goh_ref[...]
    pre = dot1(grams, big_ref[:, :384])
    act = pre * sigmoid(pre)
    for j in range(8):
        cols = slice(128 * j, 128 * j + 128)
        gbt_ref[:, cols] = jnp.transpose(act[cols, 256:])
    gxs_ref[...] = act[:, :256] * dot1(grams, big_ref[:, 1024:1280])


def gram_kernel(at_ref, goh_ref, pre_ref, step_ref, gact_ref, gbend_ref, gstep_ref):
    pre = dot1(goh_ref[...], pre_ref[:, :384])
    logistic = sigmoid(pre)
    gact_ref[...] = pre * logistic
    gbend_ref[...] = logistic * (1.0 + pre * (1.0 - logistic))
    gstep_ref[...] = dot1(goh_ref[...], step_ref[...])


def shifted(symbols, by):
    row = iota((128, 128), 0)
    col = iota((128, 128), 1)
    if by > 0:
        rolled = pltpu.roll(symbols, by, axis=1)
        other = jnp.where(row == 0, 0, pltpu.roll(rolled, 1, axis=0))
        return jnp.where(col < by, other, rolled)
    rolled = pltpu.roll(symbols, 128 + by, axis=1)
    other = jnp.where(row == 127, 0, pltpu.roll(rolled, 127, axis=0))
    return jnp.where(col >= 128 + by, other, rolled)


def read_symbols(
    seq, ids_ref, ca_ref, cb_ref, taps_ref, oh_ref, oht_ref
):
    symbols = []
    for shard in range(16):
        mask = jnp.bitwise_xor(seq, shard)
        near = jnp.bitwise_and(mask, 1) + 2 * jnp.bitwise_and(mask // 8, 1)
        symbols.append(ids_ref[jnp.bitwise_and(mask // 2, 3) * 4 + near])
    symbols = jnp.concatenate(symbols, axis=0) + 1
    taps = [shifted(symbols, 3 - k) if k < 3 else symbols for k in range(4)]
    turned = [complement_padded(shifted(symbols, k - 3) if k < 3 else symbols) for k in range(4)]
    row = iota((128, 128), 0)
    is_before = row < seq * 8
    far = [jnp.where(is_before, a, b) for a, b in zip(taps, turned)]
    ca_ref[...] = encode(far[0], far[1]) + jnp.where(is_before, 0, CODES)
    cb_ref[...] = encode(far[2], far[3])
    for k in range(4):
        taps_ref[k] = taps[k]
        taps_ref[4 + k] = turned[k]
    at = pl.ds(pl.multiple_of(seq * 8, 8), 8)
    own = [taps_ref[k, at, :] for k in range(8)]
    sub = iota((8, 128), 0)
    for j in range(8):
        groups = []
        for k in range(8):
            hit = (own[k][j : j + 1] == sub) & (sub > 0)
            if k % 4 == 0:
                hit = hit | (sub == 6)
            groups.append(jnp.where(hit, 1.0, 0.0))
        rows = jnp.concatenate(groups + groups, axis=0)
        cols = slice(128 * j, 128 * j + 128)
        oht_ref[:, cols] = rows.astype(bf16)
        oh_ref[cols, :] = jnp.transpose(rows).astype(bf16)
    is_own = (row >= seq * 8) & (row < seq * 8 + 8)
    return jnp.where(is_own, 0, far[3])


def triangle(lower, column, row, inner, sign=1.0):
    half = BLOCK // 2
    apart = iota((half, half), 0) - iota((half, half), 1)
    keep = apart >= 0 if lower else apart <= 0
    parts = []
    for i in range(2):
        rows = slice(half * i, half * i + half)
        line = []
        for j in range(2):
            cols = slice(half * j, half * j + half)
            if (i < j) if lower else (i > j):
                line.append(jnp.zeros((half, half), f32))
                continue
            apart = column[rows] - row[:, cols] if sign > 0 else row[:, cols] - column[rows]
            if i == j:
                apart = jnp.where(keep, apart, -1e30)
            value = jnp.exp2(apart)
            line.append(value if inner is None else value * inner[rows, cols])
        parts.append(jnp.concatenate(line, axis=1))
    return jnp.concatenate(parts, axis=0)


def gram_sums(ca_ref, cb_ref, decay_ref, lhs_ref, rhs_ref):
    early_codes = iota((2 * CODES, 128), 0)
    late_codes = iota((CODES, 128), 0)

    def add(k, total):
        for j in range(32):
            if j % 8 == 0:
                at = pl.ds(pl.multiple_of(k * 32 + j, 8), 8)
                early = ca_ref[at, :]
                late = cb_ref[at, :]
                decays = [decay_ref[h, at, :] for h in range(4)]
            cols = slice(128 * j, 128 * j + 128)
            one = slice(j % 8, j % 8 + 1)
            rhs_ref[:, cols] = ones_where(early[one] == early_codes)
            mine = late[one] == late_codes
            for h in range(4):
                lhs_ref[32 * h : 32 * h + 32, cols] = jnp.where(mine, decays[h][one], 0.0).astype(
                    bf16
                )
        return total + dot1(rhs_ref[...], lhs_ref[...], NT)

    return lax.fori_loop(0, 4, add, jnp.zeros((2 * CODES, 128), f32), unroll=2)


def forward_kernel(
    at_ref, ids_ref, pre_ref, step_ref, lx_ref, lrow_ref, wide_ref, gxs_ref, gbt_ref,
    y_first_ref, y_second_ref, states_ref, sums_ref, decay_ref, after_ref, oh_ref, oht_ref,
    ca_ref, cb_ref,
    taps_ref, lhs_ref, rhs_ref, carry_ref,
):
    step_at = pl.program_id(0)
    y_refs = (y_first_ref, y_second_ref)

    @pl.when(step_at == 0)
    def _():
        seq = at_ref[0]
        first = seq * 8
        symbols = read_symbols(seq, ids_ref, ca_ref, cb_ref, taps_ref, oh_ref, oht_ref)
        log_small = lrow_ref[0:8, :] + pltpu.roll(lrow_ref[0:8, :], 64, axis=1)
        row = iota((128, 128), 0)
        col = iota((128, 128), 1)
        upto = ones_where(row <= col)
        every = jnp.ones((128, 128), bf16)
        signs = (jnp.where(col < row, 1.0, 0.0) - jnp.where(col < first, 1.0, 0.0)).astype(bf16)
        is_before = row < first
        logs = [jnp.zeros((128, 128), f32) for _ in range(4)]
        for symbol in range(1, 6):
            here = symbols == symbol
            found = ones_where(here)
            upper = dot1(found, upto) + dot1(signs, dot1(found, every))
            after = jnp.where(is_before, -upper, upper - jnp.where(here, 1.0, 0.0))
            after_ref[symbol - 1] = after
            for h in range(4):
                logs[h] = logs[h] + after * log_small[h : h + 1, 24 + symbol : 25 + symbol]
        for h in range(4):
            decay_ref[h] = jnp.where(symbols > 0, jnp.exp2(logs[h]), 0.0)
        sums = gram_sums(ca_ref, cb_ref, decay_ref, lhs_ref, rhs_ref)
        sums_ref[...] = sums
        gram_xs = gxs_ref[...]
        both = jnp.concatenate([weights * gram_xs for weights in expand_grams(sums)], axis=1)
        states = dot3(gbt_ref[...], both)
        carry_ref[0] = states[:, :256]
        carry_ref[1] = states[:, 256:]

    for branch in range(2):
        block = step_at if branch == 0 else 3 - step_at
        rows = pl.ds(pl.multiple_of(block * BLOCK, BLOCK), BLOCK)
        apart = iota((BLOCK, BLOCK), 0) - iota((BLOCK, BLOCK), 1)
        lower = branch == 0
        behind = apart >= 0 if lower else apart <= 0
        ahead = apart <= 0 if lower else apart >= 0
        pre, step, counts_t, log_wide, log_rows = scan_inputs(
            oh_ref[rows, :], oht_ref[:, rows], pre_ref[:, 512 * branch : 512 * branch + 512],
            step_ref[:, 256 * branch : 256 * branch + 256],
            lx_ref[:, 256 * branch : 256 * branch + 256],
            lrow_ref[8 * branch : 8 * branch + 8, :], ahead, behind,
        )
        act = pre * sigmoid(pre)
        x = act[:, :256]
        b = act[:, 256:384]
        c = act[:, 384:]
        xs = x * step
        state = carry_ref[branch]
        states_ref[branch, 0] = state
        inner = dot3(c, b, NT)
        parts = []
        for h in range(4):
            decays = triangle(
                lower, log_wide[:, h * HDIM : h * HDIM + 1], log_rows[h : h + 1, :], inner
            )
            parts.append(dot1(decays, xs[:, h * HDIM : (h + 1) * HDIM]))
        within = jnp.concatenate(parts, axis=1)
        y = within + dot3(c, state) * jnp.exp2(log_wide)
        y_refs[branch][...] = y + wide_ref[17:18, :] * x
        edge = log_wide[BLOCK - 1 :] if lower else log_wide[:1]
        carry_ref[branch] = jnp.exp2(edge) * state + dot3(b, jnp.exp2(edge - log_wide) * xs, TN)


def own_row(ref, rank):
    return jnp.concatenate([ref[pl.ds(2 * rank, 1), :], ref[pl.ds(2 * rank + 1, 1), :]], axis=1)


def slope_kernel(
    at_ref, y_first_ref, y_second_ref, oh_ref, gate_ref, cot_ref, ow_ref, gain_ref,
    slope_ref, sums_ref,
):
    slope = lax.dot_general(cot_ref[...], ow_ref[...], NT, preferred_element_type=f32)
    slope_ref[...] = slope
    weighted = slope * own_row(gain_ref, at_ref[1])
    gates = dot1(oh_ref[...], gate_ref[...])
    for branch in range(2):
        g = (y_first_ref, y_second_ref)[branch][...] * gates[:, 256 * branch : 256 * branch + 256]
        for kind, product in enumerate((g * g, weighted * g)):
            at = 2 * branch + kind
            product = product[:, :128] + product[:, 128:]
            for j in range(product.shape[0] // 128):
                cols = slice(128 * j, 128 * j + 128)
                total = jnp.sum(jnp.transpose(product[cols]), axis=0, keepdims=True)
                for peer in range(sums_ref.shape[0]):
                    sums_ref[peer, at : at + 1, cols] = total


def mix_rows(y_refs, oh_ref, oht_ref, slope_ref, sums_ref, gate_ref, gain, dgate_ref, dgain_ref):
    slope = slope_ref[...]
    sums = sums_ref[0]
    for peer in range(1, sums_ref.shape[0]):
        sums = sums + sums_ref[peer]
    scale = lax.rsqrt(sums / INNER + EPSILON)
    crossed = jnp.concatenate([sums[1:2], sums[1:2], sums[3:4], sums[3:4]], axis=0)
    weight = scale * scale * scale * crossed / INNER
    kind = iota(sums.shape, 0)
    weight = jnp.concatenate([weight[0:1], weight[0:1], weight[2:3], weight[2:3]], axis=0)
    rows = jnp.where(kind % 2 == 0, scale, weight)
    rows = jnp.concatenate([rows, rows] * 16, axis=0)
    parts = []
    for j in range(rows.shape[1] // 128):
        parts.append(jnp.transpose(rows[:, 128 * j : 128 * j + 128]))
    columns = jnp.concatenate(parts, axis=0)
    sloped = slope * gain
    gates = dot1(oh_ref[...], gate_ref[...])
    total = None
    dys = []
    for branch in range(2):
        gate = gates[:, 256 * branch : 256 * branch + 256]
        y = y_refs[branch][...]
        g = y * gate
        scale = columns[:, 2 * branch : 2 * branch + 1]
        weight = columns[:, 2 * branch + 1 : 2 * branch + 2]
        normed = g * scale
        total = normed if total is None else total + normed
        dg = scale * sloped - weight * g
        dys.append(dg * gate)
        lanes = oht_ref[32 * branch : 32 * branch + 32, :]
        dgate_ref[branch] += dot2(lanes, dg * y)
    dgain_ref[...] += jnp.sum(slope * total, axis=0, keepdims=True)
    return (total * gain).astype(bf16), dys


def backward_scan(
    branch, oh_ref, oht_ref, y_ref, state_ref, later_ref, dy_ref, pre_ref, step_ref, lx_ref,
    lrow_ref, wide_ref,
    tables_ref, steps_ref, logs_ref, skips_ref, carry_ref,
):
    skip = wide_ref[17:18, :]
    apart = iota((BLOCK, BLOCK), 0) - iota((BLOCK, BLOCK), 1)
    ahead = apart <= 0 if branch == 0 else apart >= 0
    behind = apart >= 0 if branch == 0 else apart <= 0
    onehot_t = oht_ref[32 * branch : 32 * branch + 32, :]
    pre, step, counts_t, log_wide, log_rows = scan_inputs(
        oh_ref[...], oht_ref[...], pre_ref[:, 512 * branch : 512 * branch + 512],
        step_ref[:, 256 * branch : 256 * branch + 256],
        lx_ref[:, 256 * branch : 256 * branch + 256],
        lrow_ref[8 * branch : 8 * branch + 8, :], ahead, behind,
    )
    counts_t = counts_t[32 * branch : 32 * branch + 32]
    logistic = sigmoid(pre)
    act = pre * logistic
    bend = logistic * (1.0 + pre * (1.0 - logistic))
    x = act[:, :256]
    b = act[:, 256:384]
    c = act[:, 384:]
    xs = x * step
    dy = dy_ref[...]
    own = y_ref[...] - skip * x
    state = state_ref[0, 0]
    pull = carry_ref[branch]
    xs_low = xs.astype(bf16)
    dy_low = dy.astype(bf16)
    inner = dot3(b, c, NT)
    parts = []
    slopes = jnp.zeros((BLOCK, BLOCK), f32)
    for h in range(4):
        wide = slice(h * HDIM, (h + 1) * HDIM)
        decays = triangle(
            branch == 1, log_wide[:, h * HDIM : h * HDIM + 1], log_rows[h : h + 1, :], None, -1.0
        )
        parts.append(dot1(inner * decays, dy_low[:, wide]))
        slopes = slopes + dot1(xs_low[:, wide], dy_low[:, wide], NT) * decays
    within = jnp.concatenate(parts, axis=1)
    faded = jnp.exp2(log_wide) * dy
    edge = log_wide[BLOCK - 1 :] if branch == 0 else log_wide[:1]
    tail = jnp.exp2(edge - log_wide)
    db = dot1(slopes, c) + dot1(tail * xs, pull, NT)
    dc = dot1(slopes, b, TN) + dot1(faded, state, NT)
    dxs = within + tail * dot1(b, pull)
    dlog = dy_low.astype(f32) * own - xs_low.astype(f32) * dxs
    edge_count = counts_t[:, BLOCK - 1 :] if branch == 0 else counts_t[:, :1]
    ahead = jnp.sum(later_ref[0, 0] * pull, axis=0, keepdims=True)
    logs_ref[...] += dot2(counts_t, dlog) + edge_count * ahead
    carry_ref[branch] = dot1(c, faded, TN) + jnp.exp2(edge) * pull
    dpre = jnp.concatenate([step * dxs + skip * dy, db, dc], axis=1) * bend
    tables_ref[...] += dot2(onehot_t, dpre)
    steps_ref[...] += dot2(onehot_t, x * dxs)
    skips_ref[...] += jnp.sum(dy * x, axis=0, keepdims=True)


def first_backward_kernel(at_ref, *refs):
    upper, lower, tables = refs[0:5], refs[5:10], refs[10:15]
    (
        upper_second_ref, lower_first_ref, upper_slope_ref, lower_slope_ref, upper_cot_ref,
        lower_cot_ref, upper_sums_ref, lower_sums_ref, gate_ref, gain_ref,
    ) = refs[15:25]
    sums, outer_ref = refs[25:30], refs[30]
    mixed_ref, first_out_ref, second_out_ref, dgate_ref, dgain_ref = refs[31:36]
    first_ref, second_ref = refs[36:38]
    step_at = pl.program_id(0)

    @pl.when(step_at == 0)
    def _():
        for ref in (*sums, outer_ref, dgate_ref, dgain_ref):
            ref[...] = jnp.zeros_like(ref)

    gain = own_row(gain_ref, at_ref[1])
    upper_mixed, (dy, dy_later) = mix_rows(
        (upper[2], upper_second_ref), upper[0], upper[1], upper_slope_ref, upper_sums_ref,
        gate_ref, gain, dgate_ref, dgain_ref,
    )
    first_ref[...] = dy
    second_out_ref[...] = dy_later
    lower_mixed, (dy_later, dy) = mix_rows(
        (lower_first_ref, lower[2]), lower[0], lower[1], lower_slope_ref, lower_sums_ref,
        gate_ref, gain, dgate_ref, dgain_ref,
    )
    second_ref[...] = dy
    first_out_ref[...] = dy_later
    mixed_ref[pl.ds(pl.multiple_of((3 - step_at) * BLOCK, BLOCK), BLOCK), :] = upper_mixed
    mixed_ref[pl.ds(pl.multiple_of(step_at * BLOCK, BLOCK), BLOCK), :] = lower_mixed
    backward_scan(0, *upper, first_ref, *tables, *sums)
    backward_scan(1, *lower, second_ref, *tables, *sums)
    cot = jnp.concatenate([upper_cot_ref[...], lower_cot_ref[...]], axis=0)
    mixed = jnp.concatenate([upper_mixed, lower_mixed], axis=0)
    outer_ref[...] += lax.dot_general(cot, mixed, TN, preferred_element_type=f32)


def second_backward_kernel(at_ref, *refs):
    blocks = (refs[0:6], refs[6:12])
    tables, sums_in = refs[12:17], refs[17:22]
    (
        ca_ref, cb_ref, tokens_ref, goht_ref, sums_ref, decay_ref, after_ref, gact_any, gbend_any,
        gstep_any, tab_ref, weight_any, cot_any, conv_x_ref, conv_bc_ref, dgate_ref, dgain_ref,
        packed_ref,
        mark_ref, found_ref, tables_ref, steps_ref, logs_ref, skips_ref, pull_ref,
        gact_ref, gbend_ref, gstep_ref, gate_w_ref, x_w_ref, bc_w_ref, step_w_ref, cot_ref, sems,
    ) = refs[22:]
    wide_ref = tables[4]
    sums = (tables_ref, steps_ref, logs_ref, skips_ref, pull_ref)
    own_at = pl.multiple_of(at_ref[1] * 256, 256)
    fetched = (
        (gact_any, gact_ref),
        (gbend_any, gbend_ref),
        (gstep_any, gstep_ref),
        (weight_any.at[pl.ds(own_at, 256), :], gate_w_ref),
        (weight_any.at[pl.ds(INNER + own_at, 256), :], x_w_ref),
        (weight_any.at[pl.ds(2 * INNER, 256), :], bc_w_ref),
        (weight_any.at[pl.ds(2 * INNER + 256, HEADS), :], step_w_ref),
        (cot_any, cot_ref),
    )
    copies = [
        pltpu.make_async_copy(source, target, sems.at[k])
        for k, (source, target) in enumerate(fetched)
    ]

    @pl.when(pl.program_id(0) == 0)
    def _():
        for copy in copies:
            copy.start()
        for ref, ref_in in zip(sums, sums_in):
            ref[...] = ref_in[...]

    for branch in range(2):
        backward_scan(branch, *blocks[branch], *tables, *sums)

    @pl.when(pl.program_id(0) == 1)
    def _():
        for copy in copies:
            copy.wait()
        far_and_pack(
            at_ref[1], pull_ref, wide_ref, ca_ref, cb_ref, tokens_ref, goht_ref,
            sums_ref, decay_ref, after_ref, gact_ref, gbend_ref, gstep_ref, tab_ref, gate_w_ref,
            x_w_ref, bc_w_ref, step_w_ref, cot_ref, conv_x_ref, conv_bc_ref, dgate_ref, dgain_ref,
            packed_ref, mark_ref, found_ref, tables_ref, steps_ref, logs_ref, skips_ref,
        )


def far_and_pack(
    rank, pull_ref, wide_ref, ca_ref, cb_ref, tokens_ref, goht_ref,
    sums_ref, decay_ref, after_ref, gact_ref, gbend_ref, gstep_ref, tab_ref, gate_w_ref,
    x_w_ref, bc_w_ref, step_w_ref, cot_ref, conv_x_ref, conv_bc_ref, dgate_ref, dgain_ref,
    packed_ref, mark_ref, found_ref, tables_ref, steps_ref, logs_ref, skips_ref,
):
    gram_x = gact_ref[:, :256]
    gram_b = gact_ref[:, 256:]
    gram_step = gstep_ref[...]
    gram_xs = gram_x * gram_step
    dxs = jnp.zeros((CODES * CODES, 256), f32)
    db = jnp.zeros((CODES * CODES, 128), f32)
    found = []
    expanded = expand_grams(sums_ref[...])
    for branch, weights in enumerate(expanded):
        pull = pull_ref[branch]
        met = dot1(gram_b, pull)
        dxs = dxs + weights * met
        db = db + dot1(weights * gram_xs, pull, NT)
        found.append(gram_xs * met)
    dpre = jnp.concatenate([gram_step * dxs, db], axis=1) * gbend_ref[...]
    gram_t = goht_ref[...]
    tables_ref[:, :384] += dot2(gram_t, dpre)
    steps_ref[...] += dot2(gram_t, gram_x * dxs)
    table = gather_grams(found).astype(bf16)
    early_codes = iota((2 * CODES, 128), 0)
    late_codes = iota((CODES, 128), 0)

    def look_up(shard, unused):
        at = pl.ds(pl.multiple_of(shard * 8, 8), 8)
        early = ca_ref[at, :]
        late = cb_ref[at, :]
        for j in range(8):
            mark_ref[:, 128 * j : 128 * j + 128] = ones_where(early[j : j + 1] == early_codes)
        looked = dot1(table, mark_ref[...], TN)
        for h in range(4):
            rows = []
            for j in range(8):
                part = looked[32 * h : 32 * h + 32, 128 * j : 128 * j + 128]
                mine = late[j : j + 1] == late_codes
                rows.append(jnp.sum(jnp.where(mine, part, 0.0), axis=0, keepdims=True))
            found_ref[h, at, :] = jnp.concatenate(rows, axis=0)
        return unused

    lax.fori_loop(0, 16, look_up, 0, unroll=4)
    lane_head = iota((1, 256), 1) // HDIM
    sub = iota((8, 256), 0)
    far = jnp.zeros((8, 256), f32)
    for h in range(4):
        weighted = found_ref[h] * decay_ref[h]
        for symbol in range(5):
            total = jnp.sum(weighted * after_ref[symbol], axis=0, keepdims=True)
            total = jnp.sum(total, axis=1, keepdims=True)
            far = far + jnp.where((lane_head == h) & (sub == symbol + 1), total, 0.0)

    gate_tab = tab_ref[:, :256]
    x_tab = tab_ref[:, 256:512]
    bc_tab = tab_ref[:, 512:768]
    logistic = sigmoid(gate_tab)
    gate_part = (dgate_ref[0, 24:32, :] + dgate_ref[1, 24:32, :]) * (
        logistic * (1.0 + gate_tab * (1.0 - logistic))
    )
    conv_x = conv_x_ref[...]
    conv_bc = conv_bc_ref[...]
    x_part = jnp.zeros((8, 256), f32)
    bc_part = jnp.zeros((8, 256), f32)
    x_taps = []
    bc_taps = []
    for k in range(KCONV):
        dtap_x = tables_ref[8 * k : 8 * k + 8, :256]
        dtap_bc = tables_ref[8 * k : 8 * k + 8, 256:]
        x_part = x_part + conv_x[k : k + 1] * dtap_x
        bc_part = bc_part + conv_bc[k : k + 1] * dtap_bc
        x_taps.append(jnp.sum(dtap_x * x_tab, axis=0, keepdims=True))
        bc_taps.append(jnp.sum(dtap_bc * bc_tab, axis=0, keepdims=True))
    bias = tables_ref[6:7, :]
    same = ones_where(iota((256, 256), 0) // HDIM == iota((256, 256), 1) // HDIM)
    log_part = dot_exact(logs_ref[24:32, :], same) + far
    step_part = dot_exact(steps_ref[24:32, :], same) - wide_ref[16:17, :] * log_part
    step_part = step_part * wide_ref[0:8, :]
    rate_part = jnp.sum(log_part * wide_ref[8:16, :], axis=0, keepdims=True)
    skip_part = dot_exact(jnp.broadcast_to(skips_ref[...], (8, 256)), same)
    valid = (sub >= 1) & (sub <= 5)
    step_part = jnp.where(valid, step_part, 0.0)
    step_rows = jnp.where(
        sub == 0,
        jnp.sum(step_part, axis=0, keepdims=True),
        jnp.where(sub == 6, rate_part, jnp.where(sub == 7, skip_part, step_part)),
    )
    spread = iota((256, 128), 1)
    narrow = ones_where(
        (iota((256, 128), 0) % HDIM == 0)
        & (rank * 4 + iota((256, 128), 0) // HDIM == spread)
    )
    step_heads = dot_exact(step_rows, narrow)

    def against(part, weights):
        first_piece = part.astype(bf16)
        rest = part - first_piece.astype(f32)
        second_piece = rest.astype(bf16)
        third_piece = rest - second_piece.astype(f32)
        return dot1(first_piece, weights) + (
            dot1(second_piece, weights) + dot1(third_piece, weights)
        )

    embed_part = (
        dot1(tokens_ref[...], cot_ref[...])[24:32]
        + against(jnp.where(valid, gate_part, 0.0), gate_w_ref[...])
        + against(jnp.where(valid, x_part, 0.0), x_w_ref[...])
        + against(jnp.where(valid, bc_part, 0.0), bc_w_ref[...])
        + against(jnp.where(valid[:, :HEADS], step_heads[:, :HEADS], 0.0), step_w_ref[...])
    )

    def rows_of(part, zero, six, seven):
        return jnp.where(
            sub == 0, zero, jnp.where(sub == 6, six, jnp.where(sub == 7, seven, part))
        )

    gate_rows = rows_of(gate_part, x_taps[0], x_taps[1], x_taps[2])
    x_rows = rows_of(x_part, x_taps[3], bias[:, :256], dgain_ref[...])
    bc_rows = rows_of(bc_part, bc_taps[0], bc_taps[1], bc_taps[2])
    embed_first = rows_of(embed_part[:, :256], bc_taps[3], bias[:, 256:], 0.0)
    for half in range(2):
        cols = slice(128 * half, 128 * half + 128)
        packed_ref[half] = gate_rows[:, cols]
        packed_ref[2 + half] = x_rows[:, cols]
        packed_ref[4 + half] = bc_rows[:, cols]
        packed_ref[7 + half] = embed_first[:, cols]
    packed_ref[6] = step_heads
    for piece in range(2, 8):
        packed_ref[7 + piece] = embed_part[:, 128 * piece : 128 * piece + 128]
    packed_ref[15] = jnp.zeros((8, 128), f32)


def out_kernel(mixed_ref, ow_ref, token_ref, embed_ref, out_ref):
    total = dot1(token_ref[...], embed_ref[...])
    for peer in range(mixed_ref.shape[0]):
        total = total + dot1(mixed_ref[peer], ow_ref[256 * peer : 256 * peer + 256, :])
    out_ref[...] = total.astype(bf16)


def final_kernel(
    whole_ref, embed_ref,
    w_in_ref, embedding_ref, conv_ref, bias_ref, dt_ref, rate_ref, skip_ref, gain_ref,
):
    def summed(piece):
        total = whole_ref[0, piece]
        for k in range(1, 8):
            total = total + whole_ref[k, piece]
        return total

    embed = embed_ref[...]

    def outer(table, first):
        one = table.astype(bf16)
        rest = table - one.astype(f32)
        two = rest.astype(bf16)
        three = rest - two.astype(f32)
        pieces = jnp.concatenate([one.astype(f32), two.astype(f32), three], axis=0)
        value = dot1(embed, pieces)
        w_in_ref[:, first : first + table.shape[1]] = value

    for rank in range(8):
        for half in range(2):
            gate = whole_ref[rank, half]
            x = whole_ref[rank, 2 + half]
            at = 256 * rank + 128 * half
            cols = slice(at, at + 128)
            outer(gate, at)
            outer(x, INNER + at)
            conv_ref[0:1, cols] = gate[0:1]
            conv_ref[1:2, cols] = gate[6:7]
            conv_ref[2:3, cols] = gate[7:8]
            conv_ref[3:4, cols] = x[0:1]
            bias_ref[2 * rank + half : 2 * rank + half + 1, :] = x[6:7]
            gain_ref[2 * rank + half : 2 * rank + half + 1, :] = x[7:8]
    for half in range(2):
        bc = summed(4 + half)
        at = INNER + 128 * half
        cols = slice(at, at + 128)
        outer(bc, INNER + at)
        rest = summed(7 + half)
        conv_ref[0:1, cols] = bc[0:1]
        conv_ref[1:2, cols] = bc[6:7]
        conv_ref[2:3, cols] = bc[7:8]
        conv_ref[3:4, cols] = rest[0:1]
        bias_ref[16 + half : 17 + half, :] = rest[6:7]
    steps = summed(6)[:, :HEADS]
    outer(steps, 2 * INNER + 2 * STATE)
    dt_ref[...] = steps[0:1]
    rate_ref[...] = steps[6:7]
    skip_ref[...] = steps[7:8]
    for piece in range(8):
        embedding_ref[:, 128 * piece : 128 * piece + 128] = summed(7 + piece)[1:6]


VMEM = pl.BlockSpec(memory_space=pltpu.VMEM)
VMEM_LIMIT = 62 * 1024 * 1024
TOKEN_STEPS = 2
ANY = pl.BlockSpec(memory_space=pl.ANY)


def whole(array):
    zeros = (0,) * array.ndim
    return pl.BlockSpec(array.shape, lambda i, at: zeros)


def own(shape, index):
    return pl.BlockSpec(shape, index)


def call(kernel, at, operands, outs, scratch=(), cost=5e9, steps=1):
    arrays = [item[0] if isinstance(item, tuple) else item for item in operands]
    specs = [
        (own(*item[1:]) if len(item) > 2 else ANY) if isinstance(item, tuple) else whole(item)
        for item in operands
    ]
    shapes = [jax.ShapeDtypeStruct(item[0], item[1]) for item in outs]
    out_specs = [
        own(item[2], item[3]) if len(item) > 2 else whole(shape)
        for item, shape in zip(outs, shapes)
    ]
    return pl.pallas_call(
        kernel,
        out_shape=shapes,
        grid_spec=pltpu.PrefetchScalarGridSpec(
            num_scalar_prefetch=1,
            grid=(steps,),
            in_specs=specs,
            out_specs=out_specs,
            scratch_shapes=list(scratch),
        ),
        compiler_params=pltpu.CompilerParams(vmem_limit_bytes=VMEM_LIMIT),
        cost_estimate=pl.CostEstimate(flops=int(cost), bytes_accessed=4000000, transcendentals=0),
    )(at, *arrays)


def call_plain(kernel, operands, outs, cost=1e9):
    return pl.pallas_call(
        kernel,
        out_shape=[jax.ShapeDtypeStruct(shape, kind) for shape, kind in outs],
        in_specs=[VMEM] * len(operands),
        out_specs=[VMEM] * len(outs),
        compiler_params=pltpu.CompilerParams(vmem_limit_bytes=VMEM_LIMIT),
        cost_estimate=pl.CostEstimate(flops=int(cost), bytes_accessed=1000000, transcendentals=0),
    )(*operands)


def gather(shard, axis):
    devices = lax.axis_size(axis)
    spread = jnp.broadcast_to(shard[None], (devices,) + shard.shape)
    return lax.all_to_all(spread, axis, split_axis=0, concat_axis=0, tiled=True)


def gather_by_flips(array, axis, flips):
    pairs = [[(i, i ^ flip) for i in range(lax.axis_size(axis))] for flip in flips]
    return jnp.concatenate([array] + [lax.ppermute(array, axis, pair) for pair in pairs], axis=0)


def sum_by_flips(array, axis, flips):
    pairs = [[(i, i ^ flip) for i in range(lax.axis_size(axis))] for flip in flips]
    one, two, three = [lax.ppermute(array, axis, pair) for pair in pairs]
    return (array + one) + (two + three)


def exchange(array, axis):
    return lax.all_to_all(array, axis, split_axis=0, concat_axis=0, tiled=True)


def body(
    base_ids, embedding, in_weight, conv_weight, conv_bias, dt_bias, a_log, skip_weight, norm_gain,
    out_weight, cotangent,
):
    groups = lax.axis_size("head")
    shards = lax.axis_size("seq")
    width = HEADS // groups * HDIM
    head_rank = lax.axis_index("head")
    seq_rank = lax.axis_index("seq")
    length = base_ids.shape[0]
    token_rows = length // groups
    at = jnp.stack([seq_rank, head_rank]).astype(jnp.int32)

    near = gather_by_flips(base_ids.reshape(1, 8, 128), "seq", (1, 8, 9))
    near, in_weight = lax.optimization_barrier((near, in_weight))
    ids = gather_by_flips(near, "seq", (2, 4, 6))
    cot_all = gather(cotangent, "head").reshape(length, D)
    weight_t = in_weight.T
    gain_rows = norm_gain.reshape(INNER // 128, 128)
    grams = _gram_onehot()
    gram_rows = jnp.asarray(grams, bf16)
    gram_cols = jnp.asarray(np.ascontiguousarray(grams[:, :32].T), bf16)
    weights = [
        (weight_t, (width, D), lambda i, at: (at[1], 0)),
        (weight_t, (width, D), lambda i, at: (INNER // width + at[1], 0)),
        (weight_t, (256, D), lambda i, at: (16, 0)),
        (weight_t, (128, D), lambda i, at: (34, 0)),
    ]
    convs = [
        (conv_weight, (KCONV, width), lambda i, at: (0, at[1])),
        (conv_weight, (KCONV, width), lambda i, at: (0, INNER // width)),
    ]
    count = CODES * CODES
    big, logs, log_rows, tab, wide, gxs, gbt = call(
        prep_kernel,
        at,
        [
            embedding,
            *weights,
            *convs,
            conv_bias.reshape(conv_bias.shape[0] // 128, 128),
            dt_bias[None, :],
            a_log[None, :],
            skip_weight[None, :],
            gram_rows,
        ],
        [
            ((128, 2048), bf16),
            ((128, 512), bf16),
            ((16, 128), f32),
            ((8, 768), f32),
            ((24, width), f32),
            ((count, width), f32),
            ((STATE, count), f32),
        ],
        cost=6e9,
    )

    blocks = length // BLOCK

    tables = [
        (big, (128, 1024), lambda k, at: (0, 0)),
        (big, (128, 512), lambda k, at: (0, 2)),
        logs,
        log_rows,
        wide,
    ]

    def rows_at(array, rows, index):
        return (array, (rows, array.shape[1]), lambda k, at: (index(k), 0))

    y_first, y_second, states, sums, decays, after, onehot, onehot_t, early, late = call(
        forward_kernel,
        at,
        [ids, *tables, gxs, gbt],
        [
            ((length, width), f32, (BLOCK, width), lambda k, at: (k, 0)),
            ((length, width), f32, (BLOCK, width), lambda k, at: (blocks - 1 - k, 0)),
            (
                (2, blocks, STATE, width), f32,
                (2, 1, STATE, width), lambda k, at: (0, k, 0, 0),
            ),
            ((2 * CODES, 128), f32),
            ((4, 128, 128), f32),
            ((5, 128, 128), f32),
            ((length, 128), bf16),
            ((128, length), bf16),
            ((128, 128), jnp.int32),
            ((128, 128), jnp.int32),
        ],
        [
            pltpu.VMEM((8, 128, 128), jnp.int32),
            pltpu.VMEM((128, 4096), bf16),
            pltpu.VMEM((2 * CODES, 4096), bf16),
            pltpu.VMEM((2, STATE, width), f32),
        ],
        cost=1.5e10,
        steps=blocks,
    )

    chunk = length // TOKEN_STEPS
    gates = (big, (128, 512), lambda k, at: (0, 3))
    y_rows = [rows_at(y, chunk, lambda k: k) for y in (y_first, y_second)]
    hot_rows = rows_at(onehot, chunk, lambda k: k)
    slope, row_sums = call(
        slope_kernel,
        at,
        [
            *y_rows,
            hot_rows,
            gates,
            rows_at(cot_all, chunk, lambda k: k),
            (out_weight, (width, D), lambda k, at: (at[1], 0)),
            gain_rows,
        ],
        [
            ((length, width), f32, (chunk, width), lambda k, at: (k, 0)),
            ((groups, 4, length), f32, (groups, 4, chunk), lambda k, at: (0, 0, k)),
        ],
        cost=4e9,
        steps=TOKEN_STEPS,
    )
    row_sums, big, ids_later, embed_later = lax.optimization_barrier(
        (row_sums, big, base_ids, embedding)
    )
    gact, gbend, gstep = call(
        gram_kernel,
        at,
        [
            gram_rows,
            (big, (128, 512), lambda k, at: (0, 0)),
            (big, (128, 256), lambda k, at: (0, 4)),
        ],
        [((count, 384), f32), ((count, 384), f32), ((count, width), f32)],
        cost=2e9,
    )
    row_sums = exchange(row_sums, "head")
    def scan_operands(first_step):
        operands = []
        for branch, y in ((0, y_first), (1, y_second)):

            def nth(k):
                return first_step + k

            def block(k, branch=branch):
                return blocks - 1 - nth(k) if branch == 0 else nth(k)

            def state(k, at, branch=branch):
                return (branch, blocks - 1 - nth(k), 0, 0)

            def later(k, at, branch=branch):
                return (branch, jnp.minimum(blocks - nth(k), blocks - 1), 0, 0)

            one = (1, 1, STATE, width)
            operands.append(
                [
                    rows_at(onehot, BLOCK, block),
                    (onehot_t, (128, BLOCK), lambda k, at, block=block: (0, block(k))),
                    rows_at(y, BLOCK, block),
                    (states, one, state),
                    (states, one, later),
                ]
            )
        return operands

    accumulators = [
        ((32, 512), f32),
        ((32, width), f32),
        ((32, width), f32),
        ((1, width), f32),
        ((2, STATE, width), f32),
    ]
    first, second = scan_operands(0)

    def upper(k):
        return blocks - 1 - k

    def lower(k):
        return k

    def sums_at(index):
        return (row_sums, (groups, 4, BLOCK), lambda k, at: (0, 0, index(k)))

    *grads, partial, mixed, dy_first, dy_second, dgate, dgain = call(
        first_backward_kernel,
        at,
        [
            *first,
            *second,
            *tables,
            rows_at(y_second, BLOCK, upper),
            rows_at(y_first, BLOCK, lower),
            rows_at(slope, BLOCK, upper),
            rows_at(slope, BLOCK, lower),
            rows_at(cot_all, BLOCK, upper),
            rows_at(cot_all, BLOCK, lower),
            sums_at(upper),
            sums_at(lower),
            gates,
            gain_rows,
        ],
        accumulators
        + [
            ((D, width), f32),
            ((length, width), bf16),
            ((length // 2, width), f32, (BLOCK, width), lambda k, at: (k, 0)),
            ((length // 2, width), f32, (BLOCK, width), lambda k, at: (1 - k, 0)),
            ((2, 32, width), f32),
            ((1, width), f32),
        ],
        [pltpu.VMEM((BLOCK, width), f32), pltpu.VMEM((BLOCK, width), f32)],
        cost=2e10,
        steps=blocks // 2,
    )
    partial = exchange(partial.reshape(shards, D // shards, width), "seq")
    first, second = scan_operands(blocks // 2)
    (packed,) = call(
        second_backward_kernel,
        at,
        [
            *first,
            rows_at(dy_first, BLOCK, lambda k: 1 - k),
            *second,
            rows_at(dy_second, BLOCK, lambda k: k),
            *tables,
            *grads,
            early,
            late,
            (onehot_t, (32, token_rows), lambda k, at: (0, at[1])),
            gram_cols,
            sums,
            decays,
            after,
            (gact,),
            (gbend,),
            (gstep,),
            tab,
            (weight_t,),
            (cotangent,),
            *convs,
            dgate,
            dgain,
        ],
        [((shards, 8, 128), f32)],
        [
            pltpu.VMEM((2 * CODES, 1024), bf16),
            pltpu.VMEM((4, 128, 128), f32),
            *[pltpu.VMEM(shape, kind) for shape, kind in accumulators],
            pltpu.VMEM((count, 384), f32),
            pltpu.VMEM((count, 384), f32),
            pltpu.VMEM((count, width), f32),
            pltpu.VMEM((width, D), bf16),
            pltpu.VMEM((width, D), bf16),
            pltpu.VMEM((256, D), bf16),
            pltpu.VMEM((HEADS, D), bf16),
            pltpu.VMEM((token_rows, D), bf16),
            pltpu.SemaphoreType.DMA((8,)),
        ],
        cost=2e10,
        steps=blocks // 2,
    )
    packed, partial, mixed = lax.optimization_barrier((packed, partial, mixed))
    mixed_all = exchange(mixed.reshape(groups, token_rows, width), "head")
    total = sum_by_flips(packed, "seq", (1, 8, 9))
    total = sum_by_flips(total, "seq", (2, 4, 6))

    grad_w_out = jnp.sum(partial, axis=0).T
    token_ids = lax.dynamic_slice_in_dim(ids_later, head_rank * token_rows, token_rows, 0)
    alphabet = jnp.arange(5, dtype=jnp.int32)
    token_hot = (token_ids[:, None] == alphabet[None, :]).astype(bf16)
    (layer_out,) = call_plain(
        out_kernel,
        [mixed_all, out_weight, token_hot, embedding],
        [((token_rows, D), bf16)],
        4e9,
    )

    row_count = D // shards
    columns = lax.dynamic_slice_in_dim(embed_later, seq_rank * row_count, row_count, 1)
    columns = jnp.pad(columns, ((1, 2), (0, 0)))
    columns = jnp.concatenate([columns] * 3, axis=0).T
    everything = gather(total, "head")
    w_in, embed, conv, bias, dt, rate, skip, gain = call_plain(
        final_kernel,
        [everything, columns],
        [
            ((row_count, in_weight.shape[1]), f32),
            (embedding.shape, f32),
            (conv_weight.shape, f32),
            ((conv_bias.shape[0] // 128, 128), f32),
            ((1, HEADS), f32),
            ((1, HEADS), f32),
            ((1, HEADS), f32),
            ((INNER // 128, 128), f32),
        ],
    )
    return (
        layer_out, w_in, grad_w_out, embed, conv, bias.reshape(-1), dt[0], rate[0], skip[0],
        gain.reshape(-1),
    )


def solution(mesh):
    return jax.shard_map(
        body,
        mesh=mesh,
        in_specs=(P("seq"), P(), P(), P(), P(), P(), P(), P(), P(), P(), P(("seq", "head"), None)),
        out_specs=(
            P(("seq", "head"), None),
            P("seq", None),
            P("head", "seq"),
            P(),
            P(),
            P(),
            P(),
            P(),
            P(),
            P(),
        ),
        check_vma=False,
    )
```

```python
import jax
import jax.numpy as jnp
import numpy as np
from jax import lax
from jax.experimental import pallas as pl
from jax.experimental.pallas import tpu as pltpu
from jax.sharding import PartitionSpec as P

D = 1024
HEADS = 32
HDIM = 64
STATE = 128
BLOCK = 256
KCONV = 4
INNER = 2048
EPSILON = 1e-05
LOG2E = 1.4426950408889634

f32 = jnp.float32
bf16 = jnp.bfloat16
NN = (((1,), (0,)), ((), ()))
NT = (((1,), (1,)), ((), ()))
TN = (((0,), (0,)), ((), ()))

CODES = 32

OWN = 4
SHARED = 11


def _decode_codes():
    first = np.zeros((CODES,), np.int32)
    second = np.zeros((CODES,), np.int32)
    for code in range(25):
        first[code], second[code] = code // 5 + 1, code % 5 + 1
    for code in range(25, 30):
        second[code] = code - 24
    return first, second


def _gram_onehot():
    first, second = _decode_codes()
    early, late = np.divmod(np.arange(CODES * CODES), CODES)
    symbols = (first[early], second[early], first[late], second[late])
    rows = np.zeros((CODES * CODES, 128), np.float32)
    for tap, symbol in enumerate(symbols):
        valid = symbol > 0
        rows[np.arange(CODES * CODES)[valid], (8 * tap + symbol)[valid]] = 1.0
    rows[:, 6] = 1.0
    rows[:, 64:96] = rows[:, :32]
    return rows


def encode(earlier, later):
    return jnp.where(
        earlier > 0, (earlier - 1) * 5 + later - 1, jnp.where(later > 0, 24 + later, 30)
    )


def complement_padded(symbols):
    return jnp.where((symbols >= 1) & (symbols <= 4), 5 - symbols, symbols)


def halves(values):
    high = values.astype(bf16)
    return high, (values - high.astype(f32)).astype(bf16)


def dot1(a, b, dims=NN):
    return lax.dot_general(a.astype(bf16), b.astype(bf16), dims, preferred_element_type=f32)


def doubled(values, axis):
    return jnp.concatenate([values, values], axis=axis)


def dot2(a, b, dims=NN):
    high, low = halves(b)
    a = a.astype(bf16)
    if a.shape[dims[0][0][0]] <= 128:
        pieces = jnp.concatenate([high, low], axis=dims[0][1][0])
        return dot1(doubled(a, dims[0][0][0]), pieces, dims)
    return dot1(a, high, dims) + dot1(a, low, dims)


def dot2l(a, b, dims=NN):
    high, low = halves(a)
    b = b.astype(bf16)
    if b.shape[dims[0][1][0]] <= 128:
        pieces = jnp.concatenate([high, low], axis=dims[0][0][0])
        return dot1(pieces, doubled(b, dims[0][1][0]), dims)
    return dot1(high, b, dims) + dot1(low, b, dims)


def dot3(a, b, dims=NN):
    a_high, a_low = halves(a)
    b_high, b_low = halves(b)
    if a.shape[dims[0][0][0]] <= 128:
        pieces = jnp.concatenate([a_high, a_low], axis=dims[0][0][0])
        return dot1(pieces, doubled(b_high, dims[0][1][0]), dims) + dot1(a_high, b_low, dims)
    return dot1(a_high, b_high, dims) + (dot1(a_high, b_low, dims) + dot1(a_low, b_high, dims))


def dot_exact(a, b, dims=NN):
    first = a.astype(bf16)
    rest = a - first.astype(f32)
    second = rest.astype(bf16)
    third = rest - second.astype(f32)
    b = b.astype(bf16)
    return dot1(first, b, dims) + (dot1(second, b, dims) + dot1(third, b, dims))


def iota(shape, axis):
    return lax.broadcasted_iota(jnp.int32, shape, axis)


def ones_where(condition):
    return jnp.where(condition, 1.0, 0.0).astype(bf16)


def expand_grams(sums):
    grams = CODES * CODES
    early = ones_where(iota((grams, CODES), 0) // CODES == iota((grams, CODES), 1))
    both = dot2(early, jnp.concatenate([sums[:CODES], sums[CODES:]], axis=1))
    mine = iota((grams, 128), 0) % CODES == iota((grams, 128), 1) % CODES
    widen = ones_where(iota((128, 256), 0) // CODES == iota((128, 256), 1) // HDIM)
    return [
        dot2l(jnp.where(mine, both[:, 128 * k : 128 * k + 128], 0.0), widen) for k in range(2)
    ]


def gather_grams(values):
    grams = CODES * CODES
    narrow = ones_where(iota((256, 128), 0) // HDIM == iota((256, 128), 1) // CODES)
    mine = iota((grams, 128), 0) % CODES == iota((grams, 128), 1) % CODES
    spread = [jnp.where(mine, dot1(value, narrow), 0.0) for value in values]
    early = ones_where(iota((CODES, grams), 1) // CODES == iota((CODES, grams), 0))
    both = dot1(early, jnp.concatenate(spread, axis=1))
    return jnp.concatenate([both[:, :128], both[:, 128:]], axis=0)


def sigmoid(values):
    return 0.5 * jnp.tanh(0.5 * values) + 0.5


def scan_inputs(onehot, onehot_t, pre_tab, step_tab, log_tab, log_rows, ahead, behind):
    pre = dot1(onehot, pre_tab)
    step = dot1(onehot, step_tab)
    counts = dot1(ones_where(behind), onehot).astype(bf16)
    counts_t = dot1(onehot_t, ones_where(ahead))
    log_wide = dot1(counts, log_tab)
    log_rows = dot1(log_rows.astype(bf16), counts_t)
    return pre, step, counts_t, log_wide, log_rows


def prep_kernel(
    at_ref, embed_ref, gate_w_ref, x_w_ref, bc_w_ref, step_w_ref, conv_x_ref, conv_bc_ref,
    bias_ref, dt_ref, rate_ref, skip_ref, goh_ref,
    big_ref, logs_ref, lrow_ref, tab_ref, wide_ref, gxs_ref, gbt_ref,
):
    rank = at_ref[1]
    place = ones_where(iota((8, 5), 0) == iota((8, 5), 1) + 1)
    embed = dot1(place, embed_ref[...]).astype(bf16)
    gate_w = gate_w_ref[...]
    x_w = x_w_ref[...]
    bc_w = bc_w_ref[...]
    step_w = step_w_ref[...]
    step_w = jnp.where(iota((128, D), 0) < HEADS, step_w.astype(f32), 0.0).astype(bf16)

    def heads_row(ref):
        return jnp.concatenate([ref[...], jnp.zeros((1, 128 - HEADS), f32)], axis=1)

    bias_x = jnp.concatenate(
        [bias_ref[pl.ds(2 * rank, 1), :], bias_ref[pl.ds(2 * rank + 1, 1), :]], axis=1
    )
    bias_bc = jnp.concatenate([bias_ref[16:17, :], bias_ref[17:18, :]], axis=1)
    gate = dot1(embed, gate_w, NT)
    x = dot1(embed, x_w, NT)
    bc = dot1(embed, bc_w, NT)
    tab_ref[:, :256] = gate
    tab_ref[:, 256:512] = x
    tab_ref[:, 512:768] = bc
    row = iota((8, 128), 0)
    lane = iota((8, 128), 1)
    valid = (row >= 1) & (row <= 5)
    pre = dot1(embed, step_w, NT) + heads_row(dt_ref)
    valid = valid & (lane < HEADS)
    step = jnp.maximum(pre, 0.0) + jnp.log1p(jnp.exp(-jnp.abs(pre)))
    rate = jnp.exp(heads_row(rate_ref))
    logs = jnp.where(valid, -(rate * step), 0.0)
    step = jnp.where(valid, step, 0.0)
    bent = jnp.where(valid, sigmoid(pre), 0.0)
    widen = ones_where(iota((128, 256), 0) == rank * 4 + iota((128, 256), 1) // HDIM)
    step_wide = dot_exact(step, widen)
    logs_wide = dot_exact(logs, widen)
    logs = logs * LOG2E
    wide_ref[0:8, :] = dot_exact(bent, widen)
    wide_ref[8:16, :] = logs_wide
    others = jnp.where(row == 0, rate, jnp.where(row == 1, heads_row(skip_ref), 0.0))
    others = jnp.where(lane < HEADS, others, 0.0)
    wide_ref[16:24, :] = dot_exact(others, widen)
    one_row = iota((8, 256), 0) == 6
    conv_x = conv_x_ref[...]
    conv_bc = conv_bc_ref[...]
    taps = []
    for k in range(4):
        tap_x = conv_x[k : k + 1] * x
        tap_bc = conv_bc[k : k + 1] * bc
        if k == 0:
            tap_x = jnp.where(one_row, bias_x, tap_x)
            tap_bc = jnp.where(one_row, bias_bc, tap_bc)
        taps.append(jnp.concatenate([tap_x, tap_bc], axis=1))
    silu_gate = gate * sigmoid(gate)

    def put(ref, start, pieces):
        nothing = jnp.zeros(pieces[0][1].shape, f32)
        pieces = dict(pieces)
        table = jnp.concatenate([pieces.get(k, nothing) for k in range(8)], axis=0)
        high, low = halves(table)
        ref[0:64, start : start + table.shape[1]] = high
        ref[64:128, start : start + table.shape[1]] = low
        return high, low

    first_high, first_low = put(big_ref, 0, list(enumerate(taps)))
    put(big_ref, 512, [(4 + k, tap) for k, tap in enumerate(taps)])
    step_high, step_low = put(big_ref, 1024, [(3, step_wide)])
    put(big_ref, 1280, [(7, step_wide)])
    put(big_ref, 1536, [(3, silu_gate)])
    put(big_ref, 1792, [(7, silu_gate)])
    put(logs_ref, 0, [(3, logs_wide * LOG2E)])
    put(logs_ref, 256, [(7, logs_wide * LOG2E)])
    pick = ones_where((iota((8, 128), 1) == rank * 4 + row) & (row < 4))
    nothing = jnp.zeros((8, 128), f32)
    for branch in range(2):
        spot = 3 + 4 * branch
        rows = jnp.concatenate([logs if k % 8 == spot else nothing for k in range(16)], axis=0)
        first = rows.astype(bf16)
        rest = rows - first.astype(f32)
        second = rest.astype(bf16)
        third = rest - second.astype(f32)
        values = dot1(pick, first, NT) + (dot1(pick, second, NT) + dot1(pick, third, NT))
        high = values.astype(bf16).astype(f32)
        lrow_ref[8 * branch : 8 * branch + 8, :] = jnp.where(lane < 64, high, values - high)
    grams = goh_ref[...]
    pre = dot1(grams, big_ref[:, :384])
    act = pre * sigmoid(pre)
    for j in range(8):
        cols = slice(128 * j, 128 * j + 128)
        gbt_ref[:, cols] = jnp.transpose(act[cols, 256:])
    gxs_ref[...] = act[:, :256] * dot1(grams, big_ref[:, 1024:1280])


def gram_kernel(at_ref, goh_ref, pre_ref, step_ref, gact_ref, gbend_ref, gstep_ref):
    pre = dot1(goh_ref[...], pre_ref[:, :384])
    logistic = sigmoid(pre)
    gact_ref[...] = pre * logistic
    gbend_ref[...] = logistic * (1.0 + pre * (1.0 - logistic))
    gstep_ref[...] = dot1(goh_ref[...], step_ref[...])


def shifted(symbols, by):
    row = iota((128, 128), 0)
    col = iota((128, 128), 1)
    if by > 0:
        rolled = pltpu.roll(symbols, by, axis=1)
        other = jnp.where(row == 0, 0, pltpu.roll(rolled, 1, axis=0))
        return jnp.where(col < by, other, rolled)
    rolled = pltpu.roll(symbols, 128 + by, axis=1)
    other = jnp.where(row == 127, 0, pltpu.roll(rolled, 127, axis=0))
    return jnp.where(col >= 128 + by, other, rolled)


def read_symbols(
    seq, ids_ref, ca_ref, cb_ref, taps_ref, oh_ref, oht_ref
):
    symbols = []
    for shard in range(16):
        mask = jnp.bitwise_xor(seq, shard)
        near = jnp.bitwise_and(mask, 1) + 2 * jnp.bitwise_and(mask // 8, 1)
        symbols.append(ids_ref[jnp.bitwise_and(mask // 2, 3) * 4 + near])
    symbols = jnp.concatenate(symbols, axis=0) + 1
    taps = [shifted(symbols, 3 - k) if k < 3 else symbols for k in range(4)]
    turned = [complement_padded(shifted(symbols, k - 3) if k < 3 else symbols) for k in range(4)]
    row = iota((128, 128), 0)
    is_before = row < seq * 8
    far = [jnp.where(is_before, a, b) for a, b in zip(taps, turned)]
    ca_ref[...] = encode(far[0], far[1]) + jnp.where(is_before, 0, CODES)
    cb_ref[...] = encode(far[2], far[3])
    for k in range(4):
        taps_ref[k] = taps[k]
        taps_ref[4 + k] = turned[k]
    at = pl.ds(pl.multiple_of(seq * 8, 8), 8)
    own = [taps_ref[k, at, :] for k in range(8)]
    sub = iota((8, 128), 0)
    for j in range(8):
        groups = []
        for k in range(8):
            hit = (own[k][j : j + 1] == sub) & (sub > 0)
            if k % 4 == 0:
                hit = hit | (sub == 6)
            groups.append(jnp.where(hit, 1.0, 0.0))
        rows = jnp.concatenate(groups + groups, axis=0)
        cols = slice(128 * j, 128 * j + 128)
        oht_ref[:, cols] = rows.astype(bf16)
        oh_ref[cols, :] = jnp.transpose(rows).astype(bf16)
    is_own = (row >= seq * 8) & (row < seq * 8 + 8)
    return jnp.where(is_own, 0, far[3])


def triangle(lower, column, row, inner, sign=1.0):
    half = BLOCK // 2
    apart = iota((half, half), 0) - iota((half, half), 1)
    keep = apart >= 0 if lower else apart <= 0
    parts = []
    for i in range(2):
        rows = slice(half * i, half * i + half)
        line = []
        for j in range(2):
            cols = slice(half * j, half * j + half)
            if (i < j) if lower else (i > j):
                line.append(jnp.zeros((half, half), f32))
                continue
            apart = column[rows] - row[:, cols] if sign > 0 else row[:, cols] - column[rows]
            if i == j:
                apart = jnp.where(keep, apart, -1e30)
            value = jnp.exp2(apart)
            line.append(value if inner is None else value * inner[rows, cols])
        parts.append(jnp.concatenate(line, axis=1))
    return jnp.concatenate(parts, axis=0)


def gram_sums(ca_ref, cb_ref, decay_ref, lhs_ref, rhs_ref):
    early_codes = iota((2 * CODES, 128), 0)
    late_codes = iota((CODES, 128), 0)

    def add(k, total):
        for j in range(32):
            if j % 8 == 0:
                at = pl.ds(pl.multiple_of(k * 32 + j, 8), 8)
                early = ca_ref[at, :]
                late = cb_ref[at, :]
                decays = [decay_ref[h, at, :] for h in range(4)]
            cols = slice(128 * j, 128 * j + 128)
            one = slice(j % 8, j % 8 + 1)
            rhs_ref[:, cols] = ones_where(early[one] == early_codes)
            mine = late[one] == late_codes
            for h in range(4):
                lhs_ref[32 * h : 32 * h + 32, cols] = jnp.where(mine, decays[h][one], 0.0).astype(
                    bf16
                )
        return total + dot1(rhs_ref[...], lhs_ref[...], NT)

    return lax.fori_loop(0, 4, add, jnp.zeros((2 * CODES, 128), f32), unroll=2)


def forward_kernel(
    at_ref, ids_ref, pre_ref, step_ref, lx_ref, lrow_ref, wide_ref, gxs_ref, gbt_ref,
    y_first_ref, y_second_ref, states_ref, sums_ref, decay_ref, after_ref, oh_ref, oht_ref,
    ca_ref, cb_ref,
    taps_ref, lhs_ref, rhs_ref, carry_ref,
):
    step_at = pl.program_id(0)
    y_refs = (y_first_ref, y_second_ref)

    @pl.when(step_at == 0)
    def _():
        seq = at_ref[0]
        first = seq * 8
        symbols = read_symbols(seq, ids_ref, ca_ref, cb_ref, taps_ref, oh_ref, oht_ref)
        log_small = lrow_ref[0:8, :] + pltpu.roll(lrow_ref[0:8, :], 64, axis=1)
        row = iota((128, 128), 0)
        col = iota((128, 128), 1)
        upto = ones_where(row <= col)
        every = jnp.ones((128, 128), bf16)
        signs = (jnp.where(col < row, 1.0, 0.0) - jnp.where(col < first, 1.0, 0.0)).astype(bf16)
        is_before = row < first
        logs = [jnp.zeros((128, 128), f32) for _ in range(4)]
        for symbol in range(1, 6):
            here = symbols == symbol
            found = ones_where(here)
            upper = dot1(found, upto) + dot1(signs, dot1(found, every))
            after = jnp.where(is_before, -upper, upper - jnp.where(here, 1.0, 0.0))
            after_ref[symbol - 1] = after
            for h in range(4):
                logs[h] = logs[h] + after * log_small[h : h + 1, 24 + symbol : 25 + symbol]
        for h in range(4):
            decay_ref[h] = jnp.where(symbols > 0, jnp.exp2(logs[h]), 0.0)
        sums = gram_sums(ca_ref, cb_ref, decay_ref, lhs_ref, rhs_ref)
        sums_ref[...] = sums
        gram_xs = gxs_ref[...]
        both = jnp.concatenate([weights * gram_xs for weights in expand_grams(sums)], axis=1)
        states = dot3(gbt_ref[...], both)
        carry_ref[0] = states[:, :256]
        carry_ref[1] = states[:, 256:]

    for branch in range(2):
        block = step_at if branch == 0 else 3 - step_at
        rows = pl.ds(pl.multiple_of(block * BLOCK, BLOCK), BLOCK)
        apart = iota((BLOCK, BLOCK), 0) - iota((BLOCK, BLOCK), 1)
        lower = branch == 0
        behind = apart >= 0 if lower else apart <= 0
        ahead = apart <= 0 if lower else apart >= 0
        pre, step, counts_t, log_wide, log_rows = scan_inputs(
            oh_ref[rows, :], oht_ref[:, rows], pre_ref[:, 512 * branch : 512 * branch + 512],
            step_ref[:, 256 * branch : 256 * branch + 256],
            lx_ref[:, 256 * branch : 256 * branch + 256],
            lrow_ref[8 * branch : 8 * branch + 8, :], ahead, behind,
        )
        act = pre * sigmoid(pre)
        x = act[:, :256]
        b = act[:, 256:384]
        c = act[:, 384:]
        xs = x * step
        state = carry_ref[branch]
        states_ref[branch, 0] = state
        inner = dot3(c, b, NT)
        parts = []
        for h in range(4):
            decays = triangle(
                lower, log_wide[:, h * HDIM : h * HDIM + 1], log_rows[h : h + 1, :], inner
            )
            parts.append(dot1(decays, xs[:, h * HDIM : (h + 1) * HDIM]))
        within = jnp.concatenate(parts, axis=1)
        y = within + dot3(c, state) * jnp.exp2(log_wide)
        y_refs[branch][...] = y + wide_ref[17:18, :] * x
        edge = log_wide[BLOCK - 1 :] if lower else log_wide[:1]
        carry_ref[branch] = jnp.exp2(edge) * state + dot3(b, jnp.exp2(edge - log_wide) * xs, TN)


def own_row(ref, rank):
    return jnp.concatenate([ref[pl.ds(2 * rank, 1), :], ref[pl.ds(2 * rank + 1, 1), :]], axis=1)


def slope_kernel(
    at_ref, y_first_ref, y_second_ref, oh_ref, gate_ref, cot_ref, ow_ref, gain_ref,
    slope_ref, sums_ref,
):
    slope = lax.dot_general(cot_ref[...], ow_ref[...], NT, preferred_element_type=f32)
    slope_ref[...] = slope
    weighted = slope * own_row(gain_ref, at_ref[1])
    gates = dot1(oh_ref[...], gate_ref[...])
    for branch in range(2):
        g = (y_first_ref, y_second_ref)[branch][...] * gates[:, 256 * branch : 256 * branch + 256]
        for kind, product in enumerate((g * g, weighted * g)):
            at = 2 * branch + kind
            product = product[:, :128] + product[:, 128:]
            for j in range(product.shape[0] // 128):
                cols = slice(128 * j, 128 * j + 128)
                total = jnp.sum(jnp.transpose(product[cols]), axis=0, keepdims=True)
                for peer in range(sums_ref.shape[0]):
                    sums_ref[peer, at : at + 1, cols] = total


def mix_rows(y_refs, oh_ref, oht_ref, slope_ref, sums_ref, gate_ref, gain, dgate_ref, dgain_ref):
    slope = slope_ref[...]
    sums = sums_ref[0]
    for peer in range(1, sums_ref.shape[0]):
        sums = sums + sums_ref[peer]
    scale = lax.rsqrt(sums / INNER + EPSILON)
    crossed = jnp.concatenate([sums[1:2], sums[1:2], sums[3:4], sums[3:4]], axis=0)
    weight = scale * scale * scale * crossed / INNER
    kind = iota(sums.shape, 0)
    weight = jnp.concatenate([weight[0:1], weight[0:1], weight[2:3], weight[2:3]], axis=0)
    rows = jnp.where(kind % 2 == 0, scale, weight)
    rows = jnp.concatenate([rows, rows] * 16, axis=0)
    parts = []
    for j in range(rows.shape[1] // 128):
        parts.append(jnp.transpose(rows[:, 128 * j : 128 * j + 128]))
    columns = jnp.concatenate(parts, axis=0)
    sloped = slope * gain
    gates = dot1(oh_ref[...], gate_ref[...])
    total = None
    dys = []
    for branch in range(2):
        gate = gates[:, 256 * branch : 256 * branch + 256]
        y = y_refs[branch][...]
        g = y * gate
        scale = columns[:, 2 * branch : 2 * branch + 1]
        weight = columns[:, 2 * branch + 1 : 2 * branch + 2]
        normed = g * scale
        total = normed if total is None else total + normed
        dg = scale * sloped - weight * g
        dys.append(dg * gate)
        lanes = oht_ref[32 * branch : 32 * branch + 32, :]
        dgate_ref[branch] += dot2(lanes, dg * y)
    dgain_ref[...] += jnp.sum(slope * total, axis=0, keepdims=True)
    return (total * gain).astype(bf16), dys


def backward_scan(
    branch, oh_ref, oht_ref, y_ref, state_ref, later_ref, dy_ref, pre_ref, step_ref, lx_ref,
    lrow_ref, wide_ref,
    tables_ref, steps_ref, logs_ref, skips_ref, carry_ref,
):
    skip = wide_ref[17:18, :]
    apart = iota((BLOCK, BLOCK), 0) - iota((BLOCK, BLOCK), 1)
    ahead = apart <= 0 if branch == 0 else apart >= 0
    behind = apart >= 0 if branch == 0 else apart <= 0
    onehot_t = oht_ref[32 * branch : 32 * branch + 32, :]
    pre, step, counts_t, log_wide, log_rows = scan_inputs(
        oh_ref[...], oht_ref[...], pre_ref[:, 512 * branch : 512 * branch + 512],
        step_ref[:, 256 * branch : 256 * branch + 256],
        lx_ref[:, 256 * branch : 256 * branch + 256],
        lrow_ref[8 * branch : 8 * branch + 8, :], ahead, behind,
    )
    counts_t = counts_t[32 * branch : 32 * branch + 32]
    logistic = sigmoid(pre)
    act = pre * logistic
    bend = logistic * (1.0 + pre * (1.0 - logistic))
    x = act[:, :256]
    b = act[:, 256:384]
    c = act[:, 384:]
    xs = x * step
    dy = dy_ref[...]
    own = y_ref[...] - skip * x
    state = state_ref[0, 0]
    pull = carry_ref[branch]
    xs_low = xs.astype(bf16)
    dy_low = dy.astype(bf16)
    inner = dot3(b, c, NT)
    parts = []
    slopes = jnp.zeros((BLOCK, BLOCK), f32)
    for h in range(4):
        wide = slice(h * HDIM, (h + 1) * HDIM)
        decays = triangle(
            branch == 1, log_wide[:, h * HDIM : h * HDIM + 1], log_rows[h : h + 1, :], None, -1.0
        )
        parts.append(dot1(inner * decays, dy_low[:, wide]))
        slopes = slopes + dot1(xs_low[:, wide], dy_low[:, wide], NT) * decays
    within = jnp.concatenate(parts, axis=1)
    faded = jnp.exp2(log_wide) * dy
    edge = log_wide[BLOCK - 1 :] if branch == 0 else log_wide[:1]
    tail = jnp.exp2(edge - log_wide)
    db = dot1(slopes, c) + dot1(tail * xs, pull, NT)
    dc = dot1(slopes, b, TN) + dot1(faded, state, NT)
    dxs = within + tail * dot1(b, pull)
    dlog = dy_low.astype(f32) * own - xs_low.astype(f32) * dxs
    edge_count = counts_t[:, BLOCK - 1 :] if branch == 0 else counts_t[:, :1]
    ahead = jnp.sum(later_ref[0, 0] * pull, axis=0, keepdims=True)
    logs_ref[...] += dot2(counts_t, dlog) + edge_count * ahead
    carry_ref[branch] = dot1(c, faded, TN) + jnp.exp2(edge) * pull
    dpre = jnp.concatenate([step * dxs + skip * dy, db, dc], axis=1) * bend
    tables_ref[...] += dot2(onehot_t, dpre)
    steps_ref[...] += dot2(onehot_t, x * dxs)
    skips_ref[...] += jnp.sum(dy * x, axis=0, keepdims=True)


def first_backward_kernel(at_ref, *refs):
    upper, lower, tables = refs[0:5], refs[5:10], refs[10:15]
    (
        upper_second_ref, lower_first_ref, upper_slope_ref, lower_slope_ref, upper_cot_ref,
        lower_cot_ref, upper_sums_ref, lower_sums_ref, gate_ref, gain_ref,
    ) = refs[15:25]
    sums, outer_ref = refs[25:30], refs[30]
    mixed_ref, first_out_ref, second_out_ref, dgate_ref, dgain_ref = refs[31:36]
    first_ref, second_ref = refs[36:38]
    step_at = pl.program_id(0)

    @pl.when(step_at == 0)
    def _():
        for ref in (*sums, outer_ref, dgate_ref, dgain_ref):
            ref[...] = jnp.zeros_like(ref)

    gain = own_row(gain_ref, at_ref[1])
    upper_mixed, (dy, dy_later) = mix_rows(
        (upper[2], upper_second_ref), upper[0], upper[1], upper_slope_ref, upper_sums_ref,
        gate_ref, gain, dgate_ref, dgain_ref,
    )
    first_ref[...] = dy
    second_out_ref[...] = dy_later
    lower_mixed, (dy_later, dy) = mix_rows(
        (lower_first_ref, lower[2]), lower[0], lower[1], lower_slope_ref, lower_sums_ref,
        gate_ref, gain, dgate_ref, dgain_ref,
    )
    second_ref[...] = dy
    first_out_ref[...] = dy_later
    mixed_ref[pl.ds(pl.multiple_of((3 - step_at) * BLOCK, BLOCK), BLOCK), :] = upper_mixed
    mixed_ref[pl.ds(pl.multiple_of(step_at * BLOCK, BLOCK), BLOCK), :] = lower_mixed
    backward_scan(0, *upper, first_ref, *tables, *sums)
    backward_scan(1, *lower, second_ref, *tables, *sums)
    cot = jnp.concatenate([upper_cot_ref[...], lower_cot_ref[...]], axis=0)
    mixed = jnp.concatenate([upper_mixed, lower_mixed], axis=0)
    outer_ref[...] += lax.dot_general(cot, mixed, TN, preferred_element_type=f32)


def second_backward_kernel(at_ref, *refs):
    blocks = (refs[0:6], refs[6:12])
    tables, sums_in = refs[12:17], refs[17:22]
    (
        ca_ref, cb_ref, tokens_ref, goht_ref, sums_ref, decay_ref, after_ref, gact_any, gbend_any,
        gstep_any, tab_ref, weight_any, cot_any, conv_x_ref, conv_bc_ref, dgate_ref, dgain_ref,
        packed_ref,
        mark_ref, found_ref, tables_ref, steps_ref, logs_ref, skips_ref, pull_ref,
        gact_ref, gbend_ref, gstep_ref, gate_w_ref, x_w_ref, bc_w_ref, step_w_ref, cot_ref, sems,
    ) = refs[22:]
    wide_ref = tables[4]
    sums = (tables_ref, steps_ref, logs_ref, skips_ref, pull_ref)
    own_at = pl.multiple_of(at_ref[1] * 256, 256)
    fetched = (
        (gact_any, gact_ref),
        (gbend_any, gbend_ref),
        (gstep_any, gstep_ref),
        (weight_any.at[pl.ds(own_at, 256), :], gate_w_ref),
        (weight_any.at[pl.ds(INNER + own_at, 256), :], x_w_ref),
        (weight_any.at[pl.ds(2 * INNER, 256), :], bc_w_ref),
        (weight_any.at[pl.ds(2 * INNER + 256, HEADS), :], step_w_ref),
        (cot_any, cot_ref),
    )
    copies = [
        pltpu.make_async_copy(source, target, sems.at[k])
        for k, (source, target) in enumerate(fetched)
    ]

    @pl.when(pl.program_id(0) == 0)
    def _():
        for copy in copies:
            copy.start()
        for ref, ref_in in zip(sums, sums_in):
            ref[...] = ref_in[...]

    for branch in range(2):
        backward_scan(branch, *blocks[branch], *tables, *sums)

    @pl.when(pl.program_id(0) == 1)
    def _():
        for copy in copies:
            copy.wait()
        far_and_pack(
            at_ref[1], pull_ref, wide_ref, ca_ref, cb_ref, tokens_ref, goht_ref,
            sums_ref, decay_ref, after_ref, gact_ref, gbend_ref, gstep_ref, tab_ref, gate_w_ref,
            x_w_ref, bc_w_ref, step_w_ref, cot_ref, conv_x_ref, conv_bc_ref, dgate_ref, dgain_ref,
            packed_ref, mark_ref, found_ref, tables_ref, steps_ref, logs_ref, skips_ref,
        )


def far_and_pack(
    rank, pull_ref, wide_ref, ca_ref, cb_ref, tokens_ref, goht_ref,
    sums_ref, decay_ref, after_ref, gact_ref, gbend_ref, gstep_ref, tab_ref, gate_w_ref,
    x_w_ref, bc_w_ref, step_w_ref, cot_ref, conv_x_ref, conv_bc_ref, dgate_ref, dgain_ref,
    packed_ref, mark_ref, found_ref, tables_ref, steps_ref, logs_ref, skips_ref,
):
    gram_x = gact_ref[:, :256]
    gram_b = gact_ref[:, 256:]
    gram_step = gstep_ref[...]
    gram_xs = gram_x * gram_step
    dxs = jnp.zeros((CODES * CODES, 256), f32)
    db = jnp.zeros((CODES * CODES, 128), f32)
    found = []
    expanded = expand_grams(sums_ref[...])
    for branch, weights in enumerate(expanded):
        pull = pull_ref[branch]
        met = dot1(gram_b, pull)
        dxs = dxs + weights * met
        db = db + dot1(weights * gram_xs, pull, NT)
        found.append(gram_xs * met)
    dpre = jnp.concatenate([gram_step * dxs, db], axis=1) * gbend_ref[...]
    gram_t = goht_ref[...]
    tables_ref[:, :384] += dot2(gram_t, dpre)
    steps_ref[...] += dot2(gram_t, gram_x * dxs)
    table = gather_grams(found).astype(bf16)
    early_codes = iota((2 * CODES, 128), 0)
    late_codes = iota((CODES, 128), 0)

    def look_up(shard, unused):
        at = pl.ds(pl.multiple_of(shard * 8, 8), 8)
        early = ca_ref[at, :]
        late = cb_ref[at, :]
        for j in range(8):
            mark_ref[:, 128 * j : 128 * j + 128] = ones_where(early[j : j + 1] == early_codes)
        looked = dot1(table, mark_ref[...], TN)
        for h in range(4):
            rows = []
            for j in range(8):
                part = looked[32 * h : 32 * h + 32, 128 * j : 128 * j + 128]
                mine = late[j : j + 1] == late_codes
                rows.append(jnp.sum(jnp.where(mine, part, 0.0), axis=0, keepdims=True))
            found_ref[h, at, :] = jnp.concatenate(rows, axis=0)
        return unused

    lax.fori_loop(0, 16, look_up, 0, unroll=4)
    lane_head = iota((1, 256), 1) // HDIM
    sub = iota((8, 256), 0)
    far = jnp.zeros((8, 256), f32)
    for h in range(4):
        weighted = found_ref[h] * decay_ref[h]
        for symbol in range(5):
            total = jnp.sum(weighted * after_ref[symbol], axis=0, keepdims=True)
            total = jnp.sum(total, axis=1, keepdims=True)
            far = far + jnp.where((lane_head == h) & (sub == symbol + 1), total, 0.0)

    gate_tab = tab_ref[:, :256]
    x_tab = tab_ref[:, 256:512]
    bc_tab = tab_ref[:, 512:768]
    logistic = sigmoid(gate_tab)
    gate_part = (dgate_ref[0, 24:32, :] + dgate_ref[1, 24:32, :]) * (
        logistic * (1.0 + gate_tab * (1.0 - logistic))
    )
    conv_x = conv_x_ref[...]
    conv_bc = conv_bc_ref[...]
    x_part = jnp.zeros((8, 256), f32)
    bc_part = jnp.zeros((8, 256), f32)
    x_taps = []
    bc_taps = []
    for k in range(KCONV):
        dtap_x = tables_ref[8 * k : 8 * k + 8, :256]
        dtap_bc = tables_ref[8 * k : 8 * k + 8, 256:]
        x_part = x_part + conv_x[k : k + 1] * dtap_x
        bc_part = bc_part + conv_bc[k : k + 1] * dtap_bc
        x_taps.append(jnp.sum(dtap_x * x_tab, axis=0, keepdims=True))
        bc_taps.append(jnp.sum(dtap_bc * bc_tab, axis=0, keepdims=True))
    bias = tables_ref[6:7, :]
    same = ones_where(iota((256, 256), 0) // HDIM == iota((256, 256), 1) // HDIM)
    log_part = dot_exact(logs_ref[24:32, :], same) + far
    step_part = dot_exact(steps_ref[24:32, :], same) - wide_ref[16:17, :] * log_part
    step_part = step_part * wide_ref[0:8, :]
    rate_part = jnp.sum(log_part * wide_ref[8:16, :], axis=0, keepdims=True)
    skip_part = dot_exact(jnp.broadcast_to(skips_ref[...], (8, 256)), same)
    valid = (sub >= 1) & (sub <= 5)
    step_part = jnp.where(valid, step_part, 0.0)
    step_rows = jnp.where(
        sub == 0,
        jnp.sum(step_part, axis=0, keepdims=True),
        jnp.where(sub == 6, rate_part, jnp.where(sub == 7, skip_part, step_part)),
    )
    spread = iota((256, 128), 1)
    narrow = ones_where(
        (iota((256, 128), 0) % HDIM == 0)
        & (rank * 4 + iota((256, 128), 0) // HDIM == spread)
    )
    step_heads = dot_exact(step_rows, narrow)

    def against(part, weights):
        first_piece = part.astype(bf16)
        rest = part - first_piece.astype(f32)
        second_piece = rest.astype(bf16)
        third_piece = rest - second_piece.astype(f32)
        return dot1(first_piece, weights) + (
            dot1(second_piece, weights) + dot1(third_piece, weights)
        )

    embed_part = (
        dot1(tokens_ref[...], cot_ref[...])[24:32]
        + against(jnp.where(valid, gate_part, 0.0), gate_w_ref[...])
        + against(jnp.where(valid, x_part, 0.0), x_w_ref[...])
        + against(jnp.where(valid, bc_part, 0.0), bc_w_ref[...])
        + against(jnp.where(valid[:, :HEADS], step_heads[:, :HEADS], 0.0), step_w_ref[...])
    )

    def rows_of(part, zero, six, seven):
        return jnp.where(
            sub == 0, zero, jnp.where(sub == 6, six, jnp.where(sub == 7, seven, part))
        )

    gate_rows = rows_of(gate_part, x_taps[0], x_taps[1], x_taps[2])
    x_rows = rows_of(x_part, x_taps[3], bias[:, :256], dgain_ref[...])
    bc_rows = rows_of(bc_part, bc_taps[0], bc_taps[1], bc_taps[2])
    embed_first = rows_of(embed_part[:, :256], bc_taps[3], bias[:, 256:], 0.0)
    for half in range(2):
        cols = slice(128 * half, 128 * half + 128)
        packed_ref[half] = gate_rows[:, cols]
        packed_ref[2 + half] = x_rows[:, cols]
        packed_ref[4 + half] = bc_rows[:, cols]
        packed_ref[7 + half] = embed_first[:, cols]
    packed_ref[6] = step_heads
    for piece in range(2, 8):
        packed_ref[7 + piece] = embed_part[:, 128 * piece : 128 * piece + 128]


def out_kernel(mixed_ref, ow_ref, token_ref, embed_ref, out_ref):
    total = dot1(token_ref[...], embed_ref[...])
    for peer in range(mixed_ref.shape[0]):
        total = total + dot1(mixed_ref[peer], ow_ref[256 * peer : 256 * peer + 256, :])
    out_ref[...] = total.astype(bf16)


def final_kernel(
    at_ref, first_ref, second_ref, third_ref, fourth_ref, embed_ref,
    w_in_ref, embedding_ref, conv_ref, bias_ref, dt_ref, rate_ref, skip_ref, gain_ref,
):
    wholes = (first_ref, second_ref, third_ref, fourth_ref)
    me = at_ref[1]

    def summed(piece):
        one, two, three, four = [ref[2 * OWN + piece - OWN] for ref in wholes]
        return (one + two) + (three + four)

    def of_rank(rank, piece):
        apart = jnp.bitwise_xor(me, rank)
        at = jnp.bitwise_and(apart, 1) * OWN + piece
        value = wholes[0][at]
        for k in range(1, 4):
            value = jnp.where(apart // 2 == k, wholes[k][at], value)
        return value

    embed = embed_ref[...]

    def outer(table, first):
        one = table.astype(bf16)
        rest = table - one.astype(f32)
        two = rest.astype(bf16)
        three = rest - two.astype(f32)
        pieces = jnp.concatenate([one.astype(f32), two.astype(f32), three], axis=0)
        value = dot1(embed, pieces)
        w_in_ref[:, first : first + table.shape[1]] = value

    for rank in range(8):
        for half in range(2):
            gate = of_rank(rank, half)
            x = of_rank(rank, 2 + half)
            at = 256 * rank + 128 * half
            cols = slice(at, at + 128)
            outer(gate, at)
            outer(x, INNER + at)
            conv_ref[0:1, cols] = gate[0:1]
            conv_ref[1:2, cols] = gate[6:7]
            conv_ref[2:3, cols] = gate[7:8]
            conv_ref[3:4, cols] = x[0:1]
            bias_ref[2 * rank + half : 2 * rank + half + 1, :] = x[6:7]
            gain_ref[2 * rank + half : 2 * rank + half + 1, :] = x[7:8]
    for half in range(2):
        bc = summed(4 + half)
        at = INNER + 128 * half
        cols = slice(at, at + 128)
        outer(bc, INNER + at)
        rest = summed(7 + half)
        conv_ref[0:1, cols] = bc[0:1]
        conv_ref[1:2, cols] = bc[6:7]
        conv_ref[2:3, cols] = bc[7:8]
        conv_ref[3:4, cols] = rest[0:1]
        bias_ref[16 + half : 17 + half, :] = rest[6:7]
    steps = summed(6)[:, :HEADS]
    outer(steps, 2 * INNER + 2 * STATE)
    dt_ref[...] = steps[0:1]
    rate_ref[...] = steps[6:7]
    skip_ref[...] = steps[7:8]
    for piece in range(8):
        embedding_ref[:, 128 * piece : 128 * piece + 128] = summed(7 + piece)[1:6]


VMEM = pl.BlockSpec(memory_space=pltpu.VMEM)
SMEM = pl.BlockSpec(memory_space=pltpu.SMEM)
VMEM_LIMIT = 62 * 1024 * 1024
TOKEN_STEPS = 2
ANY = pl.BlockSpec(memory_space=pl.ANY)


def whole(array):
    zeros = (0,) * array.ndim
    return pl.BlockSpec(array.shape, lambda i, at: zeros)


def own(shape, index):
    return pl.BlockSpec(shape, index)


def call(kernel, at, operands, outs, scratch=(), cost=5e9, steps=1):
    arrays = [item[0] if isinstance(item, tuple) else item for item in operands]
    specs = [
        (own(*item[1:]) if len(item) > 2 else ANY) if isinstance(item, tuple) else whole(item)
        for item in operands
    ]
    shapes = [jax.ShapeDtypeStruct(item[0], item[1]) for item in outs]
    out_specs = [
        own(item[2], item[3]) if len(item) > 2 else whole(shape)
        for item, shape in zip(outs, shapes)
    ]
    return pl.pallas_call(
        kernel,
        out_shape=shapes,
        grid_spec=pltpu.PrefetchScalarGridSpec(
            num_scalar_prefetch=1,
            grid=(steps,),
            in_specs=specs,
            out_specs=out_specs,
            scratch_shapes=list(scratch),
        ),
        compiler_params=pltpu.CompilerParams(vmem_limit_bytes=VMEM_LIMIT),
        cost_estimate=pl.CostEstimate(flops=int(cost), bytes_accessed=4000000, transcendentals=0),
    )(at, *arrays)


def call_plain(kernel, operands, outs, cost=1e9):
    return pl.pallas_call(
        kernel,
        out_shape=[jax.ShapeDtypeStruct(shape, kind) for shape, kind in outs],
        in_specs=[SMEM if item.dtype == jnp.int32 else VMEM for item in operands],
        out_specs=[VMEM] * len(outs),
        compiler_params=pltpu.CompilerParams(vmem_limit_bytes=VMEM_LIMIT),
        cost_estimate=pl.CostEstimate(flops=int(cost), bytes_accessed=1000000, transcendentals=0),
    )(*operands)


def gather(shard, axis):
    devices = lax.axis_size(axis)
    spread = jnp.broadcast_to(shard[None], (devices,) + shard.shape)
    return lax.all_to_all(spread, axis, split_axis=0, concat_axis=0, tiled=True)


def gather_by_flips(array, axis, flips):
    pairs = [[(i, i ^ flip) for i in range(lax.axis_size(axis))] for flip in flips]
    return jnp.concatenate([array] + [lax.ppermute(array, axis, pair) for pair in pairs], axis=0)


def sum_by_flips(array, axis, flips):
    pairs = [[(i, i ^ flip) for i in range(lax.axis_size(axis))] for flip in flips]
    one, two, three = [lax.ppermute(array, axis, pair) for pair in pairs]
    return (array + one) + (two + three)


def exchange(array, axis):
    return lax.all_to_all(array, axis, split_axis=0, concat_axis=0, tiled=True)


def body(
    base_ids, embedding, in_weight, conv_weight, conv_bias, dt_bias, a_log, skip_weight, norm_gain,
    out_weight, cotangent,
):
    groups = lax.axis_size("head")
    shards = lax.axis_size("seq")
    width = HEADS // groups * HDIM
    head_rank = lax.axis_index("head")
    seq_rank = lax.axis_index("seq")
    length = base_ids.shape[0]
    token_rows = length // groups
    at = jnp.stack([seq_rank, head_rank]).astype(jnp.int32)

    near = gather_by_flips(base_ids.reshape(1, 8, 128), "seq", (1, 8, 9))
    near, in_weight = lax.optimization_barrier((near, in_weight))
    ids = gather_by_flips(near, "seq", (2, 4, 6))
    cot_all = gather(cotangent, "head").reshape(length, D)
    weight_t = in_weight.T
    gain_rows = norm_gain.reshape(INNER // 128, 128)
    grams = _gram_onehot()
    gram_rows = jnp.asarray(grams, bf16)
    gram_cols = jnp.asarray(np.ascontiguousarray(grams[:, :32].T), bf16)
    weights = [
        (weight_t, (width, D), lambda i, at: (at[1], 0)),
        (weight_t, (width, D), lambda i, at: (INNER // width + at[1], 0)),
        (weight_t, (256, D), lambda i, at: (16, 0)),
        (weight_t, (128, D), lambda i, at: (34, 0)),
    ]
    convs = [
        (conv_weight, (KCONV, width), lambda i, at: (0, at[1])),
        (conv_weight, (KCONV, width), lambda i, at: (0, INNER // width)),
    ]
    count = CODES * CODES
    big, logs, log_rows, tab, wide, gxs, gbt = call(
        prep_kernel,
        at,
        [
            embedding,
            *weights,
            *convs,
            conv_bias.reshape(conv_bias.shape[0] // 128, 128),
            dt_bias[None, :],
            a_log[None, :],
            skip_weight[None, :],
            gram_rows,
        ],
        [
            ((128, 2048), bf16),
            ((128, 512), bf16),
            ((16, 128), f32),
            ((8, 768), f32),
            ((24, width), f32),
            ((count, width), f32),
            ((STATE, count), f32),
        ],
        cost=6e9,
    )

    blocks = length // BLOCK

    tables = [
        (big, (128, 1024), lambda k, at: (0, 0)),
        (big, (128, 512), lambda k, at: (0, 2)),
        logs,
        log_rows,
        wide,
    ]

    def rows_at(array, rows, index):
        return (array, (rows, array.shape[1]), lambda k, at: (index(k), 0))

    y_first, y_second, states, sums, decays, after, onehot, onehot_t, early, late = call(
        forward_kernel,
        at,
        [ids, *tables, gxs, gbt],
        [
            ((length, width), f32, (BLOCK, width), lambda k, at: (k, 0)),
            ((length, width), f32, (BLOCK, width), lambda k, at: (blocks - 1 - k, 0)),
            (
                (2, blocks, STATE, width), f32,
                (2, 1, STATE, width), lambda k, at: (0, k, 0, 0),
            ),
            ((2 * CODES, 128), f32),
            ((4, 128, 128), f32),
            ((5, 128, 128), f32),
            ((length, 128), bf16),
            ((128, length), bf16),
            ((128, 128), jnp.int32),
            ((128, 128), jnp.int32),
        ],
        [
            pltpu.VMEM((8, 128, 128), jnp.int32),
            pltpu.VMEM((128, 4096), bf16),
            pltpu.VMEM((2 * CODES, 4096), bf16),
            pltpu.VMEM((2, STATE, width), f32),
        ],
        cost=1.5e10,
        steps=blocks,
    )

    chunk = length // TOKEN_STEPS
    gates = (big, (128, 512), lambda k, at: (0, 3))
    y_rows = [rows_at(y, chunk, lambda k: k) for y in (y_first, y_second)]
    hot_rows = rows_at(onehot, chunk, lambda k: k)
    slope, row_sums = call(
        slope_kernel,
        at,
        [
            *y_rows,
            hot_rows,
            gates,
            rows_at(cot_all, chunk, lambda k: k),
            (out_weight, (width, D), lambda k, at: (at[1], 0)),
            gain_rows,
        ],
        [
            ((length, width), f32, (chunk, width), lambda k, at: (k, 0)),
            ((groups, 4, length), f32, (groups, 4, chunk), lambda k, at: (0, 0, k)),
        ],
        cost=4e9,
        steps=TOKEN_STEPS,
    )
    row_sums, big, ids_later, embed_later = lax.optimization_barrier(
        (row_sums, big, base_ids, embedding)
    )
    gact, gbend, gstep = call(
        gram_kernel,
        at,
        [
            gram_rows,
            (big, (128, 512), lambda k, at: (0, 0)),
            (big, (128, 256), lambda k, at: (0, 4)),
        ],
        [((count, 384), f32), ((count, 384), f32), ((count, width), f32)],
        cost=2e9,
    )
    row_sums = exchange(row_sums, "head")
    def scan_operands(first_step):
        operands = []
        for branch, y in ((0, y_first), (1, y_second)):

            def nth(k):
                return first_step + k

            def block(k, branch=branch):
                return blocks - 1 - nth(k) if branch == 0 else nth(k)

            def state(k, at, branch=branch):
                return (branch, blocks - 1 - nth(k), 0, 0)

            def later(k, at, branch=branch):
                return (branch, jnp.minimum(blocks - nth(k), blocks - 1), 0, 0)

            one = (1, 1, STATE, width)
            operands.append(
                [
                    rows_at(onehot, BLOCK, block),
                    (onehot_t, (128, BLOCK), lambda k, at, block=block: (0, block(k))),
                    rows_at(y, BLOCK, block),
                    (states, one, state),
                    (states, one, later),
                ]
            )
        return operands

    accumulators = [
        ((32, 512), f32),
        ((32, width), f32),
        ((32, width), f32),
        ((1, width), f32),
        ((2, STATE, width), f32),
    ]
    first, second = scan_operands(0)

    def upper(k):
        return blocks - 1 - k

    def lower(k):
        return k

    def sums_at(index):
        return (row_sums, (groups, 4, BLOCK), lambda k, at: (0, 0, index(k)))

    *grads, partial, mixed, dy_first, dy_second, dgate, dgain = call(
        first_backward_kernel,
        at,
        [
            *first,
            *second,
            *tables,
            rows_at(y_second, BLOCK, upper),
            rows_at(y_first, BLOCK, lower),
            rows_at(slope, BLOCK, upper),
            rows_at(slope, BLOCK, lower),
            rows_at(cot_all, BLOCK, upper),
            rows_at(cot_all, BLOCK, lower),
            sums_at(upper),
            sums_at(lower),
            gates,
            gain_rows,
        ],
        accumulators
        + [
            ((D, width), f32),
            ((length, width), bf16),
            ((length // 2, width), f32, (BLOCK, width), lambda k, at: (k, 0)),
            ((length // 2, width), f32, (BLOCK, width), lambda k, at: (1 - k, 0)),
            ((2, 32, width), f32),
            ((1, width), f32),
        ],
        [pltpu.VMEM((BLOCK, width), f32), pltpu.VMEM((BLOCK, width), f32)],
        cost=2e10,
        steps=blocks // 2,
    )
    partial = exchange(partial.reshape(shards, D // shards, width), "seq")
    first, second = scan_operands(blocks // 2)
    (packed,) = call(
        second_backward_kernel,
        at,
        [
            *first,
            rows_at(dy_first, BLOCK, lambda k: 1 - k),
            *second,
            rows_at(dy_second, BLOCK, lambda k: k),
            *tables,
            *grads,
            early,
            late,
            (onehot_t, (32, token_rows), lambda k, at: (0, at[1])),
            gram_cols,
            sums,
            decays,
            after,
            (gact,),
            (gbend,),
            (gstep,),
            tab,
            (weight_t,),
            (cotangent,),
            *convs,
            dgate,
            dgain,
        ],
        [((OWN + SHARED, 8, 128), f32)],
        [
            pltpu.VMEM((2 * CODES, 1024), bf16),
            pltpu.VMEM((4, 128, 128), f32),
            *[pltpu.VMEM(shape, kind) for shape, kind in accumulators],
            pltpu.VMEM((count, 384), f32),
            pltpu.VMEM((count, 384), f32),
            pltpu.VMEM((count, width), f32),
            pltpu.VMEM((width, D), bf16),
            pltpu.VMEM((width, D), bf16),
            pltpu.VMEM((256, D), bf16),
            pltpu.VMEM((HEADS, D), bf16),
            pltpu.VMEM((token_rows, D), bf16),
            pltpu.SemaphoreType.DMA((8,)),
        ],
        cost=2e10,
        steps=blocks // 2,
    )
    packed, partial, mixed = lax.optimization_barrier((packed, partial, mixed))
    mixed_all = exchange(mixed.reshape(groups, token_rows, width), "head")
    total = sum_by_flips(packed, "seq", (1, 8, 9))
    total = sum_by_flips(total, "seq", (2, 4, 6))

    grad_w_out = jnp.sum(partial, axis=0).T
    token_ids = lax.dynamic_slice_in_dim(ids_later, head_rank * token_rows, token_rows, 0)
    alphabet = jnp.arange(5, dtype=jnp.int32)
    token_hot = (token_ids[:, None] == alphabet[None, :]).astype(bf16)

    row_count = D // shards
    columns = lax.dynamic_slice_in_dim(embed_later, seq_rank * row_count, row_count, 1)
    columns = jnp.pad(columns, ((1, 2), (0, 0)))
    columns = jnp.concatenate([columns] * 3, axis=0).T
    total, mixed_all = lax.optimization_barrier((total, mixed_all))
    pairs = [(i, i ^ 1) for i in range(groups)]
    beside = lax.ppermute(total, "head", pairs)
    total = jnp.concatenate([total[:OWN], beside[:OWN], total[OWN:] + beside[OWN:]], axis=0)
    everything = [total] + [
        lax.ppermute(total, "head", [(i, i ^ flip) for i in range(groups)]) for flip in (2, 4, 6)
    ]
    (layer_out,) = call_plain(
        out_kernel,
        [mixed_all, out_weight, token_hot, embedding],
        [((token_rows, D), bf16)],
        4e9,
    )
    w_in, embed, conv, bias, dt, rate, skip, gain = call_plain(
        final_kernel,
        [at, *everything, columns],
        [
            ((row_count, in_weight.shape[1]), f32),
            (embedding.shape, f32),
            (conv_weight.shape, f32),
            ((conv_bias.shape[0] // 128, 128), f32),
            ((1, HEADS), f32),
            ((1, HEADS), f32),
            ((1, HEADS), f32),
            ((INNER // 128, 128), f32),
        ],
    )
    return (
        layer_out, w_in, grad_w_out, embed, conv, bias.reshape(-1), dt[0], rate[0], skip[0],
        gain.reshape(-1),
    )


def solution(mesh):
    return jax.shard_map(
        body,
        mesh=mesh,
        in_specs=(P("seq"), P(), P(), P(), P(), P(), P(), P(), P(), P(), P(("seq", "head"), None)),
        out_specs=(
            P(("seq", "head"), None),
            P("seq", None),
            P("head", "seq"),
            P(),
            P(),
            P(),
            P(),
            P(),
            P(),
            P(),
        ),
        check_vma=False,
    )
```

```python
import jax
import jax.numpy as jnp
import numpy as np
from jax import lax
from jax.experimental import pallas as pl
from jax.experimental.pallas import tpu as pltpu
from jax.sharding import PartitionSpec as P

D = 1024
HEADS = 32
HDIM = 64
STATE = 128
BLOCK = 256
KCONV = 4
INNER = 2048
EPSILON = 1e-05
LOG2E = 1.4426950408889634

f32 = jnp.float32
bf16 = jnp.bfloat16
NN = (((1,), (0,)), ((), ()))
NT = (((1,), (1,)), ((), ()))
TN = (((0,), (0,)), ((), ()))

CODES = 32

OWN = 4
SHARED = 11


def _decode_codes():
    first = np.zeros((CODES,), np.int32)
    second = np.zeros((CODES,), np.int32)
    for code in range(25):
        first[code], second[code] = code // 5 + 1, code % 5 + 1
    for code in range(25, 30):
        second[code] = code - 24
    return first, second


def _gram_onehot():
    first, second = _decode_codes()
    early, late = np.divmod(np.arange(CODES * CODES), CODES)
    symbols = (first[early], second[early], first[late], second[late])
    rows = np.zeros((CODES * CODES, 128), np.float32)
    for tap, symbol in enumerate(symbols):
        valid = symbol > 0
        rows[np.arange(CODES * CODES)[valid], (8 * tap + symbol)[valid]] = 1.0
    rows[:, 6] = 1.0
    rows[:, 64:96] = rows[:, :32]
    return rows


def encode(earlier, later):
    return jnp.where(
        earlier > 0, (earlier - 1) * 5 + later - 1, jnp.where(later > 0, 24 + later, 30)
    )


def complement_padded(symbols):
    return jnp.where((symbols >= 1) & (symbols <= 4), 5 - symbols, symbols)


def halves(values):
    high = values.astype(bf16)
    return high, (values - high.astype(f32)).astype(bf16)


def dot1(a, b, dims=NN):
    return lax.dot_general(a.astype(bf16), b.astype(bf16), dims, preferred_element_type=f32)


def doubled(values, axis):
    return jnp.concatenate([values, values], axis=axis)


def dot2(a, b, dims=NN):
    high, low = halves(b)
    a = a.astype(bf16)
    if a.shape[dims[0][0][0]] <= 128:
        pieces = jnp.concatenate([high, low], axis=dims[0][1][0])
        return dot1(doubled(a, dims[0][0][0]), pieces, dims)
    return dot1(a, high, dims) + dot1(a, low, dims)


def dot2l(a, b, dims=NN):
    high, low = halves(a)
    b = b.astype(bf16)
    if b.shape[dims[0][1][0]] <= 128:
        pieces = jnp.concatenate([high, low], axis=dims[0][0][0])
        return dot1(pieces, doubled(b, dims[0][1][0]), dims)
    return dot1(high, b, dims) + dot1(low, b, dims)


def dot3(a, b, dims=NN):
    a_high, a_low = halves(a)
    b_high, b_low = halves(b)
    if a.shape[dims[0][0][0]] <= 128:
        pieces = jnp.concatenate([a_high, a_low], axis=dims[0][0][0])
        return dot1(pieces, doubled(b_high, dims[0][1][0]), dims) + dot1(a_high, b_low, dims)
    return dot1(a_high, b_high, dims) + (dot1(a_high, b_low, dims) + dot1(a_low, b_high, dims))


def dot_exact(a, b, dims=NN):
    first = a.astype(bf16)
    rest = a - first.astype(f32)
    second = rest.astype(bf16)
    third = rest - second.astype(f32)
    b = b.astype(bf16)
    return dot1(first, b, dims) + (dot1(second, b, dims) + dot1(third, b, dims))


def iota(shape, axis):
    return lax.broadcasted_iota(jnp.int32, shape, axis)


def ones_where(condition):
    return jnp.where(condition, 1.0, 0.0).astype(bf16)


def expand_grams(sums):
    grams = CODES * CODES
    early = ones_where(iota((grams, CODES), 0) // CODES == iota((grams, CODES), 1))
    both = dot2(early, jnp.concatenate([sums[:CODES], sums[CODES:]], axis=1))
    mine = iota((grams, 128), 0) % CODES == iota((grams, 128), 1) % CODES
    widen = ones_where(iota((128, 256), 0) // CODES == iota((128, 256), 1) // HDIM)
    return [
        dot2l(jnp.where(mine, both[:, 128 * k : 128 * k + 128], 0.0), widen) for k in range(2)
    ]


def gather_grams(values):
    grams = CODES * CODES
    narrow = ones_where(iota((256, 128), 0) // HDIM == iota((256, 128), 1) // CODES)
    mine = iota((grams, 128), 0) % CODES == iota((grams, 128), 1) % CODES
    spread = [jnp.where(mine, dot1(value, narrow), 0.0) for value in values]
    early = ones_where(iota((CODES, grams), 1) // CODES == iota((CODES, grams), 0))
    both = dot1(early, jnp.concatenate(spread, axis=1))
    return jnp.concatenate([both[:, :128], both[:, 128:]], axis=0)


def sigmoid(values):
    return 0.5 * jnp.tanh(0.5 * values) + 0.5


def scan_inputs(onehot, onehot_t, pre_tab, step_tab, log_tab, log_rows, ahead, behind):
    pre = dot1(onehot, pre_tab)
    step = dot1(onehot, step_tab)
    counts = dot1(ones_where(behind), onehot).astype(bf16)
    counts_t = dot1(onehot_t, ones_where(ahead))
    log_wide = dot1(counts, log_tab)
    log_rows = dot1(log_rows.astype(bf16), counts_t)
    return pre, step, counts_t, log_wide, log_rows


def prep_kernel(
    at_ref, embed_ref, gate_w_ref, x_w_ref, bc_w_ref, step_w_ref, conv_x_ref, conv_bc_ref,
    bias_ref, dt_ref, rate_ref, skip_ref, goh_ref,
    big_ref, logs_ref, lrow_ref, tab_ref, wide_ref, gxs_ref, gbt_ref,
):
    rank = at_ref[1]
    place = ones_where(iota((8, 5), 0) == iota((8, 5), 1) + 1)
    embed = dot1(place, embed_ref[...]).astype(bf16)
    gate_w = gate_w_ref[...]
    x_w = x_w_ref[...]
    bc_w = bc_w_ref[...]
    step_w = step_w_ref[...]

    def heads_row(ref):
        return jnp.concatenate([ref[...], jnp.zeros((1, 128 - HEADS), f32)], axis=1)

    bias_x = jnp.concatenate(
        [bias_ref[pl.ds(2 * rank, 1), :], bias_ref[pl.ds(2 * rank + 1, 1), :]], axis=1
    )
    bias_bc = jnp.concatenate([bias_ref[16:17, :], bias_ref[17:18, :]], axis=1)
    gate = dot1(embed, gate_w, NT)
    x = dot1(embed, x_w, NT)
    bc = dot1(embed, bc_w, NT)
    tab_ref[:, :256] = gate
    tab_ref[:, 256:512] = x
    tab_ref[:, 512:768] = bc
    row = iota((8, 128), 0)
    lane = iota((8, 128), 1)
    valid = (row >= 1) & (row <= 5)
    pre = dot1(embed, step_w, NT)
    pre = jnp.concatenate([pre, jnp.zeros((8, 128 - HEADS), f32)], axis=1) + heads_row(dt_ref)
    valid = valid & (lane < HEADS)
    step = jnp.maximum(pre, 0.0) + jnp.log1p(jnp.exp(-jnp.abs(pre)))
    rate = jnp.exp(heads_row(rate_ref))
    logs = jnp.where(valid, -(rate * step), 0.0)
    step = jnp.where(valid, step, 0.0)
    bent = jnp.where(valid, sigmoid(pre), 0.0)
    widen = ones_where(iota((128, 256), 0) == rank * 4 + iota((128, 256), 1) // HDIM)
    step_wide = dot_exact(step, widen)
    logs_wide = dot_exact(logs, widen)
    logs = logs * LOG2E
    wide_ref[0:8, :] = dot_exact(bent, widen)
    wide_ref[8:16, :] = logs_wide
    others = jnp.where(row == 0, rate, jnp.where(row == 1, heads_row(skip_ref), 0.0))
    others = jnp.where(lane < HEADS, others, 0.0)
    wide_ref[16:24, :] = dot_exact(others, widen)
    one_row = iota((8, 256), 0) == 6
    conv_x = conv_x_ref[...]
    conv_bc = conv_bc_ref[...]
    taps = []
    for k in range(4):
        tap_x = conv_x[k : k + 1] * x
        tap_bc = conv_bc[k : k + 1] * bc
        if k == 0:
            tap_x = jnp.where(one_row, bias_x, tap_x)
            tap_bc = jnp.where(one_row, bias_bc, tap_bc)
        taps.append(jnp.concatenate([tap_x, tap_bc], axis=1))
    silu_gate = gate * sigmoid(gate)

    def put(ref, start, pieces):
        nothing = jnp.zeros(pieces[0][1].shape, f32)
        pieces = dict(pieces)
        table = jnp.concatenate([pieces.get(k, nothing) for k in range(8)], axis=0)
        high, low = halves(table)
        ref[0:64, start : start + table.shape[1]] = high
        ref[64:128, start : start + table.shape[1]] = low
        return high, low

    first_high, first_low = put(big_ref, 0, list(enumerate(taps)))
    put(big_ref, 512, [(4 + k, tap) for k, tap in enumerate(taps)])
    step_high, step_low = put(big_ref, 1024, [(3, step_wide)])
    put(big_ref, 1280, [(7, step_wide)])
    put(big_ref, 1536, [(3, silu_gate)])
    put(big_ref, 1792, [(7, silu_gate)])
    put(logs_ref, 0, [(3, logs_wide * LOG2E)])
    put(logs_ref, 256, [(7, logs_wide * LOG2E)])
    pick = ones_where((iota((8, 128), 1) == rank * 4 + row) & (row < 4))
    nothing = jnp.zeros((8, 128), f32)
    for branch in range(2):
        spot = 3 + 4 * branch
        rows = jnp.concatenate([logs if k % 8 == spot else nothing for k in range(16)], axis=0)
        first = rows.astype(bf16)
        rest = rows - first.astype(f32)
        second = rest.astype(bf16)
        third = rest - second.astype(f32)
        values = dot1(pick, first, NT) + (dot1(pick, second, NT) + dot1(pick, third, NT))
        high = values.astype(bf16).astype(f32)
        lrow_ref[8 * branch : 8 * branch + 8, :] = jnp.where(lane < 64, high, values - high)
    grams = goh_ref[...]
    pre = dot1(grams, big_ref[:, :384])
    act = pre * sigmoid(pre)
    for j in range(8):
        cols = slice(128 * j, 128 * j + 128)
        gbt_ref[:, cols] = jnp.transpose(act[cols, 256:])
    gxs_ref[...] = act[:, :256] * dot1(grams, big_ref[:, 1024:1280])


def gram_kernel(at_ref, goh_ref, pre_ref, step_ref, gact_ref, gbend_ref, gstep_ref):
    pre = dot1(goh_ref[...], pre_ref[:, :384])
    logistic = sigmoid(pre)
    gact_ref[...] = pre * logistic
    gbend_ref[...] = logistic * (1.0 + pre * (1.0 - logistic))
    gstep_ref[...] = dot1(goh_ref[...], step_ref[...])


def shifted(symbols, by):
    row = iota((128, 128), 0)
    col = iota((128, 128), 1)
    if by > 0:
        rolled = pltpu.roll(symbols, by, axis=1)
        other = jnp.where(row == 0, 0, pltpu.roll(rolled, 1, axis=0))
        return jnp.where(col < by, other, rolled)
    rolled = pltpu.roll(symbols, 128 + by, axis=1)
    other = jnp.where(row == 127, 0, pltpu.roll(rolled, 127, axis=0))
    return jnp.where(col >= 128 + by, other, rolled)


def read_symbols(
    seq, ids_ref, ca_ref, cb_ref, taps_ref, oh_ref, oht_ref
):
    symbols = []
    for shard in range(16):
        mask = jnp.bitwise_xor(seq, shard)
        near = jnp.bitwise_and(mask, 1) + 2 * jnp.bitwise_and(mask // 8, 1)
        symbols.append(ids_ref[jnp.bitwise_and(mask // 2, 3) * 4 + near])
    symbols = jnp.concatenate(symbols, axis=0) + 1
    taps = [shifted(symbols, 3 - k) if k < 3 else symbols for k in range(4)]
    turned = [complement_padded(shifted(symbols, k - 3) if k < 3 else symbols) for k in range(4)]
    row = iota((128, 128), 0)
    is_before = row < seq * 8
    far = [jnp.where(is_before, a, b) for a, b in zip(taps, turned)]
    ca_ref[...] = encode(far[0], far[1]) + jnp.where(is_before, 0, CODES)
    cb_ref[...] = encode(far[2], far[3])
    for k in range(4):
        taps_ref[k] = taps[k]
        taps_ref[4 + k] = turned[k]
    at = pl.ds(pl.multiple_of(seq * 8, 8), 8)
    own = [taps_ref[k, at, :] for k in range(8)]
    sub = iota((8, 128), 0)
    for j in range(8):
        groups = []
        for k in range(8):
            hit = (own[k][j : j + 1] == sub) & (sub > 0)
            if k % 4 == 0:
                hit = hit | (sub == 6)
            groups.append(jnp.where(hit, 1.0, 0.0))
        rows = jnp.concatenate(groups + groups, axis=0)
        cols = slice(128 * j, 128 * j + 128)
        oht_ref[:, cols] = rows.astype(bf16)
        oh_ref[cols, :] = jnp.transpose(rows).astype(bf16)
    is_own = (row >= seq * 8) & (row < seq * 8 + 8)
    return jnp.where(is_own, 0, far[3])


def triangle(lower, column, row, inner, sign=1.0):
    half = BLOCK // 2
    apart = iota((half, half), 0) - iota((half, half), 1)
    keep = apart >= 0 if lower else apart <= 0
    parts = []
    for i in range(2):
        rows = slice(half * i, half * i + half)
        line = []
        for j in range(2):
            cols = slice(half * j, half * j + half)
            if (i < j) if lower else (i > j):
                line.append(jnp.zeros((half, half), f32))
                continue
            apart = column[rows] - row[:, cols] if sign > 0 else row[:, cols] - column[rows]
            if i == j:
                apart = jnp.where(keep, apart, -1e30)
            value = jnp.exp2(apart)
            line.append(value if inner is None else value * inner[rows, cols])
        parts.append(jnp.concatenate(line, axis=1))
    return jnp.concatenate(parts, axis=0)


def gram_sums(ca_ref, cb_ref, decay_ref, lhs_ref, rhs_ref):
    early_codes = iota((2 * CODES, 128), 0)
    late_codes = iota((CODES, 128), 0)

    def add(k, total):
        for j in range(32):
            if j % 8 == 0:
                at = pl.ds(pl.multiple_of(k * 32 + j, 8), 8)
                early = ca_ref[at, :]
                late = cb_ref[at, :]
                decays = [decay_ref[h, at, :] for h in range(4)]
            cols = slice(128 * j, 128 * j + 128)
            one = slice(j % 8, j % 8 + 1)
            rhs_ref[:, cols] = ones_where(early[one] == early_codes)
            mine = late[one] == late_codes
            for h in range(4):
                lhs_ref[32 * h : 32 * h + 32, cols] = jnp.where(mine, decays[h][one], 0.0).astype(
                    bf16
                )
        return total + dot1(rhs_ref[...], lhs_ref[...], NT)

    return lax.fori_loop(0, 4, add, jnp.zeros((2 * CODES, 128), f32), unroll=2)


def forward_kernel(
    at_ref, ids_ref, pre_ref, step_ref, lx_ref, lrow_ref, wide_ref, gxs_ref, gbt_ref,
    y_first_ref, y_second_ref, states_ref, sums_ref, decay_ref, after_ref, oh_ref, oht_ref,
    ca_ref, cb_ref,
    taps_ref, lhs_ref, rhs_ref, carry_ref,
):
    step_at = pl.program_id(0)
    y_refs = (y_first_ref, y_second_ref)

    @pl.when(step_at == 0)
    def _():
        seq = at_ref[0]
        first = seq * 8
        symbols = read_symbols(seq, ids_ref, ca_ref, cb_ref, taps_ref, oh_ref, oht_ref)
        log_small = lrow_ref[0:8, :] + pltpu.roll(lrow_ref[0:8, :], 64, axis=1)
        row = iota((128, 128), 0)
        col = iota((128, 128), 1)
        upto = ones_where(row <= col)
        every = jnp.ones((128, 128), bf16)
        signs = (jnp.where(col < row, 1.0, 0.0) - jnp.where(col < first, 1.0, 0.0)).astype(bf16)
        is_before = row < first
        logs = [jnp.zeros((128, 128), f32) for _ in range(4)]
        for symbol in range(1, 6):
            here = symbols == symbol
            found = ones_where(here)
            upper = dot1(found, upto) + dot1(signs, dot1(found, every))
            after = jnp.where(is_before, -upper, upper - jnp.where(here, 1.0, 0.0))
            after_ref[symbol - 1] = after
            for h in range(4):
                logs[h] = logs[h] + after * log_small[h : h + 1, 24 + symbol : 25 + symbol]
        for h in range(4):
            decay_ref[h] = jnp.where(symbols > 0, jnp.exp2(logs[h]), 0.0)
        sums = gram_sums(ca_ref, cb_ref, decay_ref, lhs_ref, rhs_ref)
        sums_ref[...] = sums
        gram_xs = gxs_ref[...]
        both = jnp.concatenate([weights * gram_xs for weights in expand_grams(sums)], axis=1)
        states = dot3(gbt_ref[...], both)
        carry_ref[0] = states[:, :256]
        carry_ref[1] = states[:, 256:]

    for branch in range(2):
        block = step_at if branch == 0 else 3 - step_at
        rows = pl.ds(pl.multiple_of(block * BLOCK, BLOCK), BLOCK)
        apart = iota((BLOCK, BLOCK), 0) - iota((BLOCK, BLOCK), 1)
        lower = branch == 0
        behind = apart >= 0 if lower else apart <= 0
        ahead = apart <= 0 if lower else apart >= 0
        pre, step, counts_t, log_wide, log_rows = scan_inputs(
            oh_ref[rows, :], oht_ref[:, rows], pre_ref[:, 512 * branch : 512 * branch + 512],
            step_ref[:, 256 * branch : 256 * branch + 256],
            lx_ref[:, 256 * branch : 256 * branch + 256],
            lrow_ref[8 * branch : 8 * branch + 8, :], ahead, behind,
        )
        act = pre * sigmoid(pre)
        x = act[:, :256]
        b = act[:, 256:384]
        c = act[:, 384:]
        xs = x * step
        state = carry_ref[branch]
        states_ref[branch, 0] = state
        inner = dot3(c, b, NT)
        parts = []
        for h in range(4):
            decays = triangle(
                lower, log_wide[:, h * HDIM : h * HDIM + 1], log_rows[h : h + 1, :], inner
            )
            parts.append(dot1(decays, xs[:, h * HDIM : (h + 1) * HDIM]))
        within = jnp.concatenate(parts, axis=1)
        y = within + dot3(c, state) * jnp.exp2(log_wide)
        y_refs[branch][...] = y + wide_ref[17:18, :] * x
        edge = log_wide[BLOCK - 1 :] if lower else log_wide[:1]
        carry_ref[branch] = jnp.exp2(edge) * state + dot3(b, jnp.exp2(edge - log_wide) * xs, TN)


def own_row(ref, rank):
    return jnp.concatenate([ref[pl.ds(2 * rank, 1), :], ref[pl.ds(2 * rank + 1, 1), :]], axis=1)


def slope_kernel(
    at_ref, y_first_ref, y_second_ref, oh_ref, gate_ref, cot_ref, ow_ref, gain_ref,
    slope_ref, sums_ref,
):
    slope = lax.dot_general(cot_ref[...], ow_ref[...], NT, preferred_element_type=f32)
    slope_ref[...] = slope
    weighted = slope * own_row(gain_ref, at_ref[1])
    gates = dot1(oh_ref[...], gate_ref[...])
    for branch in range(2):
        g = (y_first_ref, y_second_ref)[branch][...] * gates[:, 256 * branch : 256 * branch + 256]
        for kind, product in enumerate((g * g, weighted * g)):
            at = 2 * branch + kind
            product = product[:, :128] + product[:, 128:]
            for j in range(product.shape[0] // 128):
                cols = slice(128 * j, 128 * j + 128)
                total = jnp.sum(jnp.transpose(product[cols]), axis=0, keepdims=True)
                for peer in range(sums_ref.shape[0]):
                    sums_ref[peer, at : at + 1, cols] = total


def mix_rows(y_refs, oh_ref, oht_ref, slope_ref, sums_ref, gate_ref, gain, dgate_ref, dgain_ref):
    slope = slope_ref[...]
    sums = sums_ref[0]
    for peer in range(1, sums_ref.shape[0]):
        sums = sums + sums_ref[peer]
    scale = lax.rsqrt(sums / INNER + EPSILON)
    crossed = jnp.concatenate([sums[1:2], sums[1:2], sums[3:4], sums[3:4]], axis=0)
    weight = scale * scale * scale * crossed / INNER
    kind = iota(sums.shape, 0)
    weight = jnp.concatenate([weight[0:1], weight[0:1], weight[2:3], weight[2:3]], axis=0)
    rows = jnp.where(kind % 2 == 0, scale, weight)
    rows = jnp.concatenate([rows, rows] * 16, axis=0)
    parts = []
    for j in range(rows.shape[1] // 128):
        parts.append(jnp.transpose(rows[:, 128 * j : 128 * j + 128]))
    columns = jnp.concatenate(parts, axis=0)
    sloped = slope * gain
    gates = dot1(oh_ref[...], gate_ref[...])
    total = None
    dys = []
    for branch in range(2):
        gate = gates[:, 256 * branch : 256 * branch + 256]
        y = y_refs[branch][...]
        g = y * gate
        scale = columns[:, 2 * branch : 2 * branch + 1]
        weight = columns[:, 2 * branch + 1 : 2 * branch + 2]
        normed = g * scale
        total = normed if total is None else total + normed
        dg = scale * sloped - weight * g
        dys.append(dg * gate)
        lanes = oht_ref[32 * branch : 32 * branch + 32, :]
        dgate_ref[branch] += dot2(lanes, dg * y)
    dgain_ref[...] += jnp.sum(slope * total, axis=0, keepdims=True)
    return (total * gain).astype(bf16), dys


def backward_scan(
    branch, oh_ref, oht_ref, y_ref, state_ref, later_ref, dy_ref, pre_ref, step_ref, lx_ref,
    lrow_ref, wide_ref,
    tables_ref, steps_ref, logs_ref, skips_ref, carry_ref,
):
    skip = wide_ref[17:18, :]
    apart = iota((BLOCK, BLOCK), 0) - iota((BLOCK, BLOCK), 1)
    ahead = apart <= 0 if branch == 0 else apart >= 0
    behind = apart >= 0 if branch == 0 else apart <= 0
    onehot_t = oht_ref[32 * branch : 32 * branch + 32, :]
    pre, step, counts_t, log_wide, log_rows = scan_inputs(
        oh_ref[...], oht_ref[...], pre_ref[:, 512 * branch : 512 * branch + 512],
        step_ref[:, 256 * branch : 256 * branch + 256],
        lx_ref[:, 256 * branch : 256 * branch + 256],
        lrow_ref[8 * branch : 8 * branch + 8, :], ahead, behind,
    )
    counts_t = counts_t[32 * branch : 32 * branch + 32]
    logistic = sigmoid(pre)
    act = pre * logistic
    bend = logistic * (1.0 + pre * (1.0 - logistic))
    x = act[:, :256]
    b = act[:, 256:384]
    c = act[:, 384:]
    xs = x * step
    dy = dy_ref[...]
    own = y_ref[...] - skip * x
    state = state_ref[0, 0]
    pull = carry_ref[branch]
    xs_low = xs.astype(bf16)
    dy_low = dy.astype(bf16)
    inner = dot3(b, c, NT)
    parts = []
    slopes = jnp.zeros((BLOCK, BLOCK), f32)
    for h in range(4):
        wide = slice(h * HDIM, (h + 1) * HDIM)
        decays = triangle(
            branch == 1, log_wide[:, h * HDIM : h * HDIM + 1], log_rows[h : h + 1, :], None, -1.0
        )
        parts.append(dot1(inner * decays, dy_low[:, wide]))
        slopes = slopes + dot1(xs_low[:, wide], dy_low[:, wide], NT) * decays
    within = jnp.concatenate(parts, axis=1)
    faded = jnp.exp2(log_wide) * dy
    edge = log_wide[BLOCK - 1 :] if branch == 0 else log_wide[:1]
    tail = jnp.exp2(edge - log_wide)
    db = dot1(slopes, c) + dot1(tail * xs, pull, NT)
    dc = dot1(slopes, b, TN) + dot1(faded, state, NT)
    dxs = within + tail * dot1(b, pull)
    dlog = dy_low.astype(f32) * own - xs_low.astype(f32) * dxs
    edge_count = counts_t[:, BLOCK - 1 :] if branch == 0 else counts_t[:, :1]
    ahead = jnp.sum(later_ref[0, 0] * pull, axis=0, keepdims=True)
    logs_ref[...] += dot2(counts_t, dlog) + edge_count * ahead
    carry_ref[branch] = dot1(c, faded, TN) + jnp.exp2(edge) * pull
    dpre = jnp.concatenate([step * dxs + skip * dy, db, dc], axis=1) * bend
    tables_ref[...] += dot2(onehot_t, dpre)
    steps_ref[...] += dot2(onehot_t, x * dxs)
    skips_ref[...] += jnp.sum(dy * x, axis=0, keepdims=True)


def first_backward_kernel(at_ref, *refs):
    upper, lower, tables = refs[0:5], refs[5:10], refs[10:15]
    (
        upper_second_ref, lower_first_ref, upper_slope_ref, lower_slope_ref, upper_cot_ref,
        lower_cot_ref, upper_sums_ref, lower_sums_ref, gate_ref, gain_ref,
    ) = refs[15:25]
    sums, outer_ref = refs[25:30], refs[30]
    mixed_ref, first_out_ref, second_out_ref, dgate_ref, dgain_ref = refs[31:36]
    first_ref, second_ref = refs[36:38]
    step_at = pl.program_id(0)

    @pl.when(step_at == 0)
    def _():
        for ref in (*sums, outer_ref, dgate_ref, dgain_ref):
            ref[...] = jnp.zeros_like(ref)

    gain = own_row(gain_ref, at_ref[1])
    upper_mixed, (dy, dy_later) = mix_rows(
        (upper[2], upper_second_ref), upper[0], upper[1], upper_slope_ref, upper_sums_ref,
        gate_ref, gain, dgate_ref, dgain_ref,
    )
    first_ref[...] = dy
    second_out_ref[...] = dy_later
    lower_mixed, (dy_later, dy) = mix_rows(
        (lower_first_ref, lower[2]), lower[0], lower[1], lower_slope_ref, lower_sums_ref,
        gate_ref, gain, dgate_ref, dgain_ref,
    )
    second_ref[...] = dy
    first_out_ref[...] = dy_later
    mixed_ref[pl.ds(pl.multiple_of((3 - step_at) * BLOCK, BLOCK), BLOCK), :] = upper_mixed
    mixed_ref[pl.ds(pl.multiple_of(step_at * BLOCK, BLOCK), BLOCK), :] = lower_mixed
    backward_scan(0, *upper, first_ref, *tables, *sums)
    backward_scan(1, *lower, second_ref, *tables, *sums)
    cot = jnp.concatenate([upper_cot_ref[...], lower_cot_ref[...]], axis=0)
    mixed = jnp.concatenate([upper_mixed, lower_mixed], axis=0)
    outer_ref[...] += lax.dot_general(cot, mixed, TN, preferred_element_type=f32)


def second_backward_kernel(at_ref, *refs):
    blocks = (refs[0:6], refs[6:12])
    tables, sums_in = refs[12:17], refs[17:22]
    (
        ca_ref, cb_ref, tokens_ref, goht_ref, sums_ref, decay_ref, after_ref, gact_any, gbend_any,
        gstep_any, tab_ref, weight_any, cot_any, conv_x_ref, conv_bc_ref, dgate_ref, dgain_ref,
        packed_ref,
        mark_ref, found_ref, tables_ref, steps_ref, logs_ref, skips_ref, pull_ref,
        gact_ref, gbend_ref, gstep_ref, gate_w_ref, x_w_ref, bc_w_ref, step_w_ref, cot_ref, sems,
    ) = refs[22:]
    wide_ref = tables[4]
    sums = (tables_ref, steps_ref, logs_ref, skips_ref, pull_ref)
    own_at = pl.multiple_of(at_ref[1] * 256, 256)
    fetched = (
        (gact_any, gact_ref),
        (gbend_any, gbend_ref),
        (gstep_any, gstep_ref),
        (weight_any.at[pl.ds(own_at, 256), :], gate_w_ref),
        (weight_any.at[pl.ds(INNER + own_at, 256), :], x_w_ref),
        (weight_any.at[pl.ds(2 * INNER, 256), :], bc_w_ref),
        (weight_any.at[pl.ds(2 * INNER + 256, HEADS), :], step_w_ref),
        (cot_any, cot_ref),
    )
    copies = [
        pltpu.make_async_copy(source, target, sems.at[k])
        for k, (source, target) in enumerate(fetched)
    ]

    @pl.when(pl.program_id(0) == 0)
    def _():
        for copy in copies:
            copy.start()
        for ref, ref_in in zip(sums, sums_in):
            ref[...] = ref_in[...]

    for branch in range(2):
        backward_scan(branch, *blocks[branch], *tables, *sums)

    @pl.when(pl.program_id(0) == 1)
    def _():
        for copy in copies:
            copy.wait()
        far_and_pack(
            at_ref[1], pull_ref, wide_ref, ca_ref, cb_ref, tokens_ref, goht_ref,
            sums_ref, decay_ref, after_ref, gact_ref, gbend_ref, gstep_ref, tab_ref, gate_w_ref,
            x_w_ref, bc_w_ref, step_w_ref, cot_ref, conv_x_ref, conv_bc_ref, dgate_ref, dgain_ref,
            packed_ref, mark_ref, found_ref, tables_ref, steps_ref, logs_ref, skips_ref,
        )


def far_and_pack(
    rank, pull_ref, wide_ref, ca_ref, cb_ref, tokens_ref, goht_ref,
    sums_ref, decay_ref, after_ref, gact_ref, gbend_ref, gstep_ref, tab_ref, gate_w_ref,
    x_w_ref, bc_w_ref, step_w_ref, cot_ref, conv_x_ref, conv_bc_ref, dgate_ref, dgain_ref,
    packed_ref, mark_ref, found_ref, tables_ref, steps_ref, logs_ref, skips_ref,
):
    gram_x = gact_ref[:, :256]
    gram_b = gact_ref[:, 256:]
    gram_step = gstep_ref[...]
    gram_xs = gram_x * gram_step
    dxs = jnp.zeros((CODES * CODES, 256), f32)
    db = jnp.zeros((CODES * CODES, 128), f32)
    found = []
    expanded = expand_grams(sums_ref[...])
    for branch, weights in enumerate(expanded):
        pull = pull_ref[branch]
        met = dot1(gram_b, pull)
        dxs = dxs + weights * met
        db = db + dot1(weights * gram_xs, pull, NT)
        found.append(gram_xs * met)
    dpre = jnp.concatenate([gram_step * dxs, db], axis=1) * gbend_ref[...]
    gram_t = goht_ref[...]
    tables_ref[:, :384] += dot2(gram_t, dpre)
    steps_ref[...] += dot2(gram_t, gram_x * dxs)
    table = gather_grams(found).astype(bf16)
    early_codes = iota((2 * CODES, 128), 0)
    late_codes = iota((CODES, 128), 0)

    def look_up(shard, unused):
        at = pl.ds(pl.multiple_of(shard * 8, 8), 8)
        early = ca_ref[at, :]
        late = cb_ref[at, :]
        for j in range(8):
            mark_ref[:, 128 * j : 128 * j + 128] = ones_where(early[j : j + 1] == early_codes)
        looked = dot1(table, mark_ref[...], TN)
        for h in range(4):
            rows = []
            for j in range(8):
                part = looked[32 * h : 32 * h + 32, 128 * j : 128 * j + 128]
                mine = late[j : j + 1] == late_codes
                rows.append(jnp.sum(jnp.where(mine, part, 0.0), axis=0, keepdims=True))
            found_ref[h, at, :] = jnp.concatenate(rows, axis=0)
        return unused

    lax.fori_loop(0, 16, look_up, 0, unroll=4)
    lane_head = iota((1, 256), 1) // HDIM
    sub = iota((8, 256), 0)
    far = jnp.zeros((8, 256), f32)
    for h in range(4):
        weighted = found_ref[h] * decay_ref[h]
        for symbol in range(5):
            total = jnp.sum(weighted * after_ref[symbol], axis=0, keepdims=True)
            total = jnp.sum(total, axis=1, keepdims=True)
            far = far + jnp.where((lane_head == h) & (sub == symbol + 1), total, 0.0)

    gate_tab = tab_ref[:, :256]
    x_tab = tab_ref[:, 256:512]
    bc_tab = tab_ref[:, 512:768]
    logistic = sigmoid(gate_tab)
    gate_part = (dgate_ref[0, 24:32, :] + dgate_ref[1, 24:32, :]) * (
        logistic * (1.0 + gate_tab * (1.0 - logistic))
    )
    conv_x = conv_x_ref[...]
    conv_bc = conv_bc_ref[...]
    x_part = jnp.zeros((8, 256), f32)
    bc_part = jnp.zeros((8, 256), f32)
    x_taps = []
    bc_taps = []
    for k in range(KCONV):
        dtap_x = tables_ref[8 * k : 8 * k + 8, :256]
        dtap_bc = tables_ref[8 * k : 8 * k + 8, 256:]
        x_part = x_part + conv_x[k : k + 1] * dtap_x
        bc_part = bc_part + conv_bc[k : k + 1] * dtap_bc
        x_taps.append(jnp.sum(dtap_x * x_tab, axis=0, keepdims=True))
        bc_taps.append(jnp.sum(dtap_bc * bc_tab, axis=0, keepdims=True))
    bias = tables_ref[6:7, :]
    same = ones_where(iota((256, 256), 0) // HDIM == iota((256, 256), 1) // HDIM)
    log_part = dot_exact(logs_ref[24:32, :], same) + far
    step_part = dot_exact(steps_ref[24:32, :], same) - wide_ref[16:17, :] * log_part
    step_part = step_part * wide_ref[0:8, :]
    rate_part = jnp.sum(log_part * wide_ref[8:16, :], axis=0, keepdims=True)
    skip_part = dot_exact(jnp.broadcast_to(skips_ref[...], (8, 256)), same)
    valid = (sub >= 1) & (sub <= 5)
    step_part = jnp.where(valid, step_part, 0.0)
    step_rows = jnp.where(
        sub == 0,
        jnp.sum(step_part, axis=0, keepdims=True),
        jnp.where(sub == 6, rate_part, jnp.where(sub == 7, skip_part, step_part)),
    )
    spread = iota((256, 128), 1)
    narrow = ones_where(
        (iota((256, 128), 0) % HDIM == 0)
        & (rank * 4 + iota((256, 128), 0) // HDIM == spread)
    )
    step_heads = dot_exact(step_rows, narrow)

    def against(part, weights):
        first_piece = part.astype(bf16)
        rest = part - first_piece.astype(f32)
        second_piece = rest.astype(bf16)
        third_piece = rest - second_piece.astype(f32)
        return dot1(first_piece, weights) + (
            dot1(second_piece, weights) + dot1(third_piece, weights)
        )

    embed_part = (
        dot1(tokens_ref[...], cot_ref[...])[24:32]
        + against(jnp.where(valid, gate_part, 0.0), gate_w_ref[...])
        + against(jnp.where(valid, x_part, 0.0), x_w_ref[...])
        + against(jnp.where(valid, bc_part, 0.0), bc_w_ref[...])
        + against(jnp.where(valid[:, :HEADS], step_heads[:, :HEADS], 0.0), step_w_ref[...])
    )

    def rows_of(part, zero, six, seven):
        return jnp.where(
            sub == 0, zero, jnp.where(sub == 6, six, jnp.where(sub == 7, seven, part))
        )

    gate_rows = rows_of(gate_part, x_taps[0], x_taps[1], x_taps[2])
    x_rows = rows_of(x_part, x_taps[3], bias[:, :256], dgain_ref[...])
    bc_rows = rows_of(bc_part, bc_taps[0], bc_taps[1], bc_taps[2])
    embed_first = rows_of(embed_part[:, :256], bc_taps[3], bias[:, 256:], 0.0)
    for half in range(2):
        cols = slice(128 * half, 128 * half + 128)
        packed_ref[half] = gate_rows[:, cols]
        packed_ref[2 + half] = x_rows[:, cols]
        packed_ref[4 + half] = bc_rows[:, cols]
        packed_ref[7 + half] = embed_first[:, cols]
    packed_ref[6] = step_heads
    for piece in range(2, 8):
        packed_ref[7 + piece] = embed_part[:, 128 * piece : 128 * piece + 128]


def out_kernel(mixed_ref, ow_ref, token_ref, embed_ref, out_ref):
    total = dot1(token_ref[...], embed_ref[...])
    for peer in range(mixed_ref.shape[0]):
        total = total + dot1(mixed_ref[peer], ow_ref[256 * peer : 256 * peer + 256, :])
    out_ref[...] = total.astype(bf16)


def final_kernel(
    at_ref, first_ref, second_ref, third_ref, fourth_ref, embed_ref,
    w_in_ref, embedding_ref, conv_ref, bias_ref, dt_ref, rate_ref, skip_ref, gain_ref,
):
    wholes = (first_ref, second_ref, third_ref, fourth_ref)
    me = at_ref[1]

    def summed(piece):
        one, two, three, four = [ref[2 * OWN + piece - OWN] for ref in wholes]
        return (one + two) + (three + four)

    def of_rank(rank, piece):
        apart = jnp.bitwise_xor(me, rank)
        at = jnp.bitwise_and(apart, 1) * OWN + piece
        value = wholes[0][at]
        for k in range(1, 4):
            value = jnp.where(apart // 2 == k, wholes[k][at], value)
        return value

    embed = embed_ref[...]

    def outer(table, first):
        one = table.astype(bf16)
        rest = table - one.astype(f32)
        two = rest.astype(bf16)
        three = rest - two.astype(f32)
        pieces = jnp.concatenate([one.astype(f32), two.astype(f32), three], axis=0)
        value = dot1(embed, pieces)
        w_in_ref[:, first : first + table.shape[1]] = value

    for rank in range(8):
        for half in range(2):
            gate = of_rank(rank, half)
            x = of_rank(rank, 2 + half)
            at = 256 * rank + 128 * half
            cols = slice(at, at + 128)
            outer(gate, at)
            outer(x, INNER + at)
            conv_ref[0:1, cols] = gate[0:1]
            conv_ref[1:2, cols] = gate[6:7]
            conv_ref[2:3, cols] = gate[7:8]
            conv_ref[3:4, cols] = x[0:1]
            bias_ref[2 * rank + half : 2 * rank + half + 1, :] = x[6:7]
            gain_ref[2 * rank + half : 2 * rank + half + 1, :] = x[7:8]
    for half in range(2):
        bc = summed(4 + half)
        at = INNER + 128 * half
        cols = slice(at, at + 128)
        outer(bc, INNER + at)
        rest = summed(7 + half)
        conv_ref[0:1, cols] = bc[0:1]
        conv_ref[1:2, cols] = bc[6:7]
        conv_ref[2:3, cols] = bc[7:8]
        conv_ref[3:4, cols] = rest[0:1]
        bias_ref[16 + half : 17 + half, :] = rest[6:7]
    steps = summed(6)[:, :HEADS]
    outer(steps, 2 * INNER + 2 * STATE)
    dt_ref[...] = steps[0:1]
    rate_ref[...] = steps[6:7]
    skip_ref[...] = steps[7:8]
    for piece in range(8):
        embedding_ref[:, 128 * piece : 128 * piece + 128] = summed(7 + piece)[1:6]


VMEM = pl.BlockSpec(memory_space=pltpu.VMEM)
SMEM = pl.BlockSpec(memory_space=pltpu.SMEM)
VMEM_LIMIT = 62 * 1024 * 1024
TOKEN_STEPS = 2
ANY = pl.BlockSpec(memory_space=pl.ANY)


def whole(array):
    zeros = (0,) * array.ndim
    return pl.BlockSpec(array.shape, lambda i, at: zeros)


def own(shape, index):
    return pl.BlockSpec(shape, index)


def call(kernel, at, operands, outs, scratch=(), cost=5e9, steps=1):
    arrays = [item[0] if isinstance(item, tuple) else item for item in operands]
    specs = [
        (own(*item[1:]) if len(item) > 2 else ANY) if isinstance(item, tuple) else whole(item)
        for item in operands
    ]
    shapes = [jax.ShapeDtypeStruct(item[0], item[1]) for item in outs]
    out_specs = [
        own(item[2], item[3]) if len(item) > 2 else whole(shape)
        for item, shape in zip(outs, shapes)
    ]
    return pl.pallas_call(
        kernel,
        out_shape=shapes,
        grid_spec=pltpu.PrefetchScalarGridSpec(
            num_scalar_prefetch=1,
            grid=(steps,),
            in_specs=specs,
            out_specs=out_specs,
            scratch_shapes=list(scratch),
        ),
        compiler_params=pltpu.CompilerParams(vmem_limit_bytes=VMEM_LIMIT),
        cost_estimate=pl.CostEstimate(flops=int(cost), bytes_accessed=4000000, transcendentals=0),
    )(at, *arrays)


def call_plain(kernel, operands, outs, cost=1e9):
    return pl.pallas_call(
        kernel,
        out_shape=[jax.ShapeDtypeStruct(shape, kind) for shape, kind in outs],
        in_specs=[SMEM if item.dtype == jnp.int32 else VMEM for item in operands],
        out_specs=[VMEM] * len(outs),
        compiler_params=pltpu.CompilerParams(vmem_limit_bytes=VMEM_LIMIT),
        cost_estimate=pl.CostEstimate(flops=int(cost), bytes_accessed=1000000, transcendentals=0),
    )(*operands)


def gather(shard, axis):
    devices = lax.axis_size(axis)
    spread = jnp.broadcast_to(shard[None], (devices,) + shard.shape)
    return lax.all_to_all(spread, axis, split_axis=0, concat_axis=0, tiled=True)


def gather_by_flips(array, axis, flips):
    pairs = [[(i, i ^ flip) for i in range(lax.axis_size(axis))] for flip in flips]
    return jnp.concatenate([array] + [lax.ppermute(array, axis, pair) for pair in pairs], axis=0)


def sum_by_flips(array, axis, flips):
    pairs = [[(i, i ^ flip) for i in range(lax.axis_size(axis))] for flip in flips]
    one, two, three = [lax.ppermute(array, axis, pair) for pair in pairs]
    return (array + one) + (two + three)


def exchange(array, axis):
    return lax.all_to_all(array, axis, split_axis=0, concat_axis=0, tiled=True)


def body(
    base_ids, embedding, in_weight, conv_weight, conv_bias, dt_bias, a_log, skip_weight, norm_gain,
    out_weight, cotangent,
):
    groups = lax.axis_size("head")
    shards = lax.axis_size("seq")
    width = HEADS // groups * HDIM
    head_rank = lax.axis_index("head")
    seq_rank = lax.axis_index("seq")
    length = base_ids.shape[0]
    token_rows = length // groups
    at = jnp.stack([seq_rank, head_rank]).astype(jnp.int32)

    near = gather_by_flips(base_ids.reshape(1, 8, 128), "seq", (1, 8, 9))
    near, in_weight = lax.optimization_barrier((near, in_weight))
    ids = gather_by_flips(near, "seq", (2, 4, 6))
    cot_all = gather(cotangent, "head").reshape(length, D)
    weight_t = in_weight.T
    gain_rows = norm_gain.reshape(INNER // 128, 128)
    grams = _gram_onehot()
    gram_rows = jnp.asarray(grams, bf16)
    gram_cols = jnp.asarray(np.ascontiguousarray(grams[:, :32].T), bf16)
    weights = [
        (weight_t, (width, D), lambda i, at: (at[1], 0)),
        (weight_t, (width, D), lambda i, at: (INNER // width + at[1], 0)),
        (weight_t, (256, D), lambda i, at: (16, 0)),
        (weight_t, (HEADS, D), lambda i, at: ((2 * INNER + 2 * STATE) // HEADS, 0)),
    ]
    convs = [
        (conv_weight, (KCONV, width), lambda i, at: (0, at[1])),
        (conv_weight, (KCONV, width), lambda i, at: (0, INNER // width)),
    ]
    count = CODES * CODES
    big, logs, log_rows, tab, wide, gxs, gbt = call(
        prep_kernel,
        at,
        [
            embedding,
            *weights,
            *convs,
            conv_bias.reshape(conv_bias.shape[0] // 128, 128),
            dt_bias[None, :],
            a_log[None, :],
            skip_weight[None, :],
            gram_rows,
        ],
        [
            ((128, 2048), bf16),
            ((128, 512), bf16),
            ((16, 128), f32),
            ((8, 768), f32),
            ((24, width), f32),
            ((count, width), f32),
            ((STATE, count), f32),
        ],
        cost=6e9,
    )

    blocks = length // BLOCK

    tables = [
        (big, (128, 1024), lambda k, at: (0, 0)),
        (big, (128, 512), lambda k, at: (0, 2)),
        logs,
        log_rows,
        wide,
    ]

    def rows_at(array, rows, index):
        return (array, (rows, array.shape[1]), lambda k, at: (index(k), 0))

    y_first, y_second, states, sums, decays, after, onehot, onehot_t, early, late = call(
        forward_kernel,
        at,
        [ids, *tables, gxs, gbt],
        [
            ((length, width), f32, (BLOCK, width), lambda k, at: (k, 0)),
            ((length, width), f32, (BLOCK, width), lambda k, at: (blocks - 1 - k, 0)),
            (
                (2, blocks, STATE, width), f32,
                (2, 1, STATE, width), lambda k, at: (0, k, 0, 0),
            ),
            ((2 * CODES, 128), f32),
            ((4, 128, 128), f32),
            ((5, 128, 128), f32),
            ((length, 128), bf16),
            ((128, length), bf16),
            ((128, 128), jnp.int32),
            ((128, 128), jnp.int32),
        ],
        [
            pltpu.VMEM((8, 128, 128), jnp.int32),
            pltpu.VMEM((128, 4096), bf16),
            pltpu.VMEM((2 * CODES, 4096), bf16),
            pltpu.VMEM((2, STATE, width), f32),
        ],
        cost=1.5e10,
        steps=blocks,
    )

    chunk = length // TOKEN_STEPS
    gates = (big, (128, 512), lambda k, at: (0, 3))
    y_rows = [rows_at(y, chunk, lambda k: k) for y in (y_first, y_second)]
    hot_rows = rows_at(onehot, chunk, lambda k: k)
    slope, row_sums = call(
        slope_kernel,
        at,
        [
            *y_rows,
            hot_rows,
            gates,
            rows_at(cot_all, chunk, lambda k: k),
            (out_weight, (width, D), lambda k, at: (at[1], 0)),
            gain_rows,
        ],
        [
            ((length, width), f32, (chunk, width), lambda k, at: (k, 0)),
            ((groups, 4, length), f32, (groups, 4, chunk), lambda k, at: (0, 0, k)),
        ],
        cost=4e9,
        steps=TOKEN_STEPS,
    )
    row_sums, big, ids_later, embed_later = lax.optimization_barrier(
        (row_sums, big, base_ids, embedding)
    )
    gact, gbend, gstep = call(
        gram_kernel,
        at,
        [
            gram_rows,
            (big, (128, 512), lambda k, at: (0, 0)),
            (big, (128, 256), lambda k, at: (0, 4)),
        ],
        [((count, 384), f32), ((count, 384), f32), ((count, width), f32)],
        cost=2e9,
    )
    row_sums = exchange(row_sums, "head")
    def scan_operands(first_step):
        operands = []
        for branch, y in ((0, y_first), (1, y_second)):

            def nth(k):
                return first_step + k

            def block(k, branch=branch):
                return blocks - 1 - nth(k) if branch == 0 else nth(k)

            def state(k, at, branch=branch):
                return (branch, blocks - 1 - nth(k), 0, 0)

            def later(k, at, branch=branch):
                return (branch, jnp.minimum(blocks - nth(k), blocks - 1), 0, 0)

            one = (1, 1, STATE, width)
            operands.append(
                [
                    rows_at(onehot, BLOCK, block),
                    (onehot_t, (128, BLOCK), lambda k, at, block=block: (0, block(k))),
                    rows_at(y, BLOCK, block),
                    (states, one, state),
                    (states, one, later),
                ]
            )
        return operands

    accumulators = [
        ((32, 512), f32),
        ((32, width), f32),
        ((32, width), f32),
        ((1, width), f32),
        ((2, STATE, width), f32),
    ]
    first, second = scan_operands(0)

    def upper(k):
        return blocks - 1 - k

    def lower(k):
        return k

    def sums_at(index):
        return (row_sums, (groups, 4, BLOCK), lambda k, at: (0, 0, index(k)))

    *grads, partial, mixed, dy_first, dy_second, dgate, dgain = call(
        first_backward_kernel,
        at,
        [
            *first,
            *second,
            *tables,
            rows_at(y_second, BLOCK, upper),
            rows_at(y_first, BLOCK, lower),
            rows_at(slope, BLOCK, upper),
            rows_at(slope, BLOCK, lower),
            rows_at(cot_all, BLOCK, upper),
            rows_at(cot_all, BLOCK, lower),
            sums_at(upper),
            sums_at(lower),
            gates,
            gain_rows,
        ],
        accumulators
        + [
            ((D, width), f32),
            ((length, width), bf16),
            ((length // 2, width), f32, (BLOCK, width), lambda k, at: (k, 0)),
            ((length // 2, width), f32, (BLOCK, width), lambda k, at: (1 - k, 0)),
            ((2, 32, width), f32),
            ((1, width), f32),
        ],
        [pltpu.VMEM((BLOCK, width), f32), pltpu.VMEM((BLOCK, width), f32)],
        cost=2e10,
        steps=blocks // 2,
    )
    partial = exchange(partial.reshape(shards, D // shards, width), "seq")
    first, second = scan_operands(blocks // 2)
    (packed,) = call(
        second_backward_kernel,
        at,
        [
            *first,
            rows_at(dy_first, BLOCK, lambda k: 1 - k),
            *second,
            rows_at(dy_second, BLOCK, lambda k: k),
            *tables,
            *grads,
            early,
            late,
            (onehot_t, (32, token_rows), lambda k, at: (0, at[1])),
            gram_cols,
            sums,
            decays,
            after,
            (gact,),
            (gbend,),
            (gstep,),
            tab,
            (weight_t,),
            (cotangent,),
            *convs,
            dgate,
            dgain,
        ],
        [((OWN + SHARED, 8, 128), f32)],
        [
            pltpu.VMEM((2 * CODES, 1024), bf16),
            pltpu.VMEM((4, 128, 128), f32),
            *[pltpu.VMEM(shape, kind) for shape, kind in accumulators],
            pltpu.VMEM((count, 384), f32),
            pltpu.VMEM((count, 384), f32),
            pltpu.VMEM((count, width), f32),
            pltpu.VMEM((width, D), bf16),
            pltpu.VMEM((width, D), bf16),
            pltpu.VMEM((256, D), bf16),
            pltpu.VMEM((HEADS, D), bf16),
            pltpu.VMEM((token_rows, D), bf16),
            pltpu.SemaphoreType.DMA((8,)),
        ],
        cost=2e10,
        steps=blocks // 2,
    )
    packed, partial, mixed = lax.optimization_barrier((packed, partial, mixed))
    mixed_all = exchange(mixed.reshape(groups, token_rows, width), "head")
    total = sum_by_flips(packed, "seq", (1, 8, 9))
    total = sum_by_flips(total, "seq", (2, 4, 6))

    grad_w_out = jnp.sum(partial, axis=0).T
    token_ids = lax.dynamic_slice_in_dim(ids_later, head_rank * token_rows, token_rows, 0)
    alphabet = jnp.arange(5, dtype=jnp.int32)
    token_hot = (token_ids[:, None] == alphabet[None, :]).astype(bf16)

    row_count = D // shards
    columns = lax.dynamic_slice_in_dim(embed_later, seq_rank * row_count, row_count, 1)
    columns = jnp.pad(columns, ((1, 2), (0, 0)))
    columns = jnp.concatenate([columns] * 3, axis=0).T
    total, mixed_all = lax.optimization_barrier((total, mixed_all))
    pairs = [(i, i ^ 1) for i in range(groups)]
    beside = lax.ppermute(total, "head", pairs)
    total = jnp.concatenate([total[:OWN], beside[:OWN], total[OWN:] + beside[OWN:]], axis=0)
    everything = [total] + [
        lax.ppermute(total, "head", [(i, i ^ flip) for i in range(groups)]) for flip in (2, 4, 6)
    ]
    (layer_out,) = call_plain(
        out_kernel,
        [mixed_all, out_weight, token_hot, embedding],
        [((token_rows, D), bf16)],
        4e9,
    )
    w_in, embed, conv, bias, dt, rate, skip, gain = call_plain(
        final_kernel,
        [at, *everything, columns],
        [
            ((row_count, in_weight.shape[1]), f32),
            (embedding.shape, f32),
            (conv_weight.shape, f32),
            ((conv_bias.shape[0] // 128, 128), f32),
            ((1, HEADS), f32),
            ((1, HEADS), f32),
            ((1, HEADS), f32),
            ((INNER // 128, 128), f32),
        ],
    )
    return (
        layer_out, w_in, grad_w_out, embed, conv, bias.reshape(-1), dt[0], rate[0], skip[0],
        gain.reshape(-1),
    )


def solution(mesh):
    return jax.shard_map(
        body,
        mesh=mesh,
        in_specs=(P("seq"), P(), P(), P(), P(), P(), P(), P(), P(), P(), P(("seq", "head"), None)),
        out_specs=(
            P(("seq", "head"), None),
            P("seq", None),
            P("head", "seq"),
            P(),
            P(),
            P(),
            P(),
            P(),
            P(),
            P(),
        ),
        check_vma=False,
    )
```
